32 devices in a mesh: ctx: 8 (over y, x, core), head: 4 (over z).
Axes of the slice: x: 2, y: 2, z: 4, core: 2. Of those that a mesh axis runs over, the one named last changes fastest.
Arguments:
- query_rows: bfloat16 [8192, 4096], P('ctx', 'head'), may hold values from -6 to 6
- key_rows: bfloat16 [8192, 4096], P('ctx', 'head'), may hold values from -6 to 6
- value_rows: bfloat16 [8192, 4096], P('ctx', 'head'), may hold values from -6 to 6
- frequencies: bfloat16 [32, 128, 128], P('head'), may hold values from -4.1875 to 4.1875
- norm_gain: bfloat16 [4096], P('head'), may hold values from 0.25 to 1.75
- out_weight: bfloat16 [4096, 4096], P(None, 'head'), may hold values from -0.09375 to 0.09375
Outputs:
- projected: bfloat16 [8192, 4096], P('ctx', 'head')
The draws below stay inside these ranges and needn't reach their ends.
All inputs are finite; a program needn't handle non-finite values.
Results may differ from the reference program's by a relative error of at most 0.009.
Values may be sent and summed in bfloat16 or wider, within the bound.
No kernel may reach another device: no remote copies, remote signals or barrier semaphores. Data moves between devices by JAX's collectives and lax.ppermute only.
A program may use at most 128 MiB of HBM per device.

```python
import math
import jax
import jax.numpy as jnp
from jax import lax

D = 4096
HEADS = 32
HDIM = 128
NFREQ = 128
FEATS = 256
BLOCK = 512
SEQ_LEN = 8192


def block_scale(key, shape, cuts, least, top_value):
    gain = 1.0
    for dim, parts in cuts:
        steps = jax.random.uniform(jax.random.fold_in(jax.random.fold_in(key, 6), dim), (parts,), jnp.float32, least / len(cuts), top_value / len(cuts))
        gain = gain * jnp.repeat(jnp.exp(steps), shape[dim] // parts).reshape((-1,) + (1,) * (len(shape) - 1 - dim))
    return gain


def normal_values(key, shape, deviation, most, cuts=(), dtype=jnp.bfloat16):
    level = block_scale(key, shape, cuts, -0.22, 0.18) if cuts else 1.0
    result = jax.random.normal(key, shape, jnp.float32) * deviation * level
    return jnp.minimum(jnp.maximum(result, -most), most).astype(dtype)


def setup_inputs(seed: int = 0) -> dict:
    key_list = jax.random.split(jax.random.key(seed), 7)
    query_rows = normal_values(key_list[0], (SEQ_LEN, HEADS * HDIM), 1.0, 6.0, ((0, 8), (1, 4)))
    key_rows = normal_values(key_list[1], (SEQ_LEN, HEADS * HDIM), 1.0, 6.0, ((0, 8), (1, 4)))
    value_rows = normal_values(key_list[2], (SEQ_LEN, HEADS * HDIM), 1.0, 6.0, ((0, 8), (1, 4)))
    frequencies = normal_values(key_list[3], (HEADS, HDIM, NFREQ), 0.7, 4.1875, ((0, 4),))
    norm_gain = jnp.clip(1.0 + 0.15 * jax.random.normal(key_list[4], (HEADS * HDIM,), jnp.float32), 0.25, 1.75).astype(jnp.bfloat16)
    out_weight = normal_values(key_list[5], (HEADS * HDIM, D), (HEADS * HDIM) ** -0.5, 0.09375, ((1, 4),))
    return dict(query_rows=query_rows, key_rows=key_rows, value_rows=value_rows, frequencies=frequencies, norm_gain=norm_gain, out_weight=out_weight)


def features_of(inputs, frequencies):
    phases = jnp.einsum('thd,hdf->thf', inputs.astype(jnp.float32), frequencies.astype(jnp.float32))
    joined = jnp.concatenate([jnp.cos(phases), jnp.sin(phases)], axis=-1)
    return (joined * (1.0 / math.sqrt(NFREQ))).astype(jnp.bfloat16)

def reference(query_rows, key_rows, value_rows, frequencies, norm_gain, out_weight):
    span_count = SEQ_LEN // BLOCK
    span_shape = (span_count, BLOCK, HEADS, HDIM)
    query_spans = query_rows.reshape(span_shape)
    key_spans = key_rows.reshape(span_shape)
    value_spans = value_rows.reshape(span_shape)
    gain_table = norm_gain.astype(jnp.float32).reshape(HEADS, HDIM)
    causal = jnp.arange(BLOCK)[:, None] >= jnp.arange(BLOCK)[None, :]

    def advance(running, pieces):
        query_part, key_part, value_part = pieces
        query_feat = features_of(query_part, frequencies).astype(jnp.float32)
        key_feat = features_of(key_part, frequencies).astype(jnp.float32)
        value_wide = value_part.astype(jnp.float32)
        carried_low = running.astype(jnp.bfloat16)
        scores = jnp.einsum('thf,shf->hts', query_feat, key_feat)
        scores = jnp.where(causal[None], scores, jnp.zeros_like(scores)).astype(jnp.bfloat16)
        local_part = jnp.einsum('hts,shd->thd', scores.astype(jnp.float32), value_wide)
        prior_part = jnp.einsum('thf,hfd->thd', query_feat, carried_low.astype(jnp.float32))
        attended = local_part + prior_part
        mean_square = lax.optimization_barrier(jnp.mean(attended * attended, axis=-1, keepdims=True))
        normed = (attended * lax.rsqrt(mean_square + 1e-06) * gain_table[None]).astype(jnp.bfloat16)
        projected_part = jnp.dot(normed.reshape(BLOCK, HEADS * HDIM), out_weight, preferred_element_type=jnp.float32).astype(jnp.bfloat16)
        updated = running + jnp.einsum('thf,thd->hfd', key_feat, value_wide)
        return (updated, projected_part)
    start_state = jnp.zeros((HEADS, FEATS, HDIM), jnp.float32)
    _, projected = lax.scan(advance, start_state, (query_spans, key_spans, value_spans))
    return projected.reshape(SEQ_LEN, D)
```

```python
import functools
import math

import jax
import jax.numpy as jnp
from jax import lax
from jax.experimental import pallas as pl
from jax.experimental.pallas import tpu as pltpu
from jax.sharding import PartitionSpec as P

F32 = jnp.float32
BF16 = jnp.bfloat16
SPAN = 512
TILE = 256
SIN_TERMS = (3.1415820220956054, -5.167142794166117, 2.5418990064386224, -0.5546361406826548)
COS_TERMS = (0.9999932955183647, -4.933938020185013, 4.0412838463445455, -1.2221270624224843)
ROUNDER = 1.5 * 2.0**23


def dot(a, b, contract):
    return lax.dot_general(a, b, ((contract[:1], contract[1:]), ((), ())), preferred_element_type=F32)


def poly(terms, scale, u):
    value = F32(terms[-1] * scale)
    for term in terms[-2::-1]:
        value = value * u + F32(term * scale)
    return value


def cos_sin(phase, amplitude):
    turns = phase * F32(1.0 / (2.0 * math.pi))
    part = turns - ((turns + F32(ROUNDER)) - F32(ROUNDER))
    u = part * part
    scale = math.sqrt(2.0 * amplitude)
    half_sin = poly(SIN_TERMS, scale, u) * part
    half_cos = poly(COS_TERMS, scale, u)
    return F32(amplitude) - half_sin * half_sin, half_sin * half_cos


def key_kernel(key_ref, value_ref, freq_ref, feat_ref, total_ref, prefix_ref):
    rows, _ = key_ref.shape
    count = freq_ref.shape[2]
    span = min(SPAN, rows)
    amplitude = 1.0 / math.sqrt(count)
    for start in range(0, rows, TILE):
        cols = slice(start, start + TILE)
        phase = dot(freq_ref[0], key_ref[cols, :], (0, 1))
        cosine, sine = cos_sin(phase, amplitude)
        feat_ref[0, :count, cols] = cosine.astype(BF16)
        feat_ref[0, count:, cols] = sine.astype(BF16)
    running = None
    for index in range(rows // span):
        cols = slice(index * span, (index + 1) * span)
        state = dot(feat_ref[0, :, cols], value_ref[cols, :], (1, 0))
        running = state if running is None else running + state
        prefix_ref[0, index] = running
    total_ref[0] = running.astype(BF16)


def key_side(key_rows, value_rows, frequencies):
    rows = key_rows.shape[0]
    heads, width, count = frequencies.shape
    spans = rows // min(SPAN, rows)
    return pl.pallas_call(
        key_kernel,
        grid=(heads,),
        in_specs=[
            pl.BlockSpec((rows, width), lambda h: (0, h)),
            pl.BlockSpec((rows, width), lambda h: (0, h)),
            pl.BlockSpec((1, width, count), lambda h: (h, 0, 0)),
        ],
        out_specs=[
            pl.BlockSpec((1, 2 * count, rows), lambda h: (h, 0, 0)),
            pl.BlockSpec((1, 2 * count, width), lambda h: (h, 0, 0)),
            pl.BlockSpec((1, spans, 2 * count, width), lambda h: (h, 0, 0, 0)),
        ],
        out_shape=[
            jax.ShapeDtypeStruct((heads, 2 * count, rows), BF16),
            jax.ShapeDtypeStruct((heads, 2 * count, width), BF16),
            jax.ShapeDtypeStruct((heads, spans, 2 * count, width), F32),
        ],
        compiler_params=pltpu.CompilerParams(vmem_limit_bytes=40 << 20),
        cost_estimate=pl.CostEstimate(
            flops=2 * rows * heads * width * count * 3 + 25 * rows * heads * count,
            bytes_accessed=rows * heads * (4 * width + 4 * count),
            transcendentals=0,
        ),
        name="key_side",
    )(key_rows, value_rows, frequencies)


def query_kernel(query_ref, value_ref, freq_ref, key_feat_ref, feat_ref, local_ref):
    rows, _ = query_ref.shape
    count = freq_ref.shape[2]
    span = min(SPAN, rows)
    amplitude = 1.0 / math.sqrt(count)
    for start in range(0, rows, TILE):
        mine = slice(start, start + TILE)
        phase = dot(query_ref[mine, :], freq_ref[0], (1, 0))
        cosine, sine = cos_sin(phase, amplitude)
        feat_ref[0, mine, :count] = cosine.astype(BF16)
        feat_ref[0, mine, count:] = sine.astype(BF16)
    below = lax.broadcasted_iota(jnp.int32, (TILE, TILE), 0)
    causal = below >= lax.broadcasted_iota(jnp.int32, (TILE, TILE), 1)
    for start in range(0, rows, TILE):
        mine = slice(start, start + TILE)
        total = None
        for other in range(start // span * span, start + TILE, TILE):
            theirs = slice(other, other + TILE)
            scores = dot(feat_ref[0, mine, :], key_feat_ref[0, :, theirs], (1, 0))
            if other == start:
                scores = jnp.where(causal, scores, F32(0.0))
            part = dot(scores.astype(BF16), value_ref[theirs, :], (1, 0))
            total = part if total is None else total + part
        local_ref[mine, :] = total


def query_side(query_rows, value_rows, frequencies, key_feat):
    rows = query_rows.shape[0]
    heads, width, count = frequencies.shape
    return pl.pallas_call(
        query_kernel,
        grid=(heads,),
        in_specs=[
            pl.BlockSpec((rows, width), lambda h: (0, h)),
            pl.BlockSpec((rows, width), lambda h: (0, h)),
            pl.BlockSpec((1, width, count), lambda h: (h, 0, 0)),
            pl.BlockSpec((1, 2 * count, rows), lambda h: (h, 0, 0)),
        ],
        out_specs=[
            pl.BlockSpec((1, rows, 2 * count), lambda h: (h, 0, 0)),
            pl.BlockSpec((rows, width), lambda h: (0, h)),
        ],
        out_shape=[
            jax.ShapeDtypeStruct((heads, rows, 2 * count), BF16),
            jax.ShapeDtypeStruct((rows, heads * width), F32),
        ],
        compiler_params=pltpu.CompilerParams(vmem_limit_bytes=40 << 20),
        cost_estimate=pl.CostEstimate(
            flops=2 * rows * heads * (width * count + 3 * SPAN * count) + 25 * rows * heads * count,
            bytes_accessed=rows * heads * (8 * width + 8 * count),
            transcendentals=0,
        ),
        name="query_side",
    )(query_rows, value_rows, frequencies, key_feat)


def finish_kernel(heads, span, first, feat_ref, local_ref, before_ref, prefix_ref, gain_ref, out_ref):
    rows = local_ref.shape[0]
    width = local_ref.shape[1] // heads
    step = min(TILE, span, rows)
    for head in range(heads):
        cols = slice(head * width, (head + 1) * width)
        gain = gain_ref[:, cols].astype(F32)
        for start in range(0, rows, step):
            mine = slice(start, start + step)
            block = (first + start) // span
            carried = before_ref[head]
            if block:
                carried = carried + prefix_ref[head, block - 1]
            attended = local_ref[mine, cols] + dot(feat_ref[head, mine, :], carried.astype(BF16), (1, 0))
            square = jnp.mean(attended * attended, axis=-1, keepdims=True)
            normed = attended * lax.rsqrt(square + F32(1e-6)) * gain
            out_ref[mine, cols] = normed.astype(BF16)


def finish(feat, local_part, before, prefix, gain, first, rows):
    heads, all_rows, feats = feat.shape
    width = local_part.shape[1] // heads
    spans = prefix.shape[1]
    span = all_rows // spans
    index = first // rows
    group = 4 if heads % 4 == 0 else heads
    return pl.pallas_call(
        functools.partial(finish_kernel, group, span, first),
        grid=(heads // group,),
        in_specs=[
            pl.BlockSpec((group, rows, feats), lambda h: (h, index, 0)),
            pl.BlockSpec((rows, group * width), lambda h: (index, h)),
            pl.BlockSpec((group, feats, width), lambda h: (h, 0, 0)),
            pl.BlockSpec((group, spans, feats, width), lambda h: (h, 0, 0, 0)),
            pl.BlockSpec((1, group * width), lambda h: (0, h)),
        ],
        out_specs=pl.BlockSpec((rows, group * width), lambda h: (0, h)),
        out_shape=jax.ShapeDtypeStruct((rows, heads * width), BF16),
        compiler_params=pltpu.CompilerParams(vmem_limit_bytes=40 << 20),
        cost_estimate=pl.CostEstimate(
            flops=2 * rows * heads * feats * width + 10 * rows * heads * width,
            bytes_accessed=rows * heads * (2 * feats + 6 * width) + 4 * heads * feats * width,
            transcendentals=0,
        ),
        name="finish",
    )(feat, local_part, before, prefix, gain.reshape(1, -1))


def earlier_sum(value, axis):
    count, mine = lax.axis_size(axis), lax.axis_index(axis)
    earlier = jnp.zeros(value.shape, F32)
    total = value.astype(F32)
    sent = value
    distance = 1
    while distance < count:
        pairs = [(i, i ^ distance) for i in range(count)]
        last = 2 * distance >= count
        if last:
            pairs = [(i, j) for i, j in pairs if i < j]
        theirs = lax.ppermute(sent, axis, pairs).astype(F32)
        earlier = earlier + jnp.where(mine & distance != 0, theirs, F32(0.0))
        if not last:
            total = total + theirs
            sent = total.astype(BF16)
        distance *= 2
    return earlier


def local(query_rows, key_rows, value_rows, frequencies, norm_gain, out_weight):
    rows = query_rows.shape[0]
    key_feat, total, prefix = key_side(key_rows, value_rows, frequencies)
    before = earlier_sum(total, "ctx")
    query_feat, local_part = query_side(query_rows, value_rows, frequencies, key_feat)
    normed = finish(query_feat, local_part, before, prefix, norm_gain, 0, rows)
    projected = jnp.dot(
        lax.all_gather(normed, "head", axis=1, tiled=True), out_weight, preferred_element_type=F32
    )
    return projected.astype(BF16)


def solution(mesh):
    return jax.shard_map(
        local,
        mesh=mesh,
        in_specs=(
            P("ctx", "head"),
            P("ctx", "head"),
            P("ctx", "head"),
            P("head", None, None),
            P("head"),
            P(None, "head"),
        ),
        out_specs=P("ctx", "head"),
        check_vma=False,
    )
```

```python
import functools
import math

import jax
import jax.numpy as jnp
from jax import lax
from jax.experimental import pallas as pl
from jax.experimental.pallas import tpu as pltpu
from jax.sharding import PartitionSpec as P

F32 = jnp.float32
BF16 = jnp.bfloat16
SPAN = 512
TILE = 256
SIN_TERMS = (3.1415820220956054, -5.167142794166117, 2.5418990064386224, -0.5546361406826548)
COS_TERMS = (0.9999932955183647, -4.933938020185013, 4.0412838463445455, -1.2221270624224843)
ROUNDER = 1.5 * 2.0**23
PARAMS = pltpu.CompilerParams(vmem_limit_bytes=56 << 20)
SIDE = [(0, 1), (1, 0), (2, 3), (3, 2)]
MIDDLE = [(1, 2), (2, 1)]
ACROSS = [(0, 2), (3, 1)]
INWARD = [(0, 1), (3, 2)]
OUTWARD = [(1, 0), (2, 3)]


def dot(a, b, contract):
    return lax.dot_general(a, b, ((contract[:1], contract[1:]), ((), ())), preferred_element_type=F32)


def poly(terms, scale, u):
    value = F32(terms[-1] * scale)
    for term in terms[-2::-1]:
        value = value * u + F32(term * scale)
    return value


def cos_sin(phase, amplitude):
    turns = phase * F32(1.0 / (2.0 * math.pi))
    part = turns - ((turns + F32(ROUNDER)) - F32(ROUNDER))
    u = part * part
    scale = math.sqrt(2.0 * amplitude)
    half_sin = poly(SIN_TERMS, scale, u) * part
    half_cos = poly(COS_TERMS, scale, u)
    return F32(amplitude) - half_sin * half_sin, half_sin * half_cos


def key_kernel(key_ref, value_ref, freq_ref, feat_ref, total_ref, prefix_ref):
    rows, _ = key_ref.shape
    count = freq_ref.shape[2]
    span = min(SPAN, rows)
    amplitude = 1.0 / math.sqrt(count)
    for start in range(0, rows, TILE):
        cols = slice(start, start + TILE)
        phase = dot(freq_ref[0], key_ref[cols, :], (0, 1))
        cosine, sine = cos_sin(phase, amplitude)
        feat_ref[0, :count, cols] = cosine.astype(BF16)
        feat_ref[0, count:, cols] = sine.astype(BF16)
    running = None
    for index in range(rows // span):
        cols = slice(index * span, (index + 1) * span)
        state = dot(feat_ref[0, :, cols], value_ref[cols, :], (1, 0))
        running = state if running is None else running + state
        prefix_ref[0, index] = running
    total_ref[0] = running.astype(BF16)


def key_side(key_rows, value_rows, frequencies, first, last):
    rows = key_rows.shape[0]
    _, width, count = frequencies.shape
    heads = last - first
    spans = rows // min(SPAN, rows)
    return pl.pallas_call(
        key_kernel,
        grid=(heads,),
        in_specs=[
            pl.BlockSpec((rows, width), lambda h: (0, h + first)),
            pl.BlockSpec((rows, width), lambda h: (0, h + first)),
            pl.BlockSpec((1, width, count), lambda h: (h + first, 0, 0)),
        ],
        out_specs=[
            pl.BlockSpec((1, 2 * count, rows), lambda h: (h, 0, 0)),
            pl.BlockSpec((1, 2 * count, width), lambda h: (h, 0, 0)),
            pl.BlockSpec((1, spans, 2 * count, width), lambda h: (h, 0, 0, 0)),
        ],
        out_shape=[
            jax.ShapeDtypeStruct((heads, 2 * count, rows), BF16),
            jax.ShapeDtypeStruct((heads, 2 * count, width), BF16),
            jax.ShapeDtypeStruct((heads, spans, 2 * count, width), F32),
        ],
        compiler_params=PARAMS,
        cost_estimate=pl.CostEstimate(
            flops=2 * rows * heads * width * count * 3 + 25 * rows * heads * count,
            bytes_accessed=rows * heads * (4 * width + 4 * count),
            transcendentals=0,
        ),
        name="key_side",
    )(key_rows, value_rows, frequencies)


def query_kernel(query_ref, value_ref, freq_ref, key_feat_ref, feat_ref, local_ref):
    rows, _ = query_ref.shape
    count = freq_ref.shape[2]
    span = min(SPAN, rows)
    amplitude = 1.0 / math.sqrt(count)
    for start in range(0, rows, TILE):
        mine = slice(start, start + TILE)
        phase = dot(query_ref[mine, :], freq_ref[0], (1, 0))
        cosine, sine = cos_sin(phase, amplitude)
        feat_ref[0, mine, :count] = cosine.astype(BF16)
        feat_ref[0, mine, count:] = sine.astype(BF16)
    below = lax.broadcasted_iota(jnp.int32, (TILE, TILE), 0)
    causal = below >= lax.broadcasted_iota(jnp.int32, (TILE, TILE), 1)
    for start in range(0, rows, TILE):
        mine = slice(start, start + TILE)
        total = None
        for other in range(start // span * span, start + TILE, TILE):
            theirs = slice(other, other + TILE)
            scores = dot(feat_ref[0, mine, :], key_feat_ref[0, :, theirs], (1, 0))
            if other == start:
                scores = jnp.where(causal, scores, F32(0.0))
            part = dot(scores.astype(BF16), value_ref[theirs, :], (1, 0))
            total = part if total is None else total + part
        local_ref[mine, :] = total


def query_side(query_rows, value_rows, frequencies, key_feat, first, last):
    rows = query_rows.shape[0]
    _, width, count = frequencies.shape
    heads = last - first
    return pl.pallas_call(
        query_kernel,
        grid=(heads,),
        in_specs=[
            pl.BlockSpec((rows, width), lambda h: (0, h + first)),
            pl.BlockSpec((rows, width), lambda h: (0, h + first)),
            pl.BlockSpec((1, width, count), lambda h: (h + first, 0, 0)),
            pl.BlockSpec((1, 2 * count, rows), lambda h: (h, 0, 0)),
        ],
        out_specs=[
            pl.BlockSpec((1, rows, 2 * count), lambda h: (h, 0, 0)),
            pl.BlockSpec((rows, width), lambda h: (0, h)),
        ],
        out_shape=[
            jax.ShapeDtypeStruct((heads, rows, 2 * count), BF16),
            jax.ShapeDtypeStruct((rows, heads * width), F32),
        ],
        compiler_params=PARAMS,
        cost_estimate=pl.CostEstimate(
            flops=2 * rows * heads * (width * count + 3 * SPAN * count) + 25 * rows * heads * count,
            bytes_accessed=rows * heads * (8 * width + 8 * count),
            transcendentals=0,
        ),
        name="query_side",
    )(query_rows, value_rows, frequencies, key_feat)


def finish_kernel(heads, span, cuts, feat_ref, local_ref, before_ref, prefix_ref, gain_ref, *out_refs):
    rows = local_ref.shape[0]
    width = local_ref.shape[1] // heads
    for out_ref, (first, last) in zip(out_refs, cuts):
        step = min(TILE, last - first)
        for head in range(heads):
            cols = slice(head * width, (head + 1) * width)
            gain = gain_ref[:, cols].astype(F32)
            for start in range(first, last, step):
                mine = slice(start, start + step)
                carried = before_ref[head]
                if start // span:
                    carried = carried + prefix_ref[head, start // span - 1]
                prior = dot(feat_ref[head, mine, :], carried.astype(BF16), (1, 0))
                attended = local_ref[mine, cols] + prior
                square = jnp.mean(attended * attended, axis=-1, keepdims=True)
                normed = attended * lax.rsqrt(square + F32(1e-6)) * gain
                out_ref[start - first : start - first + step, cols] = normed.astype(BF16)


def finish(feat, local_part, before, prefix, gain, cuts):
    heads, rows, feats = feat.shape
    width = local_part.shape[1] // heads
    spans = prefix.shape[1]
    group = 2 if heads % 2 == 0 else 1
    return pl.pallas_call(
        functools.partial(finish_kernel, group, rows // spans, cuts),
        grid=(heads // group,),
        in_specs=[
            pl.BlockSpec((group, rows, feats), lambda h: (h, 0, 0)),
            pl.BlockSpec((rows, group * width), lambda h: (0, h)),
            pl.BlockSpec((group, feats, width), lambda h: (h, 0, 0)),
            pl.BlockSpec((group, spans, feats, width), lambda h: (h, 0, 0, 0)),
            pl.BlockSpec((1, group * width), lambda h: (0, h)),
        ],
        out_specs=[pl.BlockSpec((last - first, group * width), lambda h: (0, h)) for first, last in cuts],
        out_shape=[jax.ShapeDtypeStruct((last - first, heads * width), BF16) for first, last in cuts],
        compiler_params=PARAMS,
        cost_estimate=pl.CostEstimate(
            flops=2 * rows * heads * feats * width + 10 * rows * heads * width,
            bytes_accessed=rows * heads * (2 * feats + 6 * width) + 4 * heads * feats * width,
            transcendentals=0,
        ),
        name="finish",
    )(feat, local_part, before, prefix, gain)


def project_kernel(sources, has_added, order_ref, *refs):
    early, late, weights = refs[:sources], refs[sources : 2 * sources], refs[2 * sources : 3 * sources]
    out_ref = refs[-1]
    cut = early[0].shape[1]
    total = refs[3 * sources][...].astype(F32) if has_added else None
    for x_ref, y_ref, w_ref in zip(early, late, weights):
        part = dot(x_ref[...], w_ref[:cut, :], (1, 0)) + dot(y_ref[...], w_ref[cut:, :], (1, 0))
        total = part if total is None else total + part
    out_ref[...] = total.astype(out_ref.dtype)


def project(early, late, weight, order, first, size, added=None, into=None, rows=None):
    sources = len(early)
    late_cols = late[0].shape[1]
    cut = early[0].shape[1]
    depth, cols = cut + late_cols, weight.shape[1]
    step = min(256, cols)
    index = first // size
    whole = rows is not None
    in_specs = [pl.BlockSpec((size, cut), lambda n, o: (index, 0)) for _ in early]
    for block in late:
        place = index if block.shape[0] > size else 0
        in_specs.append(pl.BlockSpec((size, late_cols), lambda n, o, i=place: (i, 0)))
    in_specs += [pl.BlockSpec((depth, step), lambda n, o, s=s: (o[s], n)) for s in range(sources)]
    operands = [order, *early, *late] + [weight] * sources
    if added is not None:
        in_specs.append(pl.BlockSpec((size, step), lambda n, o: (0, n)))
        operands.append(added)
    aliases = {}
    if into is not None:
        aliases = {len(operands): 0}
        in_specs.append(pl.BlockSpec(memory_space=pl.ANY))
        operands.append(into)
    out_rows = rows if whole else size
    out_index = index if whole else 0
    return pl.pallas_call(
        functools.partial(project_kernel, sources, added is not None),
        grid_spec=pltpu.PrefetchScalarGridSpec(
            num_scalar_prefetch=1,
            grid=(cols // step,),
            in_specs=in_specs,
            out_specs=pl.BlockSpec((size, step), lambda n, o: (out_index, n)),
        ),
        out_shape=jax.ShapeDtypeStruct((out_rows, cols), BF16),
        input_output_aliases=aliases,
        compiler_params=PARAMS,
        cost_estimate=pl.CostEstimate(
            flops=2 * size * sources * depth * cols,
            bytes_accessed=2 * sources * depth * (size + cols) + 4 * size * cols,
            transcendentals=0,
        ),
        name="project",
    )(*operands)


def earlier_sum(value, axis):
    count, mine = lax.axis_size(axis), lax.axis_index(axis)
    earlier = jnp.zeros(value.shape, F32)
    total = value.astype(F32)
    sent = value
    marks = []
    distance = 1
    while distance < count:
        pairs = [(i, i ^ distance) for i in range(count)]
        last = 2 * distance >= count
        if last:
            pairs = [(i, j) for i, j in pairs if i < j]
        theirs = lax.ppermute(sent, axis, pairs).astype(F32)
        earlier = earlier + jnp.where(mine & distance != 0, theirs, F32(0.0))
        if not last:
            total = total + theirs
            sent = total.astype(BF16)
            marks.append(sent)
        distance *= 2
    return earlier, marks


def far_weight(out_weight):
    count, mine = lax.axis_size("ctx"), lax.axis_index("ctx")
    place = lax.axis_index("head")
    depth = out_weight.shape[0] // 4
    piece = 2 * depth // count
    block = jnp.where(mine < count // 2, place ^ 2, place ^ 3)
    first = block * depth + (mine % (count // 2)) * piece
    share = lax.dynamic_slice_in_dim(out_weight, first, piece, axis=0)
    return lax.ppermute(share, "head", INWARD)


def after(value, *others):
    return lax.optimization_barrier((value, *others))[0]


def gain_of(norm_gain, width, first, last):
    return norm_gain[first * width : last * width].reshape(1, -1)


def line_of_four(query_rows, key_rows, value_rows, frequencies, norm_gain, out_weight):
    rows = query_rows.shape[0]
    heads, width, _ = frequencies.shape
    place = lax.axis_index("head")
    sizes = [rows // 4] * 3 + [rows // 8] * 2
    edges = [sum(sizes[:i]) for i in range(len(sizes) + 1)]
    whole = (0, rows)
    cuts = tuple(zip(edges[:-1], edges[1:]))
    split = heads // 4

    share = far_weight(out_weight)
    key_feat, total, prefix = key_side(key_rows, value_rows, frequencies, 0, split)
    before, marks = earlier_sum(total, "ctx")
    query_feat, local_part = query_side(
        query_rows, value_rows, after(frequencies, marks[0]), key_feat, 0, split
    )
    late_freq = after(frequencies, marks[-1], query_feat)
    late_feat, late_total, late_prefix = key_side(key_rows, value_rows, late_freq, split, heads)
    (early,) = finish(query_feat, local_part, before, prefix, gain_of(norm_gain, width, 0, split), (whole,))

    before, marks = earlier_sum(after(late_total, early, share), "ctx")
    query_feat, local_part = query_side(
        query_rows, value_rows, after(frequencies, marks[0], early), late_feat, split, heads
    )
    gain = gain_of(norm_gain, width, split, heads)
    blocks = finish(query_feat, local_part, before, late_prefix, gain, cuts)
    far = lax.all_gather(after(share, before), "ctx", axis=0, tiled=True)

    def spread(block):
        return [block] + [lax.ppermute(block, "head", pairs) for pairs in (SIDE, MIDDLE, ACROSS)]

    order = jnp.stack([place, place ^ 1, place ^ 3, place ^ 2]).astype(jnp.int32)
    both = jnp.arange(2, dtype=jnp.int32)
    early = spread(early)
    travelled = [early]
    out = None
    finished = []
    for index, (first, last) in enumerate(cuts):
        block = blocks[index]
        if index:
            block = after(block, *travelled[index - 1][1:])
        if index > 2:
            block = after(block, finished[index - 3])
        late = spread(block)
        travelled.append(late)
        partial = project(early[2:], late[2:], far, both, first, last - first)
        partial = lax.ppermute(partial, "head", OUTWARD)
        out = project(early, late, out_weight, order, first, last - first, added=partial, into=out, rows=rows)
        finished.append(out)
    return out


def any_line(query_rows, key_rows, value_rows, frequencies, norm_gain, out_weight):
    rows, heads = query_rows.shape[0], frequencies.shape[0]
    key_feat, total, prefix = key_side(key_rows, value_rows, frequencies, 0, heads)
    before, _ = earlier_sum(total, "ctx")
    query_feat, local_part = query_side(query_rows, value_rows, frequencies, key_feat, 0, heads)
    gain = norm_gain.reshape(1, -1)
    (normed,) = finish(query_feat, local_part, before, prefix, gain, ((0, rows),))
    gathered = lax.all_gather(normed, "head", axis=1, tiled=True)
    return jnp.dot(gathered, out_weight, preferred_element_type=F32).astype(BF16)


def solution(mesh):
    return jax.shard_map(
        line_of_four if mesh.shape["head"] == 4 else any_line,
        mesh=mesh,
        in_specs=(
            P("ctx", "head"),
            P("ctx", "head"),
            P("ctx", "head"),
            P("head", None, None),
            P("head"),
            P(None, "head"),
        ),
        out_specs=P("ctx", "head"),
        check_vma=False,
    )
```

```python
import functools
import math

import jax
import jax.numpy as jnp
from jax import lax
from jax.experimental import pallas as pl
from jax.experimental.pallas import tpu as pltpu
from jax.sharding import PartitionSpec as P

F32 = jnp.float32
BF16 = jnp.bfloat16
SPAN = 512
TILE = 256
SIN_TERMS = (3.1415820220956054, -5.167142794166117, 2.5418990064386224, -0.5546361406826548)
COS_TERMS = (0.9999932955183647, -4.933938020185013, 4.0412838463445455, -1.2221270624224843)
ROUNDER = 1.5 * 2.0**23
PARAMS = pltpu.CompilerParams(vmem_limit_bytes=56 << 20)


def dot(a, b, contract):
    return lax.dot_general(a, b, ((contract[:1], contract[1:]), ((), ())), preferred_element_type=F32)


def poly(terms, scale, u):
    value = F32(terms[-1] * scale)
    for term in terms[-2::-1]:
        value = value * u + F32(term * scale)
    return value


def cos_sin(phase, amplitude):
    turns = phase * F32(1.0 / (2.0 * math.pi))
    part = turns - ((turns + F32(ROUNDER)) - F32(ROUNDER))
    u = part * part
    scale = math.sqrt(2.0 * amplitude)
    half_sin = poly(SIN_TERMS, scale, u) * part
    half_cos = poly(COS_TERMS, scale, u)
    return F32(amplitude) - half_sin * half_sin, half_sin * half_cos


def key_kernel(core_ref, key_ref, value_ref, freq_ref, feat_ref, sent_ref, kept_ref, prefix_ref):
    rows, _ = key_ref.shape
    count = freq_ref.shape[2]
    span = min(SPAN, rows)
    amplitude = 1.0 / math.sqrt(count)
    for start in range(0, rows, TILE):
        cols = slice(start, start + TILE)
        phase = dot(freq_ref[0], key_ref[cols, :], (0, 1))
        cosine, sine = cos_sin(phase, amplitude)
        feat_ref[0, :count, cols] = cosine.astype(BF16)
        feat_ref[0, count:, cols] = sine.astype(BF16)
    running = None
    for index in range(rows // span):
        cols = slice(index * span, (index + 1) * span)
        state = dot(feat_ref[0, :, cols], value_ref[cols, :], (1, 0))
        running = state if running is None else running + state
        prefix_ref[0, index] = running
    half = pl.num_programs(0) // 2

    @pl.when(pl.program_id(0) < half)
    def _():
        sent_ref[0] = running.astype(BF16)

    @pl.when(pl.program_id(0) >= half)
    def _():
        kept_ref[0] = running.astype(BF16)


def key_side(core, key_rows, value_rows, frequencies):
    rows = key_rows.shape[0]
    heads, width, count = frequencies.shape
    spans = rows // min(SPAN, rows)
    half = heads // 2

    def head(g, c):
        return (g + half * (1 - c[0])) % heads

    return pl.pallas_call(
        key_kernel,
        grid_spec=pltpu.PrefetchScalarGridSpec(
            num_scalar_prefetch=1,
            grid=(heads,),
            in_specs=[
                pl.BlockSpec((rows, width), lambda g, c: (0, head(g, c))),
                pl.BlockSpec((rows, width), lambda g, c: (0, head(g, c))),
                pl.BlockSpec((1, width, count), lambda g, c: (head(g, c), 0, 0)),
            ],
            out_specs=[
                pl.BlockSpec((1, 2 * count, rows), lambda g, c: (head(g, c), 0, 0)),
                pl.BlockSpec((1, 2 * count, width), lambda g, c: (jnp.minimum(g, half - 1), 0, 0)),
                pl.BlockSpec((1, 2 * count, width), lambda g, c: (jnp.maximum(g - half, 0), 0, 0)),
                pl.BlockSpec((1, spans, 2 * count, width), lambda g, c: (head(g, c), 0, 0, 0)),
            ],
        ),
        out_shape=[
            jax.ShapeDtypeStruct((heads, 2 * count, rows), BF16),
            jax.ShapeDtypeStruct((half, 2 * count, width), BF16),
            jax.ShapeDtypeStruct((half, 2 * count, width), BF16),
            jax.ShapeDtypeStruct((heads, spans, 2 * count, width), F32),
        ],
        compiler_params=PARAMS,
        cost_estimate=pl.CostEstimate(
            flops=2 * rows * heads * width * count * 3 + 25 * rows * heads * count,
            bytes_accessed=rows * heads * (4 * width + 4 * count),
            transcendentals=0,
        ),
        name="key_side",
    )(core, key_rows, value_rows, frequencies)


def query_kernel(query_ref, value_ref, freq_ref, key_feat_ref, feat_ref, local_ref):
    rows, _ = query_ref.shape
    count = freq_ref.shape[2]
    span = min(SPAN, rows)
    amplitude = 1.0 / math.sqrt(count)
    for start in range(0, rows, TILE):
        mine = slice(start, start + TILE)
        phase = dot(query_ref[mine, :], freq_ref[0], (1, 0))
        cosine, sine = cos_sin(phase, amplitude)
        feat_ref[0, mine, :count] = cosine.astype(BF16)
        feat_ref[0, mine, count:] = sine.astype(BF16)
    below = lax.broadcasted_iota(jnp.int32, (TILE, TILE), 0)
    causal = below >= lax.broadcasted_iota(jnp.int32, (TILE, TILE), 1)
    for start in range(0, rows, TILE):
        mine = slice(start, start + TILE)
        total = None
        for other in range(start // span * span, start + TILE, TILE):
            theirs = slice(other, other + TILE)
            scores = dot(feat_ref[0, mine, :], key_feat_ref[0, :, theirs], (1, 0))
            if other == start:
                scores = jnp.where(causal, scores, F32(0.0))
            part = dot(scores.astype(BF16), value_ref[theirs, :], (1, 0))
            total = part if total is None else total + part
        local_ref[mine, :] = total


def query_side(query_rows, value_rows, frequencies, key_feat):
    rows = query_rows.shape[0]
    heads, width, count = frequencies.shape
    return pl.pallas_call(
        query_kernel,
        grid=(heads,),
        in_specs=[
            pl.BlockSpec((rows, width), lambda h: (0, h)),
            pl.BlockSpec((rows, width), lambda h: (0, h)),
            pl.BlockSpec((1, width, count), lambda h: (h, 0, 0)),
            pl.BlockSpec((1, 2 * count, rows), lambda h: (h, 0, 0)),
        ],
        out_specs=[
            pl.BlockSpec((1, rows, 2 * count), lambda h: (h, 0, 0)),
            pl.BlockSpec((rows, width), lambda h: (0, h)),
        ],
        out_shape=[
            jax.ShapeDtypeStruct((heads, rows, 2 * count), BF16),
            jax.ShapeDtypeStruct((rows, heads * width), F32),
        ],
        compiler_params=PARAMS,
        cost_estimate=pl.CostEstimate(
            flops=2 * rows * heads * (width * count + 3 * SPAN * count) + 25 * rows * heads * count,
            bytes_accessed=rows * heads * (8 * width + 8 * count),
            transcendentals=0,
        ),
        name="query_side",
    )(query_rows, value_rows, frequencies, key_feat)


def finish_kernel(
    heads, span, cuts, core_ref, feat_ref, local_ref, theirs_ref, mine_ref, prefix_ref, gain_ref, *out_refs
):
    width = local_ref.shape[1] // heads
    kept = pl.program_id(0) >= pl.num_programs(0) // 2
    for head in range(heads):
        cols = slice(head * width, (head + 1) * width)
        gain = gain_ref[:, cols].astype(F32)
        before = jnp.where(kept, mine_ref[head].astype(F32), theirs_ref[head].astype(F32))
        for out_ref, (first, last) in zip(out_refs, cuts):
            step = min(TILE, last - first)
            for start in range(first, last, step):
                mine = slice(start, start + step)
                carried = before
                if start // span:
                    carried = carried + prefix_ref[head, start // span - 1]
                prior = dot(feat_ref[head, mine, :], carried.astype(BF16), (1, 0))
                attended = local_ref[mine, cols] + prior
                square = jnp.mean(attended * attended, axis=-1, keepdims=True)
                normed = attended * lax.rsqrt(square + F32(1e-6)) * gain
                out_ref[start - first : start - first + step, cols] = normed.astype(BF16)


def finish(core, feat, local_part, theirs, mine, prefix, gain, cuts):
    heads, rows, feats = feat.shape
    width = local_part.shape[1] // heads
    spans = prefix.shape[1]
    half = heads // 2
    group = 2 if half % 2 == 0 else 1
    steps, half_steps = heads // group, half // group

    def block(g, c):
        return (g + half_steps * (1 - c[0])) % steps

    return pl.pallas_call(
        functools.partial(finish_kernel, group, rows // spans, cuts),
        grid_spec=pltpu.PrefetchScalarGridSpec(
            num_scalar_prefetch=1,
            grid=(steps,),
            in_specs=[
                pl.BlockSpec((group, rows, feats), lambda g, c: (block(g, c), 0, 0)),
                pl.BlockSpec((rows, group * width), lambda g, c: (0, block(g, c))),
                pl.BlockSpec((group, feats, width), lambda g, c: (jnp.minimum(g, half_steps - 1), 0, 0)),
                pl.BlockSpec((group, feats, width), lambda g, c: (jnp.maximum(g - half_steps, 0), 0, 0)),
                pl.BlockSpec((group, spans, feats, width), lambda g, c: (block(g, c), 0, 0, 0)),
                pl.BlockSpec((1, group * width), lambda g, c: (0, block(g, c))),
            ],
            out_specs=[
                pl.BlockSpec((last - first, group * width), lambda g, c: (0, block(g, c))) for first, last in cuts
            ],
        ),
        out_shape=[jax.ShapeDtypeStruct((last - first, heads * width), BF16) for first, last in cuts],
        compiler_params=PARAMS,
        cost_estimate=pl.CostEstimate(
            flops=2 * rows * heads * feats * width + 10 * rows * heads * width,
            bytes_accessed=rows * heads * (2 * feats + 6 * width) + 4 * heads * feats * width,
            transcendentals=0,
        ),
        name="finish",
    )(core, feat, local_part, theirs, mine, prefix, gain)


def project_kernel(sources, order_ref, *refs):
    out_ref = refs[-1]
    total = None
    for x_ref, w_ref in zip(refs[:sources], refs[sources : 2 * sources]):
        part = dot(x_ref[...], w_ref[...], (1, 0))
        total = part if total is None else total + part
    out_ref[...] = total.astype(out_ref.dtype)


def project(blocks, weight, order, dtype=BF16):
    size, depth = blocks[0].shape
    cols = weight.shape[1]
    sources = len(blocks)
    step = min(256, cols)
    in_specs = [pl.BlockSpec((size, depth), lambda n, o: (0, 0)) for _ in blocks]
    in_specs += [pl.BlockSpec((depth, step), lambda n, o, s=s: (o[s], n)) for s in range(sources)]
    return pl.pallas_call(
        functools.partial(project_kernel, sources),
        grid_spec=pltpu.PrefetchScalarGridSpec(
            num_scalar_prefetch=1,
            grid=(cols // step,),
            in_specs=in_specs,
            out_specs=pl.BlockSpec((size, step), lambda n, o: (0, n)),
        ),
        out_shape=jax.ShapeDtypeStruct((size, cols), dtype),
        compiler_params=PARAMS,
        cost_estimate=pl.CostEstimate(flops=0, bytes_accessed=0, transcendentals=0),
        name="project",
    )(order, *blocks, *[weight] * sources)


def join_kernel(a_ref, b_ref, *refs):
    out_ref = refs[-1]
    out_ref[...] = (a_ref[...] + b_ref[...].astype(F32)).astype(out_ref.dtype)


def join(a, b, first, rows, into=None):
    size, cols = a.shape
    step = min(128, size)
    index = first // step
    spec = pl.BlockSpec((step, cols), lambda r: (r, 0))
    return pl.pallas_call(
        join_kernel,
        grid=(size // step,),
        in_specs=[spec, spec] + [pl.BlockSpec(memory_space=pl.ANY)] * (into is not None),
        out_specs=pl.BlockSpec((step, cols), lambda r: (index + r, 0)),
        out_shape=jax.ShapeDtypeStruct((rows, cols), BF16),
        input_output_aliases={} if into is None else {2: 0},
        compiler_params=PARAMS,
        cost_estimate=pl.CostEstimate(flops=size * cols, bytes_accessed=8 * size * cols, transcendentals=0),
        name="join",
    )(a, b, *([] if into is None else [into]))


def after(value, *others):
    return lax.optimization_barrier((value, *others))[0]


def swap(value, axis, distance):
    return lax.ppermute(value, axis, [(i, i ^ distance) for i in range(lax.axis_size(axis))])


def earlier_states(sent, kept, meanwhile):
    count, mine = lax.axis_size("ctx"), lax.axis_index("ctx")
    core = mine % 2
    partner = swap(sent, "ctx", 1)
    total = (kept.astype(F32) + partner.astype(F32)).astype(BF16)
    earlier = jnp.zeros(kept.shape, F32)
    beside = meanwhile(total)
    distance = 2
    while distance < count:
        radix = min(4, count // distance)
        last = distance * radix >= count
        added = total.astype(F32)
        for step in range(1, radix):
            hop = step * distance
            pairs = [(i, i ^ hop) for i in range(count) if not last or i < i ^ hop]
            theirs = lax.ppermute(total, "ctx", pairs)
            if last:
                theirs = after(theirs, *beside)
            theirs = theirs.astype(F32)
            lower = (mine ^ hop) < mine
            earlier = earlier + jnp.where(lower, theirs, F32(0.0))
            added = added + theirs
        total = added.astype(BF16)
        distance *= radix
    own = earlier + jnp.where(core == 1, partner.astype(F32), F32(0.0))
    given = earlier + jnp.where(core == 0, kept.astype(F32), F32(0.0))
    return swap(given.astype(BF16), "ctx", 1), own.astype(BF16), beside


def weight_share(out_weight, hop):
    count, mine = lax.axis_size("ctx"), lax.axis_index("ctx")
    place = lax.axis_index("head")
    depth = out_weight.shape[0] // 4
    piece = 2 * depth // count
    block = jnp.where(mine < count // 2, place ^ hop, place ^ 3)
    first = block * depth + (mine % (count // 2)) * piece
    return swap(lax.dynamic_slice_in_dim(out_weight, first, piece, axis=0), "head", hop)


def normed_output(query_rows, key_rows, value_rows, frequencies, norm_gain, cuts):
    core = (lax.axis_index("ctx") % 2).astype(jnp.int32).reshape(1)
    key_feat, sent, kept, prefix = key_side(core, key_rows, value_rows, frequencies)

    def meanwhile(total):
        return query_side(query_rows, value_rows, after(frequencies, total), key_feat)

    theirs, own, (query_feat, local_part) = earlier_states(sent, kept, meanwhile)
    return finish(core, query_feat, local_part, theirs, own, prefix, norm_gain.reshape(1, -1), cuts), own


def line_of_four(query_rows, key_rows, value_rows, frequencies, norm_gain, out_weight):
    rows = query_rows.shape[0]
    place = lax.axis_index("head")
    half, quarter = rows // 2, rows // 4
    cuts = ((0, half), (half, half + quarter), (half + quarter, rows))
    far_share = weight_share(out_weight, 2)
    near_share = weight_share(out_weight, 1)
    (one, *two), own = normed_output(query_rows, key_rows, value_rows, frequencies, norm_gain, cuts)
    far = lax.all_gather(after(far_share, own), "ctx", axis=0, tiled=True)
    near = lax.all_gather(after(near_share, one), "ctx", axis=0, tiled=True)

    both = jnp.arange(2, dtype=jnp.int32)
    far_order = jnp.stack([place, place ^ 2]).astype(jnp.int32)
    near_order = jnp.stack([place, place ^ 1]).astype(jnp.int32)
    one = [one, swap(one, "head", 2)]
    two = [[block, swap(block, "head", 1)] for block in two]
    two_partials = [project(block, far, both) for block in two]
    two_own = [project(block, out_weight, near_order, dtype=F32) for block in two]
    one_partial = project([one[0], after(one[1], *two_partials)], near, both)
    one_own = project(one, out_weight, far_order, dtype=F32)
    two_partials = [swap(partial, "head", 2) for partial in two_partials]
    one_partial = swap(one_partial, "head", 1)
    out = join(two_own[0], two_partials[0], half, rows)
    out = join(one_own, one_partial, 0, rows, out)
    return join(two_own[1], two_partials[1], half + quarter, rows, out)


def any_line(query_rows, key_rows, value_rows, frequencies, norm_gain, out_weight):
    cuts = ((0, query_rows.shape[0]),)
    (normed,), _ = normed_output(query_rows, key_rows, value_rows, frequencies, norm_gain, cuts)
    gathered = lax.all_gather(normed, "head", axis=1, tiled=True)
    return jnp.dot(gathered, out_weight, preferred_element_type=F32).astype(BF16)


def solution(mesh):
    return jax.shard_map(
        line_of_four if mesh.shape["head"] == 4 else any_line,
        mesh=mesh,
        in_specs=(
            P("ctx", "head"),
            P("ctx", "head"),
            P("ctx", "head"),
            P("head", None, None),
            P("head"),
            P(None, "head"),
        ),
        out_specs=P("ctx", "head"),
        check_vma=False,
    )
```

```python
import functools
import math

import jax
import jax.numpy as jnp
from jax import lax
from jax.experimental import pallas as pl
from jax.experimental.pallas import tpu as pltpu
from jax.sharding import PartitionSpec as P

F32 = jnp.float32
BF16 = jnp.bfloat16
SPAN = 512
TILE = 256
SIN_TERMS = (3.1415820220956054, -5.167142794166117, 2.5418990064386224, -0.5546361406826548)
COS_TERMS = (0.9999932955183647, -4.933938020185013, 4.0412838463445455, -1.2221270624224843)
ROUNDER = 1.5 * 2.0**23
LARGE = pltpu.CompilerParams(vmem_limit_bytes=56 << 20)
SMALL = pltpu.CompilerParams(vmem_limit_bytes=20 << 20)
FREE = pl.CostEstimate(flops=0, bytes_accessed=0, transcendentals=0)


def dot(a, b, contract):
    return lax.dot_general(a, b, ((contract[:1], contract[1:]), ((), ())), preferred_element_type=F32)


def poly(terms, scale, u):
    value = F32(terms[-1] * scale)
    for term in terms[-2::-1]:
        value = value * u + F32(term * scale)
    return value


def cos_sin(phase, amplitude):
    turns = phase * F32(1.0 / (2.0 * math.pi))
    part = turns - ((turns + F32(ROUNDER)) - F32(ROUNDER))
    u = part * part
    scale = math.sqrt(2.0 * amplitude)
    half_sin = poly(SIN_TERMS, scale, u) * part
    half_cos = poly(COS_TERMS, scale, u)
    return F32(amplitude) - half_sin * half_sin, half_sin * half_cos


def key_kernel(core_ref, key_ref, value_ref, freq_ref, feat_ref, sent_ref, kept_ref, prefix_ref):
    rows, _ = key_ref.shape
    count = freq_ref.shape[2]
    span = min(SPAN, rows)
    amplitude = 1.0 / math.sqrt(count)
    for start in range(0, rows, TILE):
        cols = slice(start, start + TILE)
        phase = dot(freq_ref[0], key_ref[cols, :], (0, 1))
        cosine, sine = cos_sin(phase, amplitude)
        feat_ref[0, :count, cols] = cosine.astype(BF16)
        feat_ref[0, count:, cols] = sine.astype(BF16)
    running = None
    for index in range(rows // span):
        cols = slice(index * span, (index + 1) * span)
        state = dot(feat_ref[0, :, cols], value_ref[cols, :], (1, 0))
        running = state if running is None else running + state
        if index < prefix_ref.shape[1]:
            prefix_ref[0, index] = running
    half = pl.num_programs(0) // 2

    @pl.when(pl.program_id(0) < half)
    def _():
        sent_ref[0] = running.astype(BF16)

    @pl.when(pl.program_id(0) >= half)
    def _():
        kept_ref[0] = running.astype(BF16)


def key_side(core, key_rows, value_rows, frequencies):
    rows = key_rows.shape[0]
    heads, width, count = frequencies.shape
    prior = max(1, rows // min(SPAN, rows) - 1)
    half = heads // 2

    def head(g, c):
        return (g + half * (1 - c[0])) % heads

    return pl.pallas_call(
        key_kernel,
        grid_spec=pltpu.PrefetchScalarGridSpec(
            num_scalar_prefetch=1,
            grid=(heads,),
            in_specs=[
                pl.BlockSpec((rows, width), lambda g, c: (0, head(g, c))),
                pl.BlockSpec((rows, width), lambda g, c: (0, head(g, c))),
                pl.BlockSpec((1, width, count), lambda g, c: (head(g, c), 0, 0)),
            ],
            out_specs=[
                pl.BlockSpec((1, 2 * count, rows), lambda g, c: (head(g, c), 0, 0)),
                pl.BlockSpec((1, 2 * count, width), lambda g, c: (jnp.minimum(g, half - 1), 0, 0)),
                pl.BlockSpec((1, 2 * count, width), lambda g, c: (jnp.maximum(g - half, 0), 0, 0)),
                pl.BlockSpec((1, prior, 2 * count, width), lambda g, c: (head(g, c), 0, 0, 0)),
            ],
        ),
        out_shape=[
            jax.ShapeDtypeStruct((heads, 2 * count, rows), BF16),
            jax.ShapeDtypeStruct((half, 2 * count, width), BF16),
            jax.ShapeDtypeStruct((half, 2 * count, width), BF16),
            jax.ShapeDtypeStruct((heads, prior, 2 * count, width), F32),
        ],
        compiler_params=LARGE,
        cost_estimate=FREE,
        name="key_side",
    )(core, key_rows, value_rows, frequencies)


def query_kernel(query_ref, value_ref, freq_ref, key_feat_ref, feat_ref, local_ref):
    rows, _ = query_ref.shape
    count = freq_ref.shape[2]
    span = min(SPAN, rows)
    amplitude = 1.0 / math.sqrt(count)
    for start in range(0, rows, TILE):
        mine = slice(start, start + TILE)
        phase = dot(query_ref[mine, :], freq_ref[0], (1, 0))
        cosine, sine = cos_sin(phase, amplitude)
        feat_ref[0, mine, :count] = cosine.astype(BF16)
        feat_ref[0, mine, count:] = sine.astype(BF16)
    below = lax.broadcasted_iota(jnp.int32, (TILE, TILE), 0)
    causal = below >= lax.broadcasted_iota(jnp.int32, (TILE, TILE), 1)
    for start in range(0, rows, TILE):
        mine = slice(start, start + TILE)
        total = None
        for other in range(start // span * span, start + TILE, TILE):
            theirs = slice(other, other + TILE)
            scores = dot(feat_ref[0, mine, :], key_feat_ref[0, :, theirs], (1, 0))
            if other == start:
                scores = jnp.where(causal, scores, F32(0.0))
            part = dot(scores.astype(BF16), value_ref[theirs, :], (1, 0))
            total = part if total is None else total + part
        local_ref[mine, :] = total


def query_side(query_rows, value_rows, frequencies, key_feat):
    rows = query_rows.shape[0]
    heads, width, count = frequencies.shape
    return pl.pallas_call(
        query_kernel,
        grid=(heads,),
        in_specs=[
            pl.BlockSpec((rows, width), lambda h: (0, h)),
            pl.BlockSpec((rows, width), lambda h: (0, h)),
            pl.BlockSpec((1, width, count), lambda h: (h, 0, 0)),
            pl.BlockSpec((1, 2 * count, rows), lambda h: (h, 0, 0)),
        ],
        out_specs=[
            pl.BlockSpec((1, rows, 2 * count), lambda h: (h, 0, 0)),
            pl.BlockSpec((rows, width), lambda h: (0, h)),
        ],
        out_shape=[
            jax.ShapeDtypeStruct((heads, rows, 2 * count), BF16),
            jax.ShapeDtypeStruct((rows, heads * width), F32),
        ],
        compiler_params=SMALL,
        cost_estimate=FREE,
        name="query_side",
    )(query_rows, value_rows, frequencies, key_feat)


def finish_kernel(
    heads, span, cuts, core_ref, feat_ref, local_ref, theirs_ref, mine_ref, prefix_ref, gain_ref, *out_refs
):
    width = local_ref.shape[1] // heads
    kept = pl.program_id(0) >= pl.num_programs(0) // 2
    for head in range(heads):
        cols = slice(head * width, (head + 1) * width)
        gain = gain_ref[:, cols].astype(F32)
        before = jnp.where(kept, mine_ref[head].astype(F32), theirs_ref[head].astype(F32))
        for out_ref, (first, last) in zip(out_refs, cuts):
            step = min(TILE, last - first)
            for start in range(first, last, step):
                mine = slice(start, start + step)
                carried = before
                if start // span:
                    carried = carried + prefix_ref[head, start // span - 1]
                prior = dot(feat_ref[head, mine, :], carried.astype(BF16), (1, 0))
                attended = local_ref[mine, cols] + prior
                square = jnp.mean(attended * attended, axis=-1, keepdims=True)
                normed = attended * lax.rsqrt(square + F32(1e-6)) * gain
                out_ref[start - first : start - first + step, cols] = normed.astype(BF16)


def finish(core, feat, local_part, theirs, mine, prefix, gain, cuts):
    heads, rows, feats = feat.shape
    width = local_part.shape[1] // heads
    prior = prefix.shape[1]
    half = heads // 2
    group = 2 if half % 2 == 0 else 1
    steps, half_steps = heads // group, half // group

    def block(g, c):
        return (g + half_steps * (1 - c[0])) % steps

    return pl.pallas_call(
        functools.partial(finish_kernel, group, min(SPAN, rows), cuts),
        grid_spec=pltpu.PrefetchScalarGridSpec(
            num_scalar_prefetch=1,
            grid=(steps,),
            in_specs=[
                pl.BlockSpec((group, rows, feats), lambda g, c: (block(g, c), 0, 0)),
                pl.BlockSpec((rows, group * width), lambda g, c: (0, block(g, c))),
                pl.BlockSpec((group, feats, width), lambda g, c: (jnp.minimum(g, half_steps - 1), 0, 0)),
                pl.BlockSpec((group, feats, width), lambda g, c: (jnp.maximum(g - half_steps, 0), 0, 0)),
                pl.BlockSpec((group, prior, feats, width), lambda g, c: (block(g, c), 0, 0, 0)),
                pl.BlockSpec((1, group * width), lambda g, c: (0, block(g, c))),
            ],
            out_specs=[
                pl.BlockSpec((last - first, group * width), lambda g, c: (0, block(g, c))) for first, last in cuts
            ],
        ),
        out_shape=[jax.ShapeDtypeStruct((last - first, heads * width), BF16) for first, last in cuts],
        compiler_params=SMALL,
        cost_estimate=FREE,
        name="finish",
    )(core, feat, local_part, theirs, mine, prefix, gain)


def project_kernel(sources, place_ref, *refs):
    out_ref = refs[-1]
    total = None
    for x_ref, w_ref in zip(refs[:sources], refs[sources : 2 * sources]):
        part = dot(x_ref[...], w_ref[...], (1, 0))
        total = part if total is None else total + part
    out_ref[...] = total.astype(out_ref.dtype)


def project(blocks, weight, place, hops, dtype=BF16):
    size, depth = blocks[0].shape
    cols = weight.shape[1]
    step = min(256, cols)

    def rows_of(source):
        if hops is None:
            return lambda n, p: (source, n)
        return lambda n, p: (p[0] ^ hops[source], n)

    sources = len(blocks)
    return pl.pallas_call(
        functools.partial(project_kernel, sources),
        grid_spec=pltpu.PrefetchScalarGridSpec(
            num_scalar_prefetch=1,
            grid=(cols // step,),
            in_specs=[pl.BlockSpec((size, depth), lambda n, p: (0, 0)) for _ in blocks]
            + [pl.BlockSpec((depth, step), rows_of(source)) for source in range(sources)],
            out_specs=pl.BlockSpec((size, step), lambda n, p: (0, n)),
        ),
        out_shape=jax.ShapeDtypeStruct((size, cols), dtype),
        compiler_params=SMALL,
        cost_estimate=FREE,
        name="project",
    )(place, *blocks, *[weight] * sources)


def join_kernel(a_ref, b_ref, *refs):
    out_ref = refs[-1]
    out_ref[...] = (a_ref[...] + b_ref[...].astype(F32)).astype(out_ref.dtype)


def join(a, b, first, rows, into=None):
    size, cols = a.shape
    step = min(128, size)
    index = first // step
    spec = pl.BlockSpec((step, cols), lambda r: (r, 0))
    return pl.pallas_call(
        join_kernel,
        grid=(size // step,),
        in_specs=[spec, spec] + [pl.BlockSpec(memory_space=pl.ANY)] * (into is not None),
        out_specs=pl.BlockSpec((step, cols), lambda r: (index + r, 0)),
        out_shape=jax.ShapeDtypeStruct((rows, cols), BF16),
        input_output_aliases={} if into is None else {2: 0},
        compiler_params=SMALL,
        cost_estimate=FREE,
        name="join",
    )(a, b, *([] if into is None else [into]))


def after(value, *others):
    return lax.optimization_barrier((value, *others))[0]


def swap(value, axis, distance):
    return lax.ppermute(value, axis, [(i, i ^ distance) for i in range(lax.axis_size(axis))])


def earlier_states(sent, kept, meanwhile):
    count, mine = lax.axis_size("ctx"), lax.axis_index("ctx")
    core = mine % 2
    partner = swap(sent, "ctx", 1)
    total = (kept.astype(F32) + partner.astype(F32)).astype(BF16)
    earlier = jnp.zeros(kept.shape, F32)
    beside = meanwhile(total)
    distance = 2
    while distance < count:
        radix = min(4, count // distance)
        last = distance * radix >= count
        added = total.astype(F32)
        for step in range(1, radix):
            hop = step * distance
            pairs = [(i, i ^ hop) for i in range(count) if not last or i < i ^ hop]
            theirs = lax.ppermute(total, "ctx", pairs)
            if last:
                theirs = after(theirs, *beside)
            theirs = theirs.astype(F32)
            lower = (mine ^ hop) < mine
            earlier = earlier + jnp.where(lower, theirs, F32(0.0))
            added = added + theirs
        total = added.astype(BF16)
        distance *= radix
    own = earlier + jnp.where(core == 1, partner.astype(F32), F32(0.0))
    given = earlier + jnp.where(core == 0, kept.astype(F32), F32(0.0))
    return swap(given.astype(BF16), "ctx", 1), own.astype(BF16), beside


def weight_share(out_weight, hop):
    chips, mine = lax.axis_size("ctx") // 2, lax.axis_index("ctx")
    place = lax.axis_index("head")
    depth = out_weight.shape[0] // 4
    piece = depth // chips
    block = jnp.where(mine % 2 == 0, place ^ hop, place ^ 3)
    first = block * depth + (mine // 2) * piece
    return swap(lax.dynamic_slice_in_dim(out_weight, first, piece, axis=0), "head", hop)


def gather_chips(share):
    count = lax.axis_size("ctx")
    same_core = [list(range(core, count, 2)) for core in range(2)]
    return lax.all_gather(share, "ctx", axis=0, tiled=True, axis_index_groups=same_core)


def gather_cores(block):
    same_chip = [[first, first + 1] for first in range(0, lax.axis_size("ctx"), 2)]
    return lax.all_gather(block, "ctx", axis=0, tiled=True, axis_index_groups=same_chip)


def normed_output(query_rows, key_rows, value_rows, frequencies, norm_gain, cuts, others=()):
    core = (lax.axis_index("ctx") % 2).astype(jnp.int32).reshape(1)
    key_feat, sent, kept, prefix = key_side(core, key_rows, value_rows, frequencies)

    def meanwhile(total):
        return *query_side(query_rows, value_rows, after(frequencies, total), key_feat), *others

    theirs, own, (query_feat, local_part, *others) = earlier_states(sent, kept, meanwhile)
    others = [after(other, own) for other in others]
    return finish(core, query_feat, local_part, theirs, own, prefix, norm_gain.reshape(1, -1), cuts), others


def line_of_four(query_rows, key_rows, value_rows, frequencies, norm_gain, out_weight):
    rows = query_rows.shape[0]
    place = lax.axis_index("head").astype(jnp.int32).reshape(1)
    quarter = rows // 4
    cuts = tuple((first, first + quarter) for first in range(0, rows, quarter))
    far_share = weight_share(out_weight, 2)
    near_share = weight_share(out_weight, 1)
    parts = (query_rows, key_rows, value_rows, frequencies, norm_gain)
    blocks, (near_share,) = normed_output(*parts, cuts, [near_share])
    near = gather_chips(near_share)
    far = gather_chips(after(far_share, blocks[0]))

    one = [[block, swap(block, "head", 2)] for block in blocks[:2]]
    two = [[block, swap(block, "head", 1)] for block in blocks[2:]]
    far, near = (gather_cores(after(block, one[0][1], two[0][1])) for block in (far, near))
    two_part = [project(block, far, place, None) for block in two]
    one_part = [project(one[0], near, place, None)]
    two_ready = two_part
    two_part = [swap(part, "head", 2) for part in two_part]
    one_part.append(project([one[1][0], after(one[1][1], two_part[0], two_ready[1])], near, place, None))
    one_part = [swap(part, "head", 1) for part in one_part]
    one_own = [project(block, out_weight, place, (0, 2), F32) for block in one]
    two_own = [project(block, out_weight, place, (0, 1), F32) for block in two]
    out = join(two_own[0], two_part[0], 2 * quarter, rows)
    out = join(one_own[0], one_part[0], 0, rows, out)
    out = join(two_own[1], two_part[1], 3 * quarter, rows, out)
    return join(one_own[1], one_part[1], quarter, rows, out)


def any_line(query_rows, key_rows, value_rows, frequencies, norm_gain, out_weight):
    cuts = ((0, query_rows.shape[0]),)
    (normed,), _ = normed_output(query_rows, key_rows, value_rows, frequencies, norm_gain, cuts)
    gathered = lax.all_gather(normed, "head", axis=1, tiled=True)
    return jnp.dot(gathered, out_weight, preferred_element_type=F32).astype(BF16)


def solution(mesh):
    return jax.shard_map(
        line_of_four if mesh.shape["head"] == 4 else any_line,
        mesh=mesh,
        in_specs=(
            P("ctx", "head"),
            P("ctx", "head"),
            P("ctx", "head"),
            P("head", None, None),
            P("head"),
            P(None, "head"),
        ),
        out_specs=P("ctx", "head"),
        check_vma=False,
    )
```

```python
import functools
import math

import jax
import jax.numpy as jnp
from jax import lax
from jax.experimental import pallas as pl
from jax.experimental.pallas import tpu as pltpu
from jax.sharding import PartitionSpec as P

F32 = jnp.float32
BF16 = jnp.bfloat16
SPAN = 512
TILE = 256
SIN_TERMS = (3.1415820220956054, -5.167142794166117, 2.5418990064386224, -0.5546361406826548)
COS_TERMS = (0.9999932955183647, -4.933938020185013, 4.0412838463445455, -1.2221270624224843)
ROUNDER = 1.5 * 2.0**23
LARGE = pltpu.CompilerParams(vmem_limit_bytes=56 << 20)
SMALL = pltpu.CompilerParams(vmem_limit_bytes=20 << 20)
FREE = pl.CostEstimate(flops=0, bytes_accessed=0, transcendentals=0)


def dot(a, b, contract):
    return lax.dot_general(a, b, ((contract[:1], contract[1:]), ((), ())), preferred_element_type=F32)


def poly(terms, scale, u):
    value = F32(terms[-1] * scale)
    for term in terms[-2::-1]:
        value = value * u + F32(term * scale)
    return value


def cos_sin(phase, amplitude):
    turns = phase * F32(1.0 / (2.0 * math.pi))
    part = turns - ((turns + F32(ROUNDER)) - F32(ROUNDER))
    u = part * part
    scale = math.sqrt(2.0 * amplitude)
    half_sin = poly(SIN_TERMS, scale, u) * part
    half_cos = poly(COS_TERMS, scale, u)
    return F32(amplitude) - half_sin * half_sin, half_sin * half_cos


def key_kernel(core_ref, key_ref, value_ref, freq_ref, feat_ref, sent_ref, kept_ref, prefix_ref):
    rows, _ = key_ref.shape
    count = freq_ref.shape[2]
    span = min(SPAN, rows)
    amplitude = 1.0 / math.sqrt(count)
    for start in range(0, rows, TILE):
        cols = slice(start, start + TILE)
        phase = dot(freq_ref[0], key_ref[cols, :], (0, 1))
        cosine, sine = cos_sin(phase, amplitude)
        feat_ref[0, :count, cols] = cosine.astype(BF16)
        feat_ref[0, count:, cols] = sine.astype(BF16)
    running = None
    for index in range(rows // span):
        cols = slice(index * span, (index + 1) * span)
        state = dot(feat_ref[0, :, cols], value_ref[cols, :], (1, 0))
        running = state if running is None else running + state
        if index < prefix_ref.shape[1]:
            prefix_ref[0, index] = running
    half = pl.num_programs(0) // 2

    @pl.when(pl.program_id(0) < half)
    def _():
        sent_ref[0] = running.astype(BF16)

    @pl.when(pl.program_id(0) >= half)
    def _():
        kept_ref[0] = running.astype(BF16)


def key_side(core, key_rows, value_rows, frequencies):
    rows = key_rows.shape[0]
    heads, width, count = frequencies.shape
    prior = max(1, rows // min(SPAN, rows) - 1)
    half = heads // 2

    def head(g, c):
        return (g + half * (1 - c[0])) % heads

    return pl.pallas_call(
        key_kernel,
        grid_spec=pltpu.PrefetchScalarGridSpec(
            num_scalar_prefetch=1,
            grid=(heads,),
            in_specs=[
                pl.BlockSpec((rows, width), lambda g, c: (0, head(g, c))),
                pl.BlockSpec((rows, width), lambda g, c: (0, head(g, c))),
                pl.BlockSpec((1, width, count), lambda g, c: (head(g, c), 0, 0)),
            ],
            out_specs=[
                pl.BlockSpec((1, 2 * count, rows), lambda g, c: (head(g, c), 0, 0)),
                pl.BlockSpec((1, 2 * count, width), lambda g, c: (jnp.minimum(g, half - 1), 0, 0)),
                pl.BlockSpec((1, 2 * count, width), lambda g, c: (jnp.maximum(g - half, 0), 0, 0)),
                pl.BlockSpec((1, prior, 2 * count, width), lambda g, c: (head(g, c), 0, 0, 0)),
            ],
        ),
        out_shape=[
            jax.ShapeDtypeStruct((heads, 2 * count, rows), BF16),
            jax.ShapeDtypeStruct((half, 2 * count, width), BF16),
            jax.ShapeDtypeStruct((half, 2 * count, width), BF16),
            jax.ShapeDtypeStruct((heads, prior, 2 * count, width), F32),
        ],
        compiler_params=LARGE,
        cost_estimate=FREE,
        name="key_side",
    )(core, key_rows, value_rows, frequencies)


def query_kernel(query_ref, value_ref, freq_ref, key_feat_ref, feat_ref, local_ref):
    rows, _ = query_ref.shape
    count = freq_ref.shape[2]
    span = min(SPAN, rows)
    amplitude = 1.0 / math.sqrt(count)
    for start in range(0, rows, TILE):
        mine = slice(start, start + TILE)
        phase = dot(query_ref[mine, :], freq_ref[0], (1, 0))
        cosine, sine = cos_sin(phase, amplitude)
        feat_ref[0, mine, :count] = cosine.astype(BF16)
        feat_ref[0, mine, count:] = sine.astype(BF16)
    below = lax.broadcasted_iota(jnp.int32, (TILE, TILE), 0)
    causal = below >= lax.broadcasted_iota(jnp.int32, (TILE, TILE), 1)
    for start in range(0, rows, TILE):
        mine = slice(start, start + TILE)
        total = None
        for other in range(start // span * span, start + TILE, TILE):
            theirs = slice(other, other + TILE)
            scores = dot(feat_ref[0, mine, :], key_feat_ref[0, :, theirs], (1, 0))
            if other == start:
                scores = jnp.where(causal, scores, F32(0.0))
            part = dot(scores.astype(BF16), value_ref[theirs, :], (1, 0))
            total = part if total is None else total + part
        local_ref[mine, :] = total


def query_side(query_rows, value_rows, frequencies, key_feat):
    rows = query_rows.shape[0]
    heads, width, count = frequencies.shape
    return pl.pallas_call(
        query_kernel,
        grid=(heads,),
        in_specs=[
            pl.BlockSpec((rows, width), lambda h: (0, h)),
            pl.BlockSpec((rows, width), lambda h: (0, h)),
            pl.BlockSpec((1, width, count), lambda h: (h, 0, 0)),
            pl.BlockSpec((1, 2 * count, rows), lambda h: (h, 0, 0)),
        ],
        out_specs=[
            pl.BlockSpec((1, rows, 2 * count), lambda h: (h, 0, 0)),
            pl.BlockSpec((rows, width), lambda h: (0, h)),
        ],
        out_shape=[
            jax.ShapeDtypeStruct((heads, rows, 2 * count), BF16),
            jax.ShapeDtypeStruct((rows, heads * width), F32),
        ],
        compiler_params=LARGE,
        cost_estimate=FREE,
        name="query_side",
    )(query_rows, value_rows, frequencies, key_feat)


def finish_kernel(
    heads, span, cuts, core_ref, feat_ref, local_ref, theirs_ref, mine_ref, prefix_ref, gain_ref, *out_refs
):
    width = local_ref.shape[1] // heads
    kept = pl.program_id(0) >= pl.num_programs(0) // 2
    for head in range(heads):
        cols = slice(head * width, (head + 1) * width)
        gain = gain_ref[:, cols].astype(F32)
        before = jnp.where(kept, mine_ref[head].astype(F32), theirs_ref[head].astype(F32))
        for out_ref, (first, last) in zip(out_refs, cuts):
            starts = [first, *range(first - first % TILE + TILE, last, TILE)]
            for start, stop in zip(starts, starts[1:] + [last]):
                mine = slice(start, stop)
                carried = before
                if start // span:
                    carried = carried + prefix_ref[head, start // span - 1]
                prior = dot(feat_ref[head, mine, :], carried.astype(BF16), (1, 0))
                attended = local_ref[mine, cols] + prior
                square = jnp.mean(attended * attended, axis=-1, keepdims=True)
                normed = attended * lax.rsqrt(square + F32(1e-6)) * gain
                out_ref[start - first : stop - first, cols] = normed.astype(BF16)


def finish(core, feat, local_part, theirs, mine, prefix, gain, cuts):
    heads, rows, feats = feat.shape
    width = local_part.shape[1] // heads
    prior = prefix.shape[1]
    half = heads // 2
    group = 2 if half % 2 == 0 else 1
    steps, half_steps = heads // group, half // group

    def block(g, c):
        return (g + half_steps * (1 - c[0])) % steps

    return pl.pallas_call(
        functools.partial(finish_kernel, group, min(SPAN, rows), cuts),
        grid_spec=pltpu.PrefetchScalarGridSpec(
            num_scalar_prefetch=1,
            grid=(steps,),
            in_specs=[
                pl.BlockSpec((group, rows, feats), lambda g, c: (block(g, c), 0, 0)),
                pl.BlockSpec((rows, group * width), lambda g, c: (0, block(g, c))),
                pl.BlockSpec((group, feats, width), lambda g, c: (jnp.minimum(g, half_steps - 1), 0, 0)),
                pl.BlockSpec((group, feats, width), lambda g, c: (jnp.maximum(g - half_steps, 0), 0, 0)),
                pl.BlockSpec((group, prior, feats, width), lambda g, c: (block(g, c), 0, 0, 0)),
                pl.BlockSpec((1, group * width), lambda g, c: (0, block(g, c))),
            ],
            out_specs=[
                pl.BlockSpec((last - first, group * width), lambda g, c: (0, block(g, c))) for first, last in cuts
            ],
        ),
        out_shape=[jax.ShapeDtypeStruct((last - first, heads * width), BF16) for first, last in cuts],
        compiler_params=LARGE,
        cost_estimate=FREE,
        name="finish",
    )(core, feat, local_part, theirs, mine, prefix, gain)


def project_kernel(sources, place_ref, *refs):
    out_ref = refs[-1]
    total = None
    for x_ref, w_ref in zip(refs[:sources], refs[sources : 2 * sources]):
        part = dot(x_ref[...], w_ref[...], (1, 0))
        total = part if total is None else total + part
    out_ref[...] = total.astype(out_ref.dtype)


def project(blocks, weight, place, hops, dtype=BF16):
    size, depth = blocks[0].shape
    cols = weight.shape[1]
    step = min(256, cols)

    def rows_of(source):
        return lambda n, p: (p[0] ^ hops[source], n)

    sources = len(blocks)
    return pl.pallas_call(
        functools.partial(project_kernel, sources),
        grid_spec=pltpu.PrefetchScalarGridSpec(
            num_scalar_prefetch=1,
            grid=(cols // step,),
            in_specs=[pl.BlockSpec((size, depth), lambda n, p: (0, 0)) for _ in blocks]
            + [pl.BlockSpec((depth, step), rows_of(source)) for source in range(sources)],
            out_specs=pl.BlockSpec((size, step), lambda n, p: (0, n)),
        ),
        out_shape=jax.ShapeDtypeStruct((size, cols), dtype),
        compiler_params=SMALL,
        cost_estimate=FREE,
        name="project",
    )(place, *blocks, *[weight] * sources)


def partial_kernel(core_ref, x_ref, y_ref, mine_ref, theirs_ref, out_ref):
    first = core_ref[0] == 0
    x, y = x_ref[...], y_ref[...]
    total = dot(jnp.where(first, x, y), mine_ref[...], (1, 0))
    out_ref[...] = (total + dot(jnp.where(first, y, x), theirs_ref[...], (1, 0))).astype(out_ref.dtype)


def partial_product(core, blocks, weights):
    size, depth = blocks[0].shape
    cols = weights[0].shape[1]
    step = min(256, cols)
    return pl.pallas_call(
        partial_kernel,
        grid_spec=pltpu.PrefetchScalarGridSpec(
            num_scalar_prefetch=1,
            grid=(cols // step,),
            in_specs=[pl.BlockSpec((size, depth), lambda n, c: (0, 0)) for _ in blocks]
            + [pl.BlockSpec((depth, step), lambda n, c: (0, n)) for _ in weights],
            out_specs=pl.BlockSpec((size, step), lambda n, c: (0, n)),
        ),
        out_shape=jax.ShapeDtypeStruct((size, cols), BF16),
        compiler_params=SMALL,
        cost_estimate=FREE,
        name="partial_product",
    )(core, *blocks, *weights)


def join_kernel(a_ref, b_ref, *refs):
    out_ref = refs[-1]
    out_ref[...] = (a_ref[...] + b_ref[...].astype(F32)).astype(out_ref.dtype)


def join(a, b, first, rows, into=None):
    size, cols = a.shape
    step = min(128, size)
    index = first // step
    spec = pl.BlockSpec((step, cols), lambda r: (r, 0))
    return pl.pallas_call(
        join_kernel,
        grid=(size // step,),
        in_specs=[spec, spec] + [pl.BlockSpec(memory_space=pl.ANY)] * (into is not None),
        out_specs=pl.BlockSpec((step, cols), lambda r: (index + r, 0)),
        out_shape=jax.ShapeDtypeStruct((rows, cols), BF16),
        input_output_aliases={} if into is None else {2: 0},
        compiler_params=SMALL,
        cost_estimate=FREE,
        name="join",
    )(a, b, *([] if into is None else [into]))


def after(value, *others):
    return lax.optimization_barrier((value, *others))[0]


def swap(value, axis, distance):
    return lax.ppermute(value, axis, [(i, i ^ distance) for i in range(lax.axis_size(axis))])


def earlier_states(sent, kept, meanwhile):
    count, mine = lax.axis_size("ctx"), lax.axis_index("ctx")
    core = mine % 2
    partner = swap(sent, "ctx", 1)
    total = (kept.astype(F32) + partner.astype(F32)).astype(BF16)
    earlier = jnp.zeros(kept.shape, F32)
    beside = meanwhile(total)
    distance = 2
    while distance < count:
        radix = min(4, count // distance)
        last = distance * radix >= count
        added = total.astype(F32)
        for step in range(1, radix):
            hop = step * distance
            pairs = [(i, i ^ hop) for i in range(count) if not last or i < i ^ hop]
            theirs = lax.ppermute(total, "ctx", pairs)
            if last:
                theirs = after(theirs, *beside)
            theirs = theirs.astype(F32)
            lower = (mine ^ hop) < mine
            earlier = earlier + jnp.where(lower, theirs, F32(0.0))
            added = added + theirs
        total = added.astype(BF16)
        distance *= radix
    own = earlier + jnp.where(core == 1, partner.astype(F32), F32(0.0))
    given = earlier + jnp.where(core == 0, kept.astype(F32), F32(0.0))
    return swap(given.astype(BF16), "ctx", 1), own.astype(BF16), beside


def weight_share(out_weight):
    place, core = lax.axis_index("head"), lax.axis_index("ctx") % 2
    depth = out_weight.shape[0] // 4
    block = jnp.where(core == 0, place ^ 1, place ^ 3)
    return swap(lax.dynamic_slice_in_dim(out_weight, block * depth, depth, axis=0), "head", 1)


def normed_output(core, query_rows, key_rows, value_rows, frequencies, norm_gain, cuts):
    key_feat, sent, kept, prefix = key_side(core, key_rows, value_rows, frequencies)

    def meanwhile(total):
        return query_side(query_rows, value_rows, after(frequencies, total), key_feat)

    theirs, own, (query_feat, local_part) = earlier_states(sent, kept, meanwhile)
    return finish(core, query_feat, local_part, theirs, own, prefix, norm_gain.reshape(1, -1), cuts)


def core_index():
    return (lax.axis_index("ctx") % 2).astype(jnp.int32).reshape(1)


def line_of_four(query_rows, key_rows, value_rows, frequencies, norm_gain, out_weight):
    rows = query_rows.shape[0]
    place = lax.axis_index("head").astype(jnp.int32).reshape(1)
    core = core_index()
    sizes = [rows * eighths // 8 for eighths in (1, 2, 2, 2, 1)]
    edges = [sum(sizes[:i]) for i in range(len(sizes) + 1)]
    cuts = tuple(zip(edges[:-1], edges[1:]))
    share = weight_share(out_weight)
    blocks = normed_output(core, query_rows, key_rows, value_rows, frequencies, norm_gain, cuts)
    pairs = []
    for index, block in enumerate(blocks):
        if index > 1:
            block = after(block, pairs[index - 2][1])
        pairs.append([block, swap(block, "head", 2)])
    share = after(share, pairs[0][1])
    weights = [share, swap(share, "ctx", 1)]
    products = [project(pair, out_weight, place, (0, 2), F32) for pair in pairs]
    partials, given = [], []
    for index, (x, y) in enumerate(pairs):
        if index:
            y = after(y, given[-1])
        if index > 2:
            y = after(y, partials[index - 3])
        if index == len(pairs) - 1:
            y = after(y, *products[:-1])
        given.append(partial_product(core, [x, y], weights))
        partials.append(swap(given[-1], "head", 1))
    out = None
    for product, partial, (first, _) in zip(products, partials, cuts):
        out = join(product, partial, first, rows, out)
    return out


def any_line(query_rows, key_rows, value_rows, frequencies, norm_gain, out_weight):
    cuts = ((0, query_rows.shape[0]),)
    parts = (query_rows, key_rows, value_rows, frequencies, norm_gain)
    (normed,) = normed_output(core_index(), *parts, cuts)
    gathered = lax.all_gather(normed, "head", axis=1, tiled=True)
    return jnp.dot(gathered, out_weight, preferred_element_type=F32).astype(BF16)


def solution(mesh):
    return jax.shard_map(
        line_of_four if mesh.shape["head"] == 4 else any_line,
        mesh=mesh,
        in_specs=(
            P("ctx", "head"),
            P("ctx", "head"),
            P("ctx", "head"),
            P("head", None, None),
            P("head"),
            P(None, "head"),
        ),
        out_specs=P("ctx", "head"),
        check_vma=False,
    )
```

```python
import functools
import math

import jax
import jax.numpy as jnp
from jax import lax
from jax.experimental import pallas as pl
from jax.experimental.pallas import tpu as pltpu
from jax.sharding import PartitionSpec as P

F32 = jnp.float32
BF16 = jnp.bfloat16
SPAN = 512
TILE = 256
SIN_TERMS = (3.1415820220956054, -5.167142794166117, 2.5418990064386224, -0.5546361406826548)
COS_TERMS = (0.9999932955183647, -4.933938020185013, 4.0412838463445455, -1.2221270624224843)
ROUNDER = 1.5 * 2.0**23
LARGE = pltpu.CompilerParams(vmem_limit_bytes=56 << 20)
SMALL = pltpu.CompilerParams(vmem_limit_bytes=20 << 20)
FREE = pl.CostEstimate(flops=0, bytes_accessed=0, transcendentals=0)


def dot(a, b, contract):
    return lax.dot_general(a, b, ((contract[:1], contract[1:]), ((), ())), preferred_element_type=F32)


def poly(terms, scale, u):
    value = F32(terms[-1] * scale)
    for term in terms[-2::-1]:
        value = value * u + F32(term * scale)
    return value


def cos_sin(phase, amplitude):
    turns = phase * F32(1.0 / (2.0 * math.pi))
    part = turns - ((turns + F32(ROUNDER)) - F32(ROUNDER))
    u = part * part
    scale = math.sqrt(2.0 * amplitude)
    half_sin = poly(SIN_TERMS, scale, u) * part
    half_cos = poly(COS_TERMS, scale, u)
    return F32(amplitude) - half_sin * half_sin, half_sin * half_cos


def key_kernel(has_weight, core_ref, place_ref, key_ref, value_ref, freq_ref, *refs):
    if has_weight:
        refs[-1][...] = refs[0][...]
        refs = refs[1:]
    feat_ref, sent_ref, kept_ref, prefix_ref = refs[:4]
    rows = key_ref.shape[0]
    group, width, count = freq_ref.shape
    span = min(SPAN, rows)
    amplitude = 1.0 / math.sqrt(count)
    sums = []
    for head in range(group):
        lanes = slice(head * width, (head + 1) * width)
        for start in range(0, rows, TILE):
            cols = slice(start, start + TILE)
            phase = dot(freq_ref[head], key_ref[cols, lanes], (0, 1))
            cosine, sine = cos_sin(phase, amplitude)
            feat_ref[head, :count, cols] = cosine.astype(BF16)
            feat_ref[head, count:, cols] = sine.astype(BF16)
        running = None
        for index in range(rows // span):
            cols = slice(index * span, (index + 1) * span)
            state = dot(feat_ref[head, :, cols], value_ref[cols, lanes], (1, 0))
            running = state if running is None else running + state
            if index < prefix_ref.shape[1]:
                prefix_ref[head, index] = running
        sums.append(running.astype(BF16))
    half = pl.num_programs(0) // 2

    @pl.when(pl.program_id(0) < half)
    def _():
        for head in range(group):
            sent_ref[head] = sums[head]

    @pl.when(pl.program_id(0) >= half)
    def _():
        for head in range(group):
            kept_ref[head] = sums[head]


def key_side(core, place, key_rows, value_rows, frequencies, weight=None):
    rows = key_rows.shape[0]
    heads, width, count = frequencies.shape
    prior = max(1, rows // min(SPAN, rows) - 1)
    half = heads // 2
    group = 2 if half % 2 == 0 else 1
    steps, half_steps = heads // group, half // group

    def block(g, c):
        return (g + half_steps * (1 - c[0])) % steps

    in_specs = [
        pl.BlockSpec((rows, group * width), lambda g, c, p: (0, block(g, c))),
        pl.BlockSpec((rows, group * width), lambda g, c, p: (0, block(g, c))),
        pl.BlockSpec((group, width, count), lambda g, c, p: (block(g, c), 0, 0)),
    ]
    out_specs = [
        pl.BlockSpec((group, 2 * count, rows), lambda g, c, p: (block(g, c), 0, 0)),
        pl.BlockSpec((group, 2 * count, width), lambda g, c, p: (jnp.minimum(g, half_steps - 1), 0, 0)),
        pl.BlockSpec((group, 2 * count, width), lambda g, c, p: (jnp.maximum(g - half_steps, 0), 0, 0)),
        pl.BlockSpec((group, prior, 2 * count, width), lambda g, c, p: (block(g, c), 0, 0, 0)),
    ]
    out_shape = [
        jax.ShapeDtypeStruct((heads, 2 * count, rows), BF16),
        jax.ShapeDtypeStruct((half, 2 * count, width), BF16),
        jax.ShapeDtypeStruct((half, 2 * count, width), BF16),
        jax.ShapeDtypeStruct((heads, prior, 2 * count, width), F32),
    ]
    operands = [key_rows, value_rows, frequencies]
    if weight is not None:
        depth, cols = weight.shape[0] // 4, weight.shape[1]
        piece = depth // steps
        in_specs.append(pl.BlockSpec((piece, cols), lambda g, c, p: ((p[0] ^ (1 + 2 * c[0])) * steps + g, 0)))
        out_specs.append(pl.BlockSpec((piece, cols), lambda g, c, p: (g, 0)))
        out_shape.append(jax.ShapeDtypeStruct((depth, cols), weight.dtype))
        operands.append(weight)
    return pl.pallas_call(
        functools.partial(key_kernel, weight is not None),
        grid_spec=pltpu.PrefetchScalarGridSpec(
            num_scalar_prefetch=2, grid=(steps,), in_specs=in_specs, out_specs=out_specs
        ),
        out_shape=out_shape,
        compiler_params=LARGE,
        cost_estimate=FREE,
        name="key_side",
    )(core, place, *operands)


def query_kernel(query_ref, value_ref, freq_ref, key_feat_ref, feat_ref, local_ref):
    rows = query_ref.shape[0]
    group, width, count = freq_ref.shape
    span = min(SPAN, rows)
    amplitude = 1.0 / math.sqrt(count)
    below = lax.broadcasted_iota(jnp.int32, (TILE, TILE), 0)
    causal = below >= lax.broadcasted_iota(jnp.int32, (TILE, TILE), 1)
    for head in range(group):
        lanes = slice(head * width, (head + 1) * width)
        for start in range(0, rows, TILE):
            mine = slice(start, start + TILE)
            phase = dot(query_ref[mine, lanes], freq_ref[head], (1, 0))
            cosine, sine = cos_sin(phase, amplitude)
            feat_ref[head, mine, :count] = cosine.astype(BF16)
            feat_ref[head, mine, count:] = sine.astype(BF16)
        for start in range(0, rows, TILE):
            mine = slice(start, start + TILE)
            total = None
            for other in range(start // span * span, start + TILE, TILE):
                theirs = slice(other, other + TILE)
                scores = dot(feat_ref[head, mine, :], key_feat_ref[head, :, theirs], (1, 0))
                if other == start:
                    scores = jnp.where(causal, scores, F32(0.0))
                part = dot(scores.astype(BF16), value_ref[theirs, lanes], (1, 0))
                total = part if total is None else total + part
            local_ref[mine, lanes] = total.astype(local_ref.dtype)


def query_side(query_rows, value_rows, frequencies, key_feat):
    rows = query_rows.shape[0]
    heads, width, count = frequencies.shape
    group = 2 if heads % 2 == 0 else 1
    return pl.pallas_call(
        query_kernel,
        grid=(heads // group,),
        in_specs=[
            pl.BlockSpec((rows, group * width), lambda h: (0, h)),
            pl.BlockSpec((rows, group * width), lambda h: (0, h)),
            pl.BlockSpec((group, width, count), lambda h: (h, 0, 0)),
            pl.BlockSpec((group, 2 * count, rows), lambda h: (h, 0, 0)),
        ],
        out_specs=[
            pl.BlockSpec((group, rows, 2 * count), lambda h: (h, 0, 0)),
            pl.BlockSpec((rows, group * width), lambda h: (0, h)),
        ],
        out_shape=[
            jax.ShapeDtypeStruct((heads, rows, 2 * count), BF16),
            jax.ShapeDtypeStruct((rows, heads * width), BF16),
        ],
        compiler_params=LARGE,
        cost_estimate=FREE,
        name="query_side",
    )(query_rows, value_rows, frequencies, key_feat)


def finish_kernel(
    heads, span, cuts, core_ref, feat_ref, local_ref, theirs_ref, mine_ref, prefix_ref, gain_ref, *out_refs
):
    width = local_ref.shape[1] // heads
    kept = pl.program_id(0) >= pl.num_programs(0) // 2
    for head in range(heads):
        cols = slice(head * width, (head + 1) * width)
        gain = gain_ref[:, cols].astype(F32)
        before = jnp.where(kept, mine_ref[head].astype(F32), theirs_ref[head].astype(F32))
        for out_ref, (first, last) in zip(out_refs, cuts):
            starts = [first, *range(first - first % TILE + TILE, last, TILE)]
            for start, stop in zip(starts, starts[1:] + [last]):
                mine = slice(start, stop)
                carried = before
                if start // span:
                    carried = carried + prefix_ref[head, start // span - 1]
                prior = dot(feat_ref[head, mine, :], carried.astype(BF16), (1, 0))
                attended = local_ref[mine, cols].astype(F32) + prior
                square = jnp.mean(attended * attended, axis=-1, keepdims=True)
                normed = attended * lax.rsqrt(square + F32(1e-6)) * gain
                out_ref[start - first : stop - first, cols] = normed.astype(BF16)


def finish(core, feat, local_part, theirs, mine, prefix, gain, cuts):
    heads, all_rows, feats = feat.shape
    rows = cuts[-1][1]
    width = local_part.shape[1] // heads
    prior = prefix.shape[1]
    half = heads // 2
    group = 2 if half % 2 == 0 else 1
    steps, half_steps = heads // group, half // group

    def block(g, c):
        return (g + half_steps * (1 - c[0])) % steps

    return pl.pallas_call(
        functools.partial(finish_kernel, group, min(SPAN, all_rows), cuts),
        grid_spec=pltpu.PrefetchScalarGridSpec(
            num_scalar_prefetch=1,
            grid=(steps,),
            in_specs=[
                pl.BlockSpec((group, rows, feats), lambda g, c: (block(g, c), 0, 0)),
                pl.BlockSpec((rows, group * width), lambda g, c: (0, block(g, c))),
                pl.BlockSpec((group, feats, width), lambda g, c: (jnp.minimum(g, half_steps - 1), 0, 0)),
                pl.BlockSpec((group, feats, width), lambda g, c: (jnp.maximum(g - half_steps, 0), 0, 0)),
                pl.BlockSpec((group, prior, feats, width), lambda g, c: (block(g, c), 0, 0, 0)),
                pl.BlockSpec((1, group * width), lambda g, c: (0, block(g, c))),
            ],
            out_specs=[
                pl.BlockSpec((last - first, group * width), lambda g, c: (0, block(g, c))) for first, last in cuts
            ],
        ),
        out_shape=[jax.ShapeDtypeStruct((last - first, heads * width), BF16) for first, last in cuts],
        compiler_params=LARGE,
        cost_estimate=FREE,
        name="finish",
    )(core, feat, local_part, theirs, mine, prefix, gain)


def project_kernel(sources, place_ref, *refs):
    out_ref = refs[-1]
    total = None
    for x_ref, w_ref in zip(refs[:sources], refs[sources : 2 * sources]):
        part = dot(x_ref[...], w_ref[...], (1, 0))
        total = part if total is None else total + part
    out_ref[...] = total.astype(out_ref.dtype)


def project(blocks, weight, place, hops, dtype=BF16):
    size, depth = blocks[0].shape
    cols = weight.shape[1]
    step = min(256, cols)

    def rows_of(source):
        return lambda n, p: (p[0] ^ hops[source], n)

    sources = len(blocks)
    return pl.pallas_call(
        functools.partial(project_kernel, sources),
        grid_spec=pltpu.PrefetchScalarGridSpec(
            num_scalar_prefetch=1,
            grid=(cols // step,),
            in_specs=[pl.BlockSpec((size, depth), lambda n, p: (0, 0)) for _ in blocks]
            + [pl.BlockSpec((depth, step), rows_of(source)) for source in range(sources)],
            out_specs=pl.BlockSpec((size, step), lambda n, p: (0, n)),
        ),
        out_shape=jax.ShapeDtypeStruct((size, cols), dtype),
        compiler_params=SMALL,
        cost_estimate=FREE,
        name="project",
    )(place, *blocks, *[weight] * sources)


def partial_kernel(core_ref, x_ref, y_ref, mine_ref, theirs_ref, out_ref):
    first = core_ref[0] == 0
    x, y = x_ref[...], y_ref[...]
    total = dot(jnp.where(first, x, y), mine_ref[...], (1, 0))
    out_ref[...] = (total + dot(jnp.where(first, y, x), theirs_ref[...], (1, 0))).astype(out_ref.dtype)


def partial_product(core, blocks, weights):
    size, depth = blocks[0].shape
    cols = weights[0].shape[1]
    step = min(256, cols)
    return pl.pallas_call(
        partial_kernel,
        grid_spec=pltpu.PrefetchScalarGridSpec(
            num_scalar_prefetch=1,
            grid=(cols // step,),
            in_specs=[pl.BlockSpec((size, depth), lambda n, c: (0, 0)) for _ in blocks]
            + [pl.BlockSpec((depth, step), lambda n, c: (0, n)) for _ in weights],
            out_specs=pl.BlockSpec((size, step), lambda n, c: (0, n)),
        ),
        out_shape=jax.ShapeDtypeStruct((size, cols), BF16),
        compiler_params=SMALL,
        cost_estimate=FREE,
        name="partial_product",
    )(core, *blocks, *weights)


def join_kernel(a_ref, b_ref, *refs):
    out_ref = refs[-1]
    out_ref[...] = (a_ref[...] + b_ref[...].astype(F32)).astype(out_ref.dtype)


def join(a, b, first, rows, into=None):
    size, cols = a.shape
    step = min(128, size)
    index = first // step
    spec = pl.BlockSpec((step, cols), lambda r: (r, 0))
    return pl.pallas_call(
        join_kernel,
        grid=(size // step,),
        in_specs=[spec, spec] + [pl.BlockSpec(memory_space=pl.ANY)] * (into is not None),
        out_specs=pl.BlockSpec((step, cols), lambda r: (index + r, 0)),
        out_shape=jax.ShapeDtypeStruct((rows, cols), BF16),
        input_output_aliases={} if into is None else {2: 0},
        compiler_params=SMALL,
        cost_estimate=FREE,
        name="join",
    )(a, b, *([] if into is None else [into]))


def after(value, *others):
    return lax.optimization_barrier((value, *others))[0]


def swap(value, axis, distance):
    return lax.ppermute(value, axis, [(i, i ^ distance) for i in range(lax.axis_size(axis))])


def earlier_states(sent, kept, meanwhile):
    count, mine = lax.axis_size("ctx"), lax.axis_index("ctx")
    core = mine % 2
    partner = swap(sent, "ctx", 1)
    total = (kept.astype(F32) + partner.astype(F32)).astype(BF16)
    earlier = jnp.zeros(kept.shape, F32)
    beside = meanwhile(total)
    distance = 2
    while distance < count:
        radix = min(4, count // distance)
        last = distance * radix >= count
        added = total.astype(F32)
        for step in range(1, radix):
            hop = step * distance
            pairs = [(i, i ^ hop) for i in range(count) if not last or i < i ^ hop]
            theirs = lax.ppermute(total, "ctx", pairs)
            if last:
                theirs = after(theirs, *beside)
            theirs = theirs.astype(F32)
            lower = (mine ^ hop) < mine
            earlier = earlier + jnp.where(lower, theirs, F32(0.0))
            added = added + theirs
        total = added.astype(BF16)
        distance *= radix
    own = earlier + jnp.where(core == 1, partner.astype(F32), F32(0.0))
    given = earlier + jnp.where(core == 0, kept.astype(F32), F32(0.0))
    return swap(given.astype(BF16), "ctx", 1), own.astype(BF16), beside


def normed_output(core, place, query_rows, key_rows, value_rows, frequencies, norm_gain, cuts, weight=None):
    key_feat, sent, kept, prefix, *share = key_side(core, place, key_rows, value_rows, frequencies, weight)

    def meanwhile(total):
        return query_side(query_rows, value_rows, after(frequencies, total), key_feat)

    theirs, own, (query_feat, local_part) = earlier_states(sent, kept, meanwhile)
    parts = (core, query_feat, local_part, theirs, own, prefix, norm_gain.reshape(1, -1))
    blocks = finish(*parts, cuts[:1])
    if cuts[1:]:
        blocks = [*blocks, *finish(*parts, cuts[1:])]
    return blocks, share


def positions():
    core, place = lax.axis_index("ctx") % 2, lax.axis_index("head")
    return core.astype(jnp.int32).reshape(1), place.astype(jnp.int32).reshape(1)


def line_of_four(query_rows, key_rows, value_rows, frequencies, norm_gain, out_weight):
    rows = query_rows.shape[0]
    core, place = positions()
    sizes = [rows * eighths // 8 for eighths in (1, 2, 2, 2, 1)]
    edges = [sum(sizes[:i]) for i in range(len(sizes) + 1)]
    cuts = tuple(zip(edges[:-1], edges[1:]))
    parts = (query_rows, key_rows, value_rows, frequencies, norm_gain)
    blocks, (share,) = normed_output(core, place, *parts, cuts, out_weight)
    share = swap(share, "head", 1)
    last = len(blocks) - 1
    pairs, given, partials, products = [], [], [], []
    weights = None
    for index, block in enumerate(blocks):
        if index > 1:
            block = after(block, given[index - 2])
        pairs.append([block, swap(block, "head", 2)])
        if index == 0:
            share = after(share, pairs[0][1], blocks[1])
            weights = [share, swap(share, "ctx", 1)]
        x, y = pairs[-1]
        products.append(project([x, y], out_weight, place, (0, 2), F32))
        if index > 2:
            y = after(y, partials[index - 3])
        if index == last:
            y = after(y, *products[:-1])
        given.append(partial_product(core, [x, y], weights))
        partials.append(swap(given[-1], "head", 1))
    out = None
    for product, partial, (first, _) in zip(products, partials, cuts):
        out = join(product, partial, first, rows, out)
    return out


def any_line(query_rows, key_rows, value_rows, frequencies, norm_gain, out_weight):
    core, place = positions()
    parts = (query_rows, key_rows, value_rows, frequencies, norm_gain)
    (normed,), _ = normed_output(core, place, *parts, ((0, query_rows.shape[0]),))
    gathered = lax.all_gather(normed, "head", axis=1, tiled=True)
    return jnp.dot(gathered, out_weight, preferred_element_type=F32).astype(BF16)


def solution(mesh):
    return jax.shard_map(
        line_of_four if mesh.shape["head"] == 4 else any_line,
        mesh=mesh,
        in_specs=(
            P("ctx", "head"),
            P("ctx", "head"),
            P("ctx", "head"),
            P("head", None, None),
            P("head"),
            P(None, "head"),
        ),
        out_specs=P("ctx", "head"),
        check_vma=False,
    )
```

```python
import functools
import math

import jax
import jax.numpy as jnp
from jax import lax
from jax.experimental import pallas as pl
from jax.experimental.pallas import tpu as pltpu
from jax.sharding import PartitionSpec as P

F32 = jnp.float32
BF16 = jnp.bfloat16
SPAN = 512
TILE = 256
SIN_TERMS = (3.1415820220956054, -5.167142794166117, 2.5418990064386224, -0.5546361406826548)
COS_TERMS = (0.9999932955183647, -4.933938020185013, 4.0412838463445455, -1.2221270624224843)
ROUNDER = 1.5 * 2.0**23
LARGE = pltpu.CompilerParams(vmem_limit_bytes=56 << 20)
SMALL = pltpu.CompilerParams(vmem_limit_bytes=20 << 20)
FREE = pl.CostEstimate(flops=0, bytes_accessed=0, transcendentals=0)


def dot(a, b, contract):
    return lax.dot_general(a, b, ((contract[:1], contract[1:]), ((), ())), preferred_element_type=F32)


def poly(terms, scale, u):
    value = F32(terms[-1] * scale)
    for term in terms[-2::-1]:
        value = value * u + F32(term * scale)
    return value


def cos_sin(phase, amplitude):
    turns = phase * F32(1.0 / (2.0 * math.pi))
    part = turns - ((turns + F32(ROUNDER)) - F32(ROUNDER))
    u = part * part
    scale = math.sqrt(2.0 * amplitude)
    half_sin = poly(SIN_TERMS, scale, u) * part
    half_cos = poly(COS_TERMS, scale, u)
    return F32(amplitude) - half_sin * half_sin, half_sin * half_cos


def key_kernel(has_weight, core_ref, place_ref, key_ref, value_ref, freq_ref, *refs):
    if has_weight:
        refs[-1][...] = refs[0][...]
        refs = refs[1:]
    feat_ref, sent_ref, kept_ref, prefix_ref = refs[:4]
    rows = key_ref.shape[0]
    group, width, count = freq_ref.shape
    span = min(SPAN, rows)
    amplitude = 1.0 / math.sqrt(count)
    tiles = [(head, start) for head in range(group) for start in range(0, rows, TILE)]

    def phase_of(head, start):
        lanes = slice(head * width, (head + 1) * width)
        return dot(freq_ref[head], key_ref[start : start + TILE, lanes], (0, 1))

    def add_state(head, start, features):
        lanes = slice(head * width, (head + 1) * width)
        state = dot(features, value_ref[start : start + TILE, lanes], (1, 0))
        sums[head] = state if start == 0 else sums[head] + state
        index = (start + TILE) // span - 1
        if (start + TILE) % span == 0 and index < prefix_ref.shape[1]:
            prefix_ref[head, index] = sums[head]

    sums = [None] * group
    phase, waiting = phase_of(*tiles[0]), None
    for index, (head, start) in enumerate(tiles):
        following = phase_of(*tiles[index + 1]) if index + 1 < len(tiles) else None
        cosine, sine = cos_sin(phase, amplitude)
        features = jnp.concatenate([cosine.astype(BF16), sine.astype(BF16)], axis=0)
        feat_ref[head, :, start : start + TILE] = features
        if waiting is not None:
            add_state(*waiting)
        phase, waiting = following, (head, start, features)
    add_state(*waiting)
    sums = [total.astype(BF16) for total in sums]
    half = pl.num_programs(0) // 2

    @pl.when(pl.program_id(0) < half)
    def _():
        for head in range(group):
            sent_ref[head] = sums[head]

    @pl.when(pl.program_id(0) >= half)
    def _():
        for head in range(group):
            kept_ref[head] = sums[head]


def key_side(core, place, key_rows, value_rows, frequencies, weight=None):
    rows = key_rows.shape[0]
    heads, width, count = frequencies.shape
    prior = max(1, rows // min(SPAN, rows) - 1)
    half = heads // 2
    group = 2 if half % 2 == 0 else 1
    steps, half_steps = heads // group, half // group

    def block(g, c):
        return (g + half_steps * (1 - c[0])) % steps

    in_specs = [
        pl.BlockSpec((rows, group * width), lambda g, c, p: (0, block(g, c))),
        pl.BlockSpec((rows, group * width), lambda g, c, p: (0, block(g, c))),
        pl.BlockSpec((group, width, count), lambda g, c, p: (block(g, c), 0, 0)),
    ]
    out_specs = [
        pl.BlockSpec((group, 2 * count, rows), lambda g, c, p: (block(g, c), 0, 0)),
        pl.BlockSpec((group, 2 * count, width), lambda g, c, p: (jnp.minimum(g, half_steps - 1), 0, 0)),
        pl.BlockSpec((group, 2 * count, width), lambda g, c, p: (jnp.maximum(g - half_steps, 0), 0, 0)),
        pl.BlockSpec((group, prior, 2 * count, width), lambda g, c, p: (block(g, c), 0, 0, 0)),
    ]
    out_shape = [
        jax.ShapeDtypeStruct((heads, 2 * count, rows), BF16),
        jax.ShapeDtypeStruct((half, 2 * count, width), BF16),
        jax.ShapeDtypeStruct((half, 2 * count, width), BF16),
        jax.ShapeDtypeStruct((heads, prior, 2 * count, width), F32),
    ]
    operands = [key_rows, value_rows, frequencies]
    if weight is not None:
        depth, cols = weight.shape[0] // 4, weight.shape[1]
        piece = depth // steps
        in_specs.append(pl.BlockSpec((piece, cols), lambda g, c, p: ((p[0] ^ (1 + 2 * c[0])) * steps + g, 0)))
        out_specs.append(pl.BlockSpec((piece, cols), lambda g, c, p: (g, 0)))
        out_shape.append(jax.ShapeDtypeStruct((depth, cols), weight.dtype))
        operands.append(weight)
    return pl.pallas_call(
        functools.partial(key_kernel, weight is not None),
        grid_spec=pltpu.PrefetchScalarGridSpec(
            num_scalar_prefetch=2, grid=(steps,), in_specs=in_specs, out_specs=out_specs
        ),
        out_shape=out_shape,
        compiler_params=LARGE,
        cost_estimate=FREE,
        name="key_side",
    )(core, place, *operands)


def query_kernel(query_ref, value_ref, freq_ref, key_feat_ref, feat_ref, local_ref):
    rows = query_ref.shape[0]
    group, width, count = freq_ref.shape
    span = min(SPAN, rows)
    amplitude = 1.0 / math.sqrt(count)
    below = lax.broadcasted_iota(jnp.int32, (TILE, TILE), 0)
    causal = below >= lax.broadcasted_iota(jnp.int32, (TILE, TILE), 1)
    tiles = [(head, start) for head in range(group) for start in range(0, rows, TILE)]

    def phase_of(head, start):
        lanes = slice(head * width, (head + 1) * width)
        return dot(query_ref[start : start + TILE, lanes], freq_ref[head], (1, 0))

    def attend(head, start, features):
        lanes = slice(head * width, (head + 1) * width)
        total = None
        for other in range(start // span * span, start + TILE, TILE):
            theirs = slice(other, other + TILE)
            scores = dot(features, key_feat_ref[head, :, theirs], (1, 0))
            if other == start:
                scores = jnp.where(causal, scores, F32(0.0))
            part = dot(scores.astype(BF16), value_ref[theirs, lanes], (1, 0))
            total = part if total is None else total + part
        local_ref[start : start + TILE, lanes] = total.astype(local_ref.dtype)

    phase, waiting = phase_of(*tiles[0]), None
    for index, (head, start) in enumerate(tiles):
        following = phase_of(*tiles[index + 1]) if index + 1 < len(tiles) else None
        cosine, sine = cos_sin(phase, amplitude)
        features = jnp.concatenate([cosine.astype(BF16), sine.astype(BF16)], axis=1)
        feat_ref[head, start : start + TILE, :] = features
        if waiting is not None:
            attend(*waiting)
        phase, waiting = following, (head, start, features)
    attend(*waiting)


def query_side(query_rows, value_rows, frequencies, key_feat):
    rows = query_rows.shape[0]
    heads, width, count = frequencies.shape
    group = 2 if heads % 2 == 0 else 1
    return pl.pallas_call(
        query_kernel,
        grid=(heads // group,),
        in_specs=[
            pl.BlockSpec((rows, group * width), lambda h: (0, h)),
            pl.BlockSpec((rows, group * width), lambda h: (0, h)),
            pl.BlockSpec((group, width, count), lambda h: (h, 0, 0)),
            pl.BlockSpec((group, 2 * count, rows), lambda h: (h, 0, 0)),
        ],
        out_specs=[
            pl.BlockSpec((group, rows, 2 * count), lambda h: (h, 0, 0)),
            pl.BlockSpec((rows, group * width), lambda h: (0, h)),
        ],
        out_shape=[
            jax.ShapeDtypeStruct((heads, rows, 2 * count), BF16),
            jax.ShapeDtypeStruct((rows, heads * width), BF16),
        ],
        compiler_params=LARGE,
        cost_estimate=FREE,
        name="query_side",
    )(query_rows, value_rows, frequencies, key_feat)


def finish_kernel(
    heads, span, cuts, core_ref, feat_ref, local_ref, theirs_ref, mine_ref, gain_ref, *refs
):
    prefix_ref, out_refs = refs[0], refs[-len(cuts) :]
    width = local_ref.shape[1] // heads
    kept = pl.program_id(0) >= pl.num_programs(0) // 2
    for head in range(heads):
        cols = slice(head * width, (head + 1) * width)
        gain = gain_ref[:, cols].astype(F32)
        before = jnp.where(kept, mine_ref[head].astype(F32), theirs_ref[head].astype(F32))
        for out_ref, (first, last) in zip(out_refs, cuts):
            starts = [first, *range(first - first % TILE + TILE, last, TILE)]
            for start, stop in zip(starts, starts[1:] + [last]):
                mine = slice(start, stop)
                carried = before
                if start // span:
                    carried = carried + prefix_ref[head, start // span - 1]
                prior = dot(feat_ref[head, mine, :], carried.astype(BF16), (1, 0))
                attended = local_ref[mine, cols].astype(F32) + prior
                square = jnp.mean(attended * attended, axis=-1, keepdims=True)
                normed = attended * lax.rsqrt(square + F32(1e-6)) * gain
                out_ref[start - first : stop - first, cols] = normed.astype(BF16)


def finish(core, feat, local_part, theirs, mine, gain, prefix, cuts):
    heads, all_rows, feats = feat.shape
    rows = cuts[-1][1]
    span = min(SPAN, all_rows)
    width = local_part.shape[1] // heads
    prior = prefix.shape[1]
    half = heads // 2
    group = 4 if half % 4 == 0 and rows < span else 2 if half % 2 == 0 else 1
    steps, half_steps = heads // group, half // group

    def block(g, c):
        return (g + half_steps * (1 - c[0])) % steps

    in_specs = [
        pl.BlockSpec((group, rows, feats), lambda g, c: (block(g, c), 0, 0)),
        pl.BlockSpec((rows, group * width), lambda g, c: (0, block(g, c))),
        pl.BlockSpec((group, feats, width), lambda g, c: (jnp.minimum(g, half_steps - 1), 0, 0)),
        pl.BlockSpec((group, feats, width), lambda g, c: (jnp.maximum(g - half_steps, 0), 0, 0)),
        pl.BlockSpec((1, group * width), lambda g, c: (0, block(g, c))),
    ]
    operands = [feat, local_part, theirs, mine, gain]
    if rows > span:
        in_specs.append(pl.BlockSpec((group, prior, feats, width), lambda g, c: (block(g, c), 0, 0, 0)))
        operands.append(prefix)
    return pl.pallas_call(
        functools.partial(finish_kernel, group, span, cuts),
        grid_spec=pltpu.PrefetchScalarGridSpec(
            num_scalar_prefetch=1,
            grid=(steps,),
            in_specs=in_specs,
            out_specs=[
                pl.BlockSpec((last - first, group * width), lambda g, c: (0, block(g, c))) for first, last in cuts
            ],
        ),
        out_shape=[jax.ShapeDtypeStruct((last - first, heads * width), BF16) for first, last in cuts],
        compiler_params=LARGE,
        cost_estimate=FREE,
        name="finish",
    )(core, *operands)


def project_kernel(sources, place_ref, *refs):
    out_ref = refs[-1]
    total = None
    for x_ref, w_ref in zip(refs[:sources], refs[sources : 2 * sources]):
        part = dot(x_ref[...], w_ref[...], (1, 0))
        total = part if total is None else total + part
    out_ref[...] = total.astype(out_ref.dtype)


def project(blocks, weight, place, hops, dtype=BF16):
    size, depth = blocks[0].shape
    cols = weight.shape[1]
    step = min(256, cols)

    def rows_of(source):
        return lambda n, p: (p[0] ^ hops[source], n)

    sources = len(blocks)
    return pl.pallas_call(
        functools.partial(project_kernel, sources),
        grid_spec=pltpu.PrefetchScalarGridSpec(
            num_scalar_prefetch=1,
            grid=(cols // step,),
            in_specs=[pl.BlockSpec((size, depth), lambda n, p: (0, 0)) for _ in blocks]
            + [pl.BlockSpec((depth, step), rows_of(source)) for source in range(sources)],
            out_specs=pl.BlockSpec((size, step), lambda n, p: (0, n)),
        ),
        out_shape=jax.ShapeDtypeStruct((size, cols), dtype),
        compiler_params=SMALL,
        cost_estimate=FREE,
        name="project",
    )(place, *blocks, *[weight] * sources)


def partial_kernel(core_ref, x_ref, y_ref, mine_ref, theirs_ref, out_ref):
    first = core_ref[0] == 0
    x, y = x_ref[...], y_ref[...]
    total = dot(jnp.where(first, x, y), mine_ref[...], (1, 0))
    out_ref[...] = (total + dot(jnp.where(first, y, x), theirs_ref[...], (1, 0))).astype(out_ref.dtype)


def partial_product(core, blocks, weights):
    size, depth = blocks[0].shape
    cols = weights[0].shape[1]
    step = min(256, cols)
    return pl.pallas_call(
        partial_kernel,
        grid_spec=pltpu.PrefetchScalarGridSpec(
            num_scalar_prefetch=1,
            grid=(cols // step,),
            in_specs=[pl.BlockSpec((size, depth), lambda n, c: (0, 0)) for _ in blocks]
            + [pl.BlockSpec((depth, step), lambda n, c: (0, n)) for _ in weights],
            out_specs=pl.BlockSpec((size, step), lambda n, c: (0, n)),
        ),
        out_shape=jax.ShapeDtypeStruct((size, cols), BF16),
        compiler_params=SMALL,
        cost_estimate=FREE,
        name="partial_product",
    )(core, *blocks, *weights)


def join_kernel(a_ref, b_ref, *refs):
    out_ref = refs[-1]
    out_ref[...] = (a_ref[...] + b_ref[...].astype(F32)).astype(out_ref.dtype)


def join(a, b, first, rows, into=None):
    size, cols = a.shape
    step = min(128, size)
    index = first // step
    spec = pl.BlockSpec((step, cols), lambda r: (r, 0))
    return pl.pallas_call(
        join_kernel,
        grid=(size // step,),
        in_specs=[spec, spec] + [pl.BlockSpec(memory_space=pl.ANY)] * (into is not None),
        out_specs=pl.BlockSpec((step, cols), lambda r: (index + r, 0)),
        out_shape=jax.ShapeDtypeStruct((rows, cols), BF16),
        input_output_aliases={} if into is None else {2: 0},
        compiler_params=SMALL,
        cost_estimate=FREE,
        name="join",
    )(a, b, *([] if into is None else [into]))


def after(value, *others):
    return lax.optimization_barrier((value, *others))[0]


def swap(value, axis, distance):
    return lax.ppermute(value, axis, [(i, i ^ distance) for i in range(lax.axis_size(axis))])


def earlier_states(sent, kept, meanwhile):
    count, mine = lax.axis_size("ctx"), lax.axis_index("ctx")
    core = mine % 2
    partner = swap(sent, "ctx", 1)
    total = (kept.astype(F32) + partner.astype(F32)).astype(BF16)
    earlier = jnp.zeros(kept.shape, F32)
    beside = meanwhile(total)
    distance = 2
    while distance < count:
        radix = min(4, count // distance)
        last = distance * radix >= count
        added = total.astype(F32)
        for step in range(1, radix):
            hop = step * distance
            pairs = [(i, i ^ hop) for i in range(count) if not last or i < i ^ hop]
            theirs = lax.ppermute(total, "ctx", pairs)
            if last:
                theirs = after(theirs, *beside)
            theirs = theirs.astype(F32)
            lower = (mine ^ hop) < mine
            earlier = earlier + jnp.where(lower, theirs, F32(0.0))
            added = added + theirs
        total = added.astype(BF16)
        distance *= radix
    own = earlier + jnp.where(core == 1, partner.astype(F32), F32(0.0))
    given = earlier + jnp.where(core == 0, kept.astype(F32), F32(0.0))
    return swap(given.astype(BF16), "ctx", 1), own.astype(BF16), beside


def normed_output(core, place, query_rows, key_rows, value_rows, frequencies, norm_gain, cuts, weight=None):
    key_feat, sent, kept, prefix, *share = key_side(core, place, key_rows, value_rows, frequencies, weight)

    gain = norm_gain.reshape(1, -1)

    def meanwhile(total):
        return query_side(query_rows, value_rows, after(frequencies, total, gain), key_feat)

    theirs, own, (query_feat, local_part) = earlier_states(sent, kept, meanwhile)
    parts = (core, query_feat, local_part, theirs, own, gain, prefix)
    blocks = finish(*parts, cuts[:1])
    if cuts[1:]:
        blocks = [*blocks, *finish(*parts, cuts[1:])]
    return blocks, share


def positions():
    core, place = lax.axis_index("ctx") % 2, lax.axis_index("head")
    return core.astype(jnp.int32).reshape(1), place.astype(jnp.int32).reshape(1)


def line_of_four(query_rows, key_rows, value_rows, frequencies, norm_gain, out_weight):
    rows = query_rows.shape[0]
    core, place = positions()
    sizes = [rows * part // 16 for part in (2, 4, 4, 4, 2)]
    edges = [sum(sizes[:i]) for i in range(len(sizes) + 1)]
    cuts = tuple(zip(edges[:-1], edges[1:]))
    parts = (query_rows, key_rows, value_rows, frequencies, norm_gain)
    blocks, (share,) = normed_output(core, place, *parts, cuts, out_weight)
    share = swap(share, "head", 1)
    last = len(blocks) - 1
    pairs, given, partials, products = [], [], [], []
    weights = None
    for index, block in enumerate(blocks):
        if index > 1:
            block = after(block, partials[0] if index == 2 else given[index - 2])
        pairs.append([block, swap(block, "head", 2)])
        if index == 0:
            share = after(share, pairs[0][1], blocks[1])
            weights = [share, swap(share, "ctx", 1)]
        x, y = pairs[-1]
        products.append(project([x, y], out_weight, place, (0, 2), F32))
        if index:
            y = after(y, partials[max(0, index - 3)])
        if index == last:
            y = after(y, *products[:-1])
        given.append(partial_product(core, [x, y], weights))
        partials.append(swap(given[-1], "head", 1))
    out = None
    for product, partial, (first, _) in zip(products, partials, cuts):
        out = join(product, partial, first, rows, out)
    return out


def any_line(query_rows, key_rows, value_rows, frequencies, norm_gain, out_weight):
    core, place = positions()
    parts = (query_rows, key_rows, value_rows, frequencies, norm_gain)
    (normed,), _ = normed_output(core, place, *parts, ((0, query_rows.shape[0]),))
    gathered = lax.all_gather(normed, "head", axis=1, tiled=True)
    return jnp.dot(gathered, out_weight, preferred_element_type=F32).astype(BF16)


def solution(mesh):
    return jax.shard_map(
        line_of_four if mesh.shape["head"] == 4 else any_line,
        mesh=mesh,
        in_specs=(
            P("ctx", "head"),
            P("ctx", "head"),
            P("ctx", "head"),
            P("head", None, None),
            P("head"),
            P(None, "head"),
        ),
        out_specs=P("ctx", "head"),
        check_vma=False,
    )
```

```python
import functools
import math

import jax
import jax.numpy as jnp
from jax import lax
from jax.experimental import pallas as pl
from jax.experimental.pallas import tpu as pltpu
from jax.sharding import PartitionSpec as P

F32 = jnp.float32
BF16 = jnp.bfloat16
SPAN = 512
TILE = 256
SIN_TERMS = (3.1415820220956054, -5.167142794166117, 2.5418990064386224, -0.5546361406826548)
COS_TERMS = (0.9999932955183647, -4.933938020185013, 4.0412838463445455, -1.2221270624224843)
ROUNDER = 1.5 * 2.0**23
LARGE = pltpu.CompilerParams(vmem_limit_bytes=56 << 20)
SMALL = pltpu.CompilerParams(vmem_limit_bytes=20 << 20)
FREE = pl.CostEstimate(flops=0, bytes_accessed=0, transcendentals=0)


def dot(a, b, contract):
    return lax.dot_general(a, b, ((contract[:1], contract[1:]), ((), ())), preferred_element_type=F32)


def poly(terms, scale, u):
    value = F32(terms[-1] * scale)
    for term in terms[-2::-1]:
        value = value * u + F32(term * scale)
    return value


def cos_sin(phase, amplitude):
    turns = phase * F32(1.0 / (2.0 * math.pi))
    part = turns - ((turns + F32(ROUNDER)) - F32(ROUNDER))
    u = part * part
    scale = math.sqrt(2.0 * amplitude)
    half_sin = poly(SIN_TERMS, scale, u) * part
    half_cos = poly(COS_TERMS, scale, u)
    return F32(amplitude) - half_sin * half_sin, half_sin * half_cos


def key_kernel(has_weight, core_ref, place_ref, turn_ref, key_ref, value_ref, freq_ref, *refs):
    if has_weight:
        refs[-1][...] = refs[0][...]
        refs = refs[1:]
    feat_ref, sent_ref, kept_ref, prefix_ref = refs[:4]
    rows = key_ref.shape[0]
    group, width, count = freq_ref.shape
    span = min(SPAN, rows)
    amplitude = 1.0 / math.sqrt(count)
    tiles = [(head, start) for head in range(group) for start in range(0, rows, TILE)]

    def phase_of(head, start):
        lanes = slice(head * width, (head + 1) * width)
        return dot(freq_ref[head], key_ref[start : start + TILE, lanes], (0, 1))

    def add_state(head, start, features):
        lanes = slice(head * width, (head + 1) * width)
        state = dot(features, value_ref[start : start + TILE, lanes], (1, 0))
        sums[head] = state if start == 0 else sums[head] + state
        index = (start + TILE) // span - 1
        if (start + TILE) % span == 0 and index < prefix_ref.shape[1]:
            prefix_ref[head, index] = sums[head]

    sums = [None] * group
    phase, waiting = phase_of(*tiles[0]), None
    for index, (head, start) in enumerate(tiles):
        following = phase_of(*tiles[index + 1]) if index + 1 < len(tiles) else None
        cosine, sine = cos_sin(phase, amplitude)
        features = jnp.concatenate([cosine.astype(BF16), sine.astype(BF16)], axis=0)
        feat_ref[head, :, start : start + TILE] = features
        if waiting is not None:
            add_state(*waiting)
        phase, waiting = following, (head, start, features)
    add_state(*waiting)
    sums = [total.astype(BF16) for total in sums]
    half = pl.num_programs(0) // 2

    @pl.when(pl.program_id(0) < half)
    def _():
        for head in range(group):
            sent_ref[head] = sums[head]

    @pl.when(pl.program_id(0) >= half)
    def _():
        for head in range(group):
            kept_ref[head] = sums[head]


def key_side(core, place, turn, key_rows, value_rows, frequencies, weight=None):
    rows = key_rows.shape[0]
    heads, width, count = frequencies.shape
    prior = max(1, rows // min(SPAN, rows) - 1)
    half = heads // 2
    group = 2 if half % 2 == 0 else 1
    steps, half_steps = heads // group, half // group

    def block(g, c):
        return (g + half_steps * (1 - c[0])) % steps

    in_specs = [
        pl.BlockSpec((rows, group * width), lambda g, c, p, t: (0, block(g, c))),
        pl.BlockSpec((rows, group * width), lambda g, c, p, t: (0, block(g, c))),
        pl.BlockSpec((group, width, count), lambda g, c, p, t: (block(g, c), 0, 0)),
    ]
    out_specs = [
        pl.BlockSpec((group, 2 * count, rows), lambda g, c, p, t: (block(g, c), 0, 0)),
        pl.BlockSpec((group, 2 * count, width), lambda g, c, p, t: (jnp.minimum(g, half_steps - 1), 0, 0)),
        pl.BlockSpec((group, 2 * count, width), lambda g, c, p, t: (jnp.maximum(g - half_steps, 0), 0, 0)),
        pl.BlockSpec((group, prior, 2 * count, width), lambda g, c, p, t: (block(g, c), 0, 0, 0)),
    ]
    out_shape = [
        jax.ShapeDtypeStruct((heads, 2 * count, rows), BF16),
        jax.ShapeDtypeStruct((half, 2 * count, width), BF16),
        jax.ShapeDtypeStruct((half, 2 * count, width), BF16),
        jax.ShapeDtypeStruct((heads, prior, 2 * count, width), F32),
    ]
    operands = [key_rows, value_rows, frequencies]
    if weight is not None:
        depth, cols = weight.shape[0] // 4, weight.shape[1]
        piece = depth // 2 // steps

        def rows_of(g, c, p, t):
            return ((p[0] ^ (1 + 2 * c[0])) * 2 + t[0]) * steps + g, 0

        in_specs.append(pl.BlockSpec((piece, cols), rows_of))
        out_specs.append(pl.BlockSpec((piece, cols), lambda g, c, p, t: (g, 0)))
        out_shape.append(jax.ShapeDtypeStruct((depth // 2, cols), weight.dtype))
        operands.append(weight)
    return pl.pallas_call(
        functools.partial(key_kernel, weight is not None),
        grid_spec=pltpu.PrefetchScalarGridSpec(
            num_scalar_prefetch=3, grid=(steps,), in_specs=in_specs, out_specs=out_specs
        ),
        out_shape=out_shape,
        compiler_params=LARGE,
        cost_estimate=FREE,
        name="key_side",
    )(core, place, turn, *operands)


def query_kernel(query_ref, value_ref, freq_ref, key_feat_ref, feat_ref, local_ref):
    rows = query_ref.shape[0]
    group, width, count = freq_ref.shape
    span = min(SPAN, rows)
    amplitude = 1.0 / math.sqrt(count)
    below = lax.broadcasted_iota(jnp.int32, (TILE, TILE), 0)
    causal = below >= lax.broadcasted_iota(jnp.int32, (TILE, TILE), 1)
    tiles = [(head, start) for head in range(group) for start in range(0, rows, TILE)]

    def phase_of(head, start):
        lanes = slice(head * width, (head + 1) * width)
        return dot(query_ref[start : start + TILE, lanes], freq_ref[head], (1, 0))

    def attend(head, start, features):
        lanes = slice(head * width, (head + 1) * width)
        total = None
        for other in range(start // span * span, start + TILE, TILE):
            theirs = slice(other, other + TILE)
            scores = dot(features, key_feat_ref[head, :, theirs], (1, 0))
            if other == start:
                scores = jnp.where(causal, scores, F32(0.0))
            part = dot(scores.astype(BF16), value_ref[theirs, lanes], (1, 0))
            total = part if total is None else total + part
        local_ref[start : start + TILE, lanes] = total.astype(local_ref.dtype)

    phase, waiting = phase_of(*tiles[0]), None
    for index, (head, start) in enumerate(tiles):
        following = phase_of(*tiles[index + 1]) if index + 1 < len(tiles) else None
        cosine, sine = cos_sin(phase, amplitude)
        features = jnp.concatenate([cosine.astype(BF16), sine.astype(BF16)], axis=1)
        feat_ref[head, start : start + TILE, :] = features
        if waiting is not None:
            attend(*waiting)
        phase, waiting = following, (head, start, features)
    attend(*waiting)


def query_side(query_rows, value_rows, frequencies, key_feat):
    rows = query_rows.shape[0]
    heads, width, count = frequencies.shape
    group = 2 if heads % 2 == 0 else 1
    return pl.pallas_call(
        query_kernel,
        grid=(heads // group,),
        in_specs=[
            pl.BlockSpec((rows, group * width), lambda h: (0, h)),
            pl.BlockSpec((rows, group * width), lambda h: (0, h)),
            pl.BlockSpec((group, width, count), lambda h: (h, 0, 0)),
            pl.BlockSpec((group, 2 * count, rows), lambda h: (h, 0, 0)),
        ],
        out_specs=[
            pl.BlockSpec((group, rows, 2 * count), lambda h: (h, 0, 0)),
            pl.BlockSpec((rows, group * width), lambda h: (0, h)),
        ],
        out_shape=[
            jax.ShapeDtypeStruct((heads, rows, 2 * count), BF16),
            jax.ShapeDtypeStruct((rows, heads * width), BF16),
        ],
        compiler_params=LARGE,
        cost_estimate=FREE,
        name="query_side",
    )(query_rows, value_rows, frequencies, key_feat)


def finish_kernel(
    heads, span, cuts, core_ref, feat_ref, local_ref, theirs_ref, mine_ref, gain_ref, *refs
):
    prefix_ref, out_refs = refs[0], refs[-len(cuts) :]
    width = local_ref.shape[1] // heads
    kept = pl.program_id(0) >= pl.num_programs(0) // 2
    for head in range(heads):
        cols = slice(head * width, (head + 1) * width)
        gain = gain_ref[:, cols].astype(F32)
        before = jnp.where(kept, mine_ref[head].astype(F32), theirs_ref[head].astype(F32))
        for out_ref, (first, last) in zip(out_refs, cuts):
            starts = [first, *range(first - first % TILE + TILE, last, TILE)]
            for start, stop in zip(starts, starts[1:] + [last]):
                mine = slice(start, stop)
                carried = before
                if start // span:
                    carried = carried + prefix_ref[head, start // span - 1]
                prior = dot(feat_ref[head, mine, :], carried.astype(BF16), (1, 0))
                attended = local_ref[mine, cols].astype(F32) + prior
                square = jnp.mean(attended * attended, axis=-1, keepdims=True)
                normed = attended * lax.rsqrt(square + F32(1e-6)) * gain
                out_ref[start - first : stop - first, cols] = normed.astype(BF16)


def finish(core, feat, local_part, theirs, mine, gain, prefix, cuts):
    heads, all_rows, feats = feat.shape
    rows = cuts[-1][1]
    span = min(SPAN, all_rows)
    width = local_part.shape[1] // heads
    prior = prefix.shape[1]
    half = heads // 2
    group = 4 if half % 4 == 0 and rows < span else 2 if half % 2 == 0 else 1
    steps, half_steps = heads // group, half // group

    def block(g, c):
        return (g + half_steps * (1 - c[0])) % steps

    in_specs = [
        pl.BlockSpec((group, rows, feats), lambda g, c: (block(g, c), 0, 0)),
        pl.BlockSpec((rows, group * width), lambda g, c: (0, block(g, c))),
        pl.BlockSpec((group, feats, width), lambda g, c: (jnp.minimum(g, half_steps - 1), 0, 0)),
        pl.BlockSpec((group, feats, width), lambda g, c: (jnp.maximum(g - half_steps, 0), 0, 0)),
        pl.BlockSpec((1, group * width), lambda g, c: (0, block(g, c))),
    ]
    operands = [feat, local_part, theirs, mine, gain]
    if rows > span:
        in_specs.append(pl.BlockSpec((group, prior, feats, width), lambda g, c: (block(g, c), 0, 0, 0)))
        operands.append(prefix)
    return pl.pallas_call(
        functools.partial(finish_kernel, group, span, cuts),
        grid_spec=pltpu.PrefetchScalarGridSpec(
            num_scalar_prefetch=1,
            grid=(steps,),
            in_specs=in_specs,
            out_specs=[
                pl.BlockSpec((last - first, group * width), lambda g, c: (0, block(g, c))) for first, last in cuts
            ],
        ),
        out_shape=[jax.ShapeDtypeStruct((last - first, heads * width), BF16) for first, last in cuts],
        compiler_params=LARGE,
        cost_estimate=FREE,
        name="finish",
    )(core, *operands)


def project_kernel(sources, place_ref, *refs):
    out_ref = refs[-1]
    total = None
    for x_ref, w_ref in zip(refs[:sources], refs[sources : 2 * sources]):
        part = dot(x_ref[...], w_ref[...], (1, 0))
        total = part if total is None else total + part
    out_ref[...] = total.astype(out_ref.dtype)


def project(blocks, weight, place, hops, dtype=BF16):
    size, depth = blocks[0].shape
    cols = weight.shape[1]
    step = min(256, cols)

    def rows_of(source):
        return lambda n, p: (p[0] ^ hops[source], n)

    sources = len(blocks)
    return pl.pallas_call(
        functools.partial(project_kernel, sources),
        grid_spec=pltpu.PrefetchScalarGridSpec(
            num_scalar_prefetch=1,
            grid=(cols // step,),
            in_specs=[pl.BlockSpec((size, depth), lambda n, p: (0, 0)) for _ in blocks]
            + [pl.BlockSpec((depth, step), rows_of(source)) for source in range(sources)],
            out_specs=pl.BlockSpec((size, step), lambda n, p: (0, n)),
        ),
        out_shape=jax.ShapeDtypeStruct((size, cols), dtype),
        compiler_params=SMALL,
        cost_estimate=FREE,
        name="project",
    )(place, *blocks, *[weight] * sources)


def partial_kernel(core_ref, turn_ref, x_ref, y_ref, *refs):
    weights, out_ref = refs[:4], refs[4]
    swapped, turned = core_ref[0] != 0, turn_ref[0] != 0
    x, y = x_ref[...], y_ref[...]
    half = x.shape[1] // 2
    total = None
    for rows, pieces in ((jnp.where(swapped, y, x), weights[:2]), (jnp.where(swapped, x, y), weights[2:])):
        left, right = rows[:, :half], rows[:, half:]
        part = dot(jnp.where(turned, right, left), pieces[0][...], (1, 0))
        part = part + dot(jnp.where(turned, left, right), pieces[1][...], (1, 0))
        total = part if total is None else total + part
    out_ref[...] = total.astype(out_ref.dtype)


def partial_product(core, turn, blocks, weights):
    size, depth = blocks[0].shape
    cols = weights[0].shape[1]
    step = min(256, cols)
    return pl.pallas_call(
        partial_kernel,
        grid_spec=pltpu.PrefetchScalarGridSpec(
            num_scalar_prefetch=2,
            grid=(cols // step,),
            in_specs=[pl.BlockSpec((size, depth), lambda n, c, t: (0, 0)) for _ in blocks]
            + [pl.BlockSpec((depth // 2, step), lambda n, c, t: (0, n)) for _ in weights],
            out_specs=pl.BlockSpec((size, step), lambda n, c, t: (0, n)),
        ),
        out_shape=jax.ShapeDtypeStruct((size, cols), BF16),
        compiler_params=SMALL,
        cost_estimate=FREE,
        name="partial_product",
    )(core, turn, *blocks, *weights)


def join_kernel(a_ref, b_ref, *refs):
    out_ref = refs[-1]
    out_ref[...] = (a_ref[...] + b_ref[...].astype(F32)).astype(out_ref.dtype)


def join(a, b, first, rows, into=None):
    size, cols = a.shape
    step = math.gcd(first, size, 256)
    index = first // step
    spec = pl.BlockSpec((step, cols), lambda r: (r, 0))
    return pl.pallas_call(
        join_kernel,
        grid=(size // step,),
        in_specs=[spec, spec] + [pl.BlockSpec(memory_space=pl.ANY)] * (into is not None),
        out_specs=pl.BlockSpec((step, cols), lambda r: (index + r, 0)),
        out_shape=jax.ShapeDtypeStruct((rows, cols), BF16),
        input_output_aliases={} if into is None else {2: 0},
        compiler_params=SMALL,
        cost_estimate=FREE,
        name="join",
    )(a, b, *([] if into is None else [into]))


def after(value, *others):
    return lax.optimization_barrier((value, *others))[0]


def swap(value, axis, distance):
    return lax.ppermute(value, axis, [(i, i ^ distance) for i in range(lax.axis_size(axis))])


def earlier_states(sent, kept, meanwhile):
    count, mine = lax.axis_size("ctx"), lax.axis_index("ctx")
    core = mine % 2
    partner = swap(sent, "ctx", 1)
    total = (kept.astype(F32) + partner.astype(F32)).astype(BF16)
    earlier = jnp.zeros(kept.shape, F32)
    beside = meanwhile(total)
    distance = 2
    while distance < count:
        radix = min(4, count // distance)
        last = distance * radix >= count
        added = total.astype(F32)
        for step in range(1, radix):
            hop = step * distance
            pairs = [(i, i ^ hop) for i in range(count) if not last or i < i ^ hop]
            theirs = lax.ppermute(total, "ctx", pairs)
            if last:
                theirs = after(theirs, *beside)
            theirs = theirs.astype(F32)
            lower = (mine ^ hop) < mine
            earlier = earlier + jnp.where(lower, theirs, F32(0.0))
            added = added + theirs
        total = added.astype(BF16)
        distance *= radix
    own = earlier + jnp.where(core == 1, partner.astype(F32), F32(0.0))
    given = earlier + jnp.where(core == 0, kept.astype(F32), F32(0.0))
    return swap(given.astype(BF16), "ctx", 1), own.astype(BF16), beside


def normed_output(core, place, turn, query_rows, key_rows, value_rows, frequencies, norm_gain, cuts, weight=None):
    key_feat, sent, kept, prefix, *share = key_side(core, place, turn, key_rows, value_rows, frequencies, weight)

    gain = norm_gain.reshape(1, -1)

    def meanwhile(total):
        return query_side(query_rows, value_rows, after(frequencies, total, gain), key_feat)

    theirs, own, (query_feat, local_part) = earlier_states(sent, kept, meanwhile)
    parts = (core, query_feat, local_part, theirs, own, gain, prefix)
    blocks = finish(*parts, cuts[:1])
    if cuts[1:]:
        blocks = [*blocks, *finish(*parts, cuts[1:])]
    return blocks, share


def positions():
    spot, place = lax.axis_index("ctx"), lax.axis_index("head")
    return [value.astype(jnp.int32).reshape(1) for value in (spot % 2, place, spot // 2 % 2)]


def line_of_four(query_rows, key_rows, value_rows, frequencies, norm_gain, out_weight):
    rows = query_rows.shape[0]
    core, place, turn = positions()
    sizes = [rows * part // 16 for part in (2, 2, 5, 3, 2, 2)]
    edges = [sum(sizes[:i]) for i in range(len(sizes) + 1)]
    cuts = tuple(zip(edges[:-1], edges[1:]))
    parts = (query_rows, key_rows, value_rows, frequencies, norm_gain)
    blocks, (share,) = normed_output(core, place, turn, *parts, cuts, out_weight)
    share = swap(share, "head", 1)
    last = len(blocks) - 1
    pairs, given, partials, products = [], [], [], []
    weights = None
    for index, block in enumerate(blocks):
        if index > 2:
            block = after(block, partials[0] if index == 3 else given[index - 2])
        pairs.append([block, swap(block, "head", 2)])
        if index == 1:
            other = swap(after(share, blocks[0]), "ctx", 2)
            shares = [after(share, blocks[-1], pairs[0][1]), after(other, pairs[1][1])]
            weights = shares + [swap(part, "ctx", 1) for part in shares]
            x, y = pairs[0]
            given.append(partial_product(core, turn, [x, after(y, pairs[1][1])], weights))
            x, y = pairs[1]
            given.append(partial_product(core, turn, [x, after(y, given[0])], weights))
        elif index > 1:
            x, y = pairs[-1]
            y = after(y, partials[1 if index == 2 else index - 3], given[-1])
            if index == last:
                y = after(y, *products)
            given.append(partial_product(core, turn, [x, y], weights))
        partials += [swap(part, "head", 1) for part in given[len(partials) :]]
        products.append(project(pairs[-1], out_weight, place, (0, 2), F32))
    out = None
    for product, partial, (first, _) in zip(products, partials, cuts):
        out = join(product, partial, first, rows, out)
    return out


def any_line(query_rows, key_rows, value_rows, frequencies, norm_gain, out_weight):
    core, place, turn = positions()
    parts = (query_rows, key_rows, value_rows, frequencies, norm_gain)
    (normed,), _ = normed_output(core, place, turn, *parts, ((0, query_rows.shape[0]),))
    gathered = lax.all_gather(normed, "head", axis=1, tiled=True)
    return jnp.dot(gathered, out_weight, preferred_element_type=F32).astype(BF16)


def solution(mesh):
    return jax.shard_map(
        line_of_four if mesh.shape["head"] == 4 and mesh.shape["ctx"] % 4 == 0 else any_line,
        mesh=mesh,
        in_specs=(
            P("ctx", "head"),
            P("ctx", "head"),
            P("ctx", "head"),
            P("head", None, None),
            P("head"),
            P(None, "head"),
        ),
        out_specs=P("ctx", "head"),
        check_vma=False,
    )
```

```python
import functools
import math

import jax
import jax.numpy as jnp
from jax import lax
from jax.experimental import pallas as pl
from jax.experimental.pallas import tpu as pltpu
from jax.sharding import PartitionSpec as P

F32 = jnp.float32
BF16 = jnp.bfloat16
SPAN = 512
TILE = 256
SIN_TERMS = (3.1415820220956054, -5.167142794166117, 2.5418990064386224, -0.5546361406826548)
COS_TERMS = (0.9999932955183647, -4.933938020185013, 4.0412838463445455, -1.2221270624224843)
ROUNDER = 1.5 * 2.0**23
LARGE = pltpu.CompilerParams(vmem_limit_bytes=56 << 20)
SMALL = pltpu.CompilerParams(vmem_limit_bytes=20 << 20)
FREE = pl.CostEstimate(flops=0, bytes_accessed=0, transcendentals=0)


def dot(a, b, contract):
    return lax.dot_general(a, b, ((contract[:1], contract[1:]), ((), ())), preferred_element_type=F32)


def poly(terms, scale, u):
    value = F32(terms[-1] * scale)
    for term in terms[-2::-1]:
        value = value * u + F32(term * scale)
    return value


def cos_sin(phase, amplitude):
    turns = phase * F32(1.0 / (2.0 * math.pi))
    part = turns - ((turns + F32(ROUNDER)) - F32(ROUNDER))
    u = part * part
    scale = math.sqrt(2.0 * amplitude)
    half_sin = poly(SIN_TERMS, scale, u) * part
    half_cos = poly(COS_TERMS, scale, u)
    return F32(amplitude) - half_sin * half_sin, half_sin * half_cos


def key_kernel(has_weight, core_ref, place_ref, turn_ref, key_ref, value_ref, freq_ref, *refs):
    if has_weight:
        refs[-1][...] = refs[0][...]
        refs = refs[1:]
    feat_ref, sent_ref, kept_ref, prefix_ref = refs[:4]
    rows = key_ref.shape[0]
    group, width, count = freq_ref.shape
    span = min(SPAN, rows)
    amplitude = 1.0 / math.sqrt(count)
    tiles = [(head, start) for head in range(group) for start in range(0, rows, TILE)]

    def phase_of(head, start):
        lanes = slice(head * width, (head + 1) * width)
        return dot(freq_ref[head], key_ref[start : start + TILE, lanes], (0, 1))

    def add_state(head, start, features):
        lanes = slice(head * width, (head + 1) * width)
        state = dot(features, value_ref[start : start + TILE, lanes], (1, 0))
        sums[head] = state if start == 0 else sums[head] + state
        index = (start + TILE) // span - 1
        if (start + TILE) % span == 0 and index < prefix_ref.shape[1]:
            prefix_ref[head, index] = sums[head]

    sums = [None] * group
    phase, waiting = phase_of(*tiles[0]), None
    for index, (head, start) in enumerate(tiles):
        following = phase_of(*tiles[index + 1]) if index + 1 < len(tiles) else None
        cosine, sine = cos_sin(phase, amplitude)
        features = jnp.concatenate([cosine.astype(BF16), sine.astype(BF16)], axis=0)
        feat_ref[head, :, start : start + TILE] = features
        if waiting is not None:
            add_state(*waiting)
        phase, waiting = following, (head, start, features)
    add_state(*waiting)
    sums = [total.astype(BF16) for total in sums]
    half = pl.num_programs(0) // 2

    @pl.when(pl.program_id(0) < half)
    def _():
        for head in range(group):
            sent_ref[head] = sums[head]

    @pl.when(pl.program_id(0) >= half)
    def _():
        for head in range(group):
            kept_ref[head] = sums[head]


def key_side(core, place, turn, key_rows, value_rows, frequencies, weight=None):
    rows = key_rows.shape[0]
    heads, width, count = frequencies.shape
    prior = max(1, rows // min(SPAN, rows) - 1)
    half = heads // 2
    group = 2 if half % 2 == 0 else 1
    steps, half_steps = heads // group, half // group

    def block(g, c):
        return (g + half_steps * (1 - c[0])) % steps

    in_specs = [
        pl.BlockSpec((rows, group * width), lambda g, c, p, t: (0, block(g, c))),
        pl.BlockSpec((rows, group * width), lambda g, c, p, t: (0, block(g, c))),
        pl.BlockSpec((group, width, count), lambda g, c, p, t: (block(g, c), 0, 0)),
    ]
    out_specs = [
        pl.BlockSpec((group, 2 * count, rows), lambda g, c, p, t: (block(g, c), 0, 0)),
        pl.BlockSpec((group, 2 * count, width), lambda g, c, p, t: (jnp.minimum(g, half_steps - 1), 0, 0)),
        pl.BlockSpec((group, 2 * count, width), lambda g, c, p, t: (jnp.maximum(g - half_steps, 0), 0, 0)),
        pl.BlockSpec((group, prior, 2 * count, width), lambda g, c, p, t: (block(g, c), 0, 0, 0)),
    ]
    out_shape = [
        jax.ShapeDtypeStruct((heads, 2 * count, rows), BF16),
        jax.ShapeDtypeStruct((half, 2 * count, width), BF16),
        jax.ShapeDtypeStruct((half, 2 * count, width), BF16),
        jax.ShapeDtypeStruct((heads, prior, 2 * count, width), F32),
    ]
    operands = [key_rows, value_rows, frequencies]
    if weight is not None:
        depth, cols = weight.shape[0] // 4, weight.shape[1]
        piece = depth // 2 // steps

        def rows_of(g, c, p, t):
            return ((p[0] ^ (1 + 2 * c[0])) * 2 + t[0]) * steps + g, 0

        in_specs.append(pl.BlockSpec((piece, cols), rows_of))
        out_specs.append(pl.BlockSpec((piece, cols), lambda g, c, p, t: (g, 0)))
        out_shape.append(jax.ShapeDtypeStruct((depth // 2, cols), weight.dtype))
        operands.append(weight)
    return pl.pallas_call(
        functools.partial(key_kernel, weight is not None),
        grid_spec=pltpu.PrefetchScalarGridSpec(
            num_scalar_prefetch=3, grid=(steps,), in_specs=in_specs, out_specs=out_specs
        ),
        out_shape=out_shape,
        compiler_params=LARGE,
        cost_estimate=FREE,
        name="key_side",
    )(core, place, turn, *operands)


def query_kernel(query_ref, value_ref, freq_ref, key_feat_ref, feat_ref, local_ref):
    rows = query_ref.shape[0]
    group, width, count = freq_ref.shape
    span = min(SPAN, rows)
    amplitude = 1.0 / math.sqrt(count)
    below = lax.broadcasted_iota(jnp.int32, (TILE, TILE), 0)
    causal = below >= lax.broadcasted_iota(jnp.int32, (TILE, TILE), 1)
    tiles = [(head, start) for head in range(group) for start in range(0, rows, TILE)]

    def phase_of(head, start):
        lanes = slice(head * width, (head + 1) * width)
        return dot(query_ref[start : start + TILE, lanes], freq_ref[head], (1, 0))

    def attend(head, start, features):
        lanes = slice(head * width, (head + 1) * width)
        total = None
        for other in range(start // span * span, start + TILE, TILE):
            theirs = slice(other, other + TILE)
            scores = dot(features, key_feat_ref[head, :, theirs], (1, 0))
            if other == start:
                scores = jnp.where(causal, scores, F32(0.0))
            part = dot(scores.astype(BF16), value_ref[theirs, lanes], (1, 0))
            total = part if total is None else total + part
        local_ref[start : start + TILE, lanes] = total.astype(local_ref.dtype)

    phase, waiting = phase_of(*tiles[0]), None
    for index, (head, start) in enumerate(tiles):
        following = phase_of(*tiles[index + 1]) if index + 1 < len(tiles) else None
        cosine, sine = cos_sin(phase, amplitude)
        features = jnp.concatenate([cosine.astype(BF16), sine.astype(BF16)], axis=1)
        feat_ref[head, start : start + TILE, :] = features
        if waiting is not None:
            attend(*waiting)
        phase, waiting = following, (head, start, features)
    attend(*waiting)


def query_side(query_rows, value_rows, frequencies, key_feat):
    rows = query_rows.shape[0]
    heads, width, count = frequencies.shape
    group = 2 if heads % 2 == 0 else 1
    return pl.pallas_call(
        query_kernel,
        grid=(heads // group,),
        in_specs=[
            pl.BlockSpec((rows, group * width), lambda h: (0, h)),
            pl.BlockSpec((rows, group * width), lambda h: (0, h)),
            pl.BlockSpec((group, width, count), lambda h: (h, 0, 0)),
            pl.BlockSpec((group, 2 * count, rows), lambda h: (h, 0, 0)),
        ],
        out_specs=[
            pl.BlockSpec((group, rows, 2 * count), lambda h: (h, 0, 0)),
            pl.BlockSpec((rows, group * width), lambda h: (0, h)),
        ],
        out_shape=[
            jax.ShapeDtypeStruct((heads, rows, 2 * count), BF16),
            jax.ShapeDtypeStruct((rows, heads * width), BF16),
        ],
        compiler_params=LARGE,
        cost_estimate=FREE,
        name="query_side",
    )(query_rows, value_rows, frequencies, key_feat)


def finish_kernel(
    heads, span, cuts, core_ref, feat_ref, local_ref, theirs_ref, mine_ref, gain_ref, *refs
):
    prefix_ref, out_refs = refs[0], refs[-len(cuts) :]
    width = local_ref.shape[1] // heads
    kept = pl.program_id(0) >= pl.num_programs(0) // 2
    for head in range(heads):
        cols = slice(head * width, (head + 1) * width)
        gain = gain_ref[:, cols].astype(F32)
        before = jnp.where(kept, mine_ref[head].astype(F32), theirs_ref[head].astype(F32))
        for out_ref, (first, last) in zip(out_refs, cuts):
            starts = [first, *range(first - first % TILE + TILE, last, TILE)]
            for start, stop in zip(starts, starts[1:] + [last]):
                mine = slice(start, stop)
                carried = before
                if start // span:
                    carried = carried + prefix_ref[head, start // span - 1]
                prior = dot(feat_ref[head, mine, :], carried.astype(BF16), (1, 0))
                attended = local_ref[mine, cols].astype(F32) + prior
                square = jnp.mean(attended * attended, axis=-1, keepdims=True)
                normed = attended * lax.rsqrt(square + F32(1e-6)) * gain
                out_ref[start - first : stop - first, cols] = normed.astype(BF16)


def finish(core, feat, local_part, theirs, mine, gain, prefix, cuts):
    heads, all_rows, feats = feat.shape
    rows = cuts[-1][1]
    span = min(SPAN, all_rows)
    width = local_part.shape[1] // heads
    prior = prefix.shape[1]
    half = heads // 2
    group = 4 if half % 4 == 0 and rows < span else 2 if half % 2 == 0 else 1
    steps, half_steps = heads // group, half // group

    def block(g, c):
        return (g + half_steps * (1 - c[0])) % steps

    in_specs = [
        pl.BlockSpec((group, rows, feats), lambda g, c: (block(g, c), 0, 0)),
        pl.BlockSpec((rows, group * width), lambda g, c: (0, block(g, c))),
        pl.BlockSpec((group, feats, width), lambda g, c: (jnp.minimum(g, half_steps - 1), 0, 0)),
        pl.BlockSpec((group, feats, width), lambda g, c: (jnp.maximum(g - half_steps, 0), 0, 0)),
        pl.BlockSpec((1, group * width), lambda g, c: (0, block(g, c))),
    ]
    operands = [feat, local_part, theirs, mine, gain]
    if rows > span:
        in_specs.append(pl.BlockSpec((group, prior, feats, width), lambda g, c: (block(g, c), 0, 0, 0)))
        operands.append(prefix)
    return pl.pallas_call(
        functools.partial(finish_kernel, group, span, cuts),
        grid_spec=pltpu.PrefetchScalarGridSpec(
            num_scalar_prefetch=1,
            grid=(steps,),
            in_specs=in_specs,
            out_specs=[
                pl.BlockSpec((last - first, group * width), lambda g, c: (0, block(g, c))) for first, last in cuts
            ],
        ),
        out_shape=[jax.ShapeDtypeStruct((last - first, heads * width), BF16) for first, last in cuts],
        compiler_params=LARGE,
        cost_estimate=FREE,
        name="finish",
    )(core, *operands)


def project_kernel(sources, place_ref, *refs):
    out_ref = refs[-1]
    total = None
    for x_ref, w_ref in zip(refs[:sources], refs[sources : 2 * sources]):
        part = dot(x_ref[...], w_ref[...], (1, 0))
        total = part if total is None else total + part
    out_ref[...] = total.astype(out_ref.dtype)


def project(blocks, weight, place, hops, dtype=BF16):
    size, depth = blocks[0].shape
    cols = weight.shape[1]
    step = min(256, cols)

    def rows_of(source):
        return lambda n, p: (p[0] ^ hops[source], n)

    sources = len(blocks)
    return pl.pallas_call(
        functools.partial(project_kernel, sources),
        grid_spec=pltpu.PrefetchScalarGridSpec(
            num_scalar_prefetch=1,
            grid=(cols // step,),
            in_specs=[pl.BlockSpec((size, depth), lambda n, p: (0, 0)) for _ in blocks]
            + [pl.BlockSpec((depth, step), rows_of(source)) for source in range(sources)],
            out_specs=pl.BlockSpec((size, step), lambda n, p: (0, n)),
        ),
        out_shape=jax.ShapeDtypeStruct((size, cols), dtype),
        compiler_params=SMALL,
        cost_estimate=FREE,
        name="project",
    )(place, *blocks, *[weight] * sources)


def partial_kernel(core_ref, turn_ref, x_ref, y_ref, *refs):
    weights, out_ref = refs[:-1], refs[-1]
    count = len(weights) // 2
    swapped, turned = core_ref[0] != 0, turn_ref[0] != 0
    x, y = x_ref[...], y_ref[...]
    half = x.shape[1] // 2
    total = None
    for rows, pieces in ((jnp.where(swapped, y, x), weights[:count]), (jnp.where(swapped, x, y), weights[count:])):
        left, right = rows[:, :half], rows[:, half:]
        sides = [jnp.where(turned, right, left), jnp.where(turned, left, right)]
        rows = jnp.concatenate(sides, axis=1)
        first = 0
        for piece in pieces:
            last = first + piece.shape[0]
            part = dot(rows[:, first:last], piece[...], (1, 0))
            total = part if total is None else total + part
            first = last
    out_ref[...] = total.astype(out_ref.dtype)


def partial_product(core, turn, blocks, weights):
    size, depth = blocks[0].shape
    cols = weights[0].shape[1]
    step = min(256, cols)
    return pl.pallas_call(
        partial_kernel,
        grid_spec=pltpu.PrefetchScalarGridSpec(
            num_scalar_prefetch=2,
            grid=(cols // step,),
            in_specs=[pl.BlockSpec((size, depth), lambda n, c, t: (0, 0)) for _ in blocks]
            + [pl.BlockSpec((weight.shape[0], step), lambda n, c, t: (0, n)) for weight in weights],
            out_specs=pl.BlockSpec((size, step), lambda n, c, t: (0, n)),
        ),
        out_shape=jax.ShapeDtypeStruct((size, cols), BF16),
        compiler_params=SMALL,
        cost_estimate=FREE,
        name="partial_product",
    )(core, turn, *blocks, *weights)


def join_kernel(a_ref, b_ref, *refs):
    out_ref = refs[-1]
    out_ref[...] = (a_ref[...] + b_ref[...].astype(F32)).astype(out_ref.dtype)


def join(a, b, first, rows, into=None):
    size, cols = a.shape
    step = math.gcd(first, size, 256)
    index = first // step
    spec = pl.BlockSpec((step, cols), lambda r: (r, 0))
    return pl.pallas_call(
        join_kernel,
        grid=(size // step,),
        in_specs=[spec, spec] + [pl.BlockSpec(memory_space=pl.ANY)] * (into is not None),
        out_specs=pl.BlockSpec((step, cols), lambda r: (index + r, 0)),
        out_shape=jax.ShapeDtypeStruct((rows, cols), BF16),
        input_output_aliases={} if into is None else {2: 0},
        compiler_params=SMALL,
        cost_estimate=FREE,
        name="join",
    )(a, b, *([] if into is None else [into]))


def after(value, *others):
    return lax.optimization_barrier((value, *others))[0]


def swap(value, axis, distance):
    return lax.ppermute(value, axis, [(i, i ^ distance) for i in range(lax.axis_size(axis))])


def earlier_states(sent, kept, meanwhile):
    count, mine = lax.axis_size("ctx"), lax.axis_index("ctx")
    core = mine % 2
    partner = swap(sent, "ctx", 1)
    total = (kept.astype(F32) + partner.astype(F32)).astype(BF16)
    earlier = jnp.zeros(kept.shape, F32)
    beside = meanwhile(total)
    distance = 2
    while distance < count:
        radix = min(4, count // distance)
        last = distance * radix >= count
        added = total.astype(F32)
        for step in range(1, radix):
            hop = step * distance
            pairs = [(i, i ^ hop) for i in range(count) if not last or i < i ^ hop]
            theirs = lax.ppermute(total, "ctx", pairs)
            if last:
                theirs = after(theirs, *beside)
            theirs = theirs.astype(F32)
            lower = (mine ^ hop) < mine
            earlier = earlier + jnp.where(lower, theirs, F32(0.0))
            added = added + theirs
        total = added.astype(BF16)
        distance *= radix
    own = earlier + jnp.where(core == 1, partner.astype(F32), F32(0.0))
    given = earlier + jnp.where(core == 0, kept.astype(F32), F32(0.0))
    return swap(given.astype(BF16), "ctx", 1), own.astype(BF16), beside


def normed_output(core, place, turn, query_rows, key_rows, value_rows, frequencies, norm_gain, weight=None):
    key_feat, sent, kept, prefix, *share = key_side(core, place, turn, key_rows, value_rows, frequencies, weight)

    gain = norm_gain.reshape(1, -1)

    def meanwhile(total):
        return query_side(query_rows, value_rows, after(frequencies, total, gain), key_feat)

    theirs, own, (query_feat, local_part) = earlier_states(sent, kept, meanwhile)

    def blocks_of(cuts, *others):
        return finish(core, after(query_feat, *others), local_part, theirs, own, gain, prefix, cuts)

    return blocks_of, share


def positions():
    spot, place = lax.axis_index("ctx"), lax.axis_index("head")
    return [value.astype(jnp.int32).reshape(1) for value in (spot % 2, place, (spot // 2 + spot // 4) % 2)]


def line_of_four(query_rows, key_rows, value_rows, frequencies, norm_gain, out_weight):
    rows = query_rows.shape[0]
    core, place, turn = positions()
    sizes = [rows * part // 16 for part in (2, 2, 3, 3, 2, 2, 2)]
    edges = [sum(sizes[:i]) for i in range(len(sizes) + 1)]
    cuts = tuple(zip(edges[:-1], edges[1:]))
    parts = (query_rows, key_rows, value_rows, frequencies, norm_gain)
    blocks_of, (share,) = normed_output(core, place, turn, *parts, out_weight)
    blocks = blocks_of(cuts[:1])
    share = after(swap(share, "head", 1), *blocks)
    half = share.shape[0] // 2
    halves = [share[:half], share[half:]]
    blocks = [*blocks, *blocks_of(cuts[1:], *halves)]
    last = len(blocks) - 1
    pairs, given, partials, products = [], [], [], []
    weights = None
    for index, block in enumerate(blocks):
        if index > 2:
            block = after(block, partials[0] if index == 3 else given[index - 2])
        pairs.append([block, swap(block, "head", 2)])
        if index == 1:
            others = [swap(part, "ctx", hop) for part, hop in zip(halves, (2, 4))]
            shares = [after(share, blocks[-1], pairs[0][1])] + [after(other, pairs[0][1]) for other in others]
            weights = shares + [swap(part, "ctx", 1) for part in shares]
            x, y = pairs[0]
            given.append(partial_product(core, turn, [x, y], weights))
            x, y = pairs[1]
            given.append(partial_product(core, turn, [x, after(y, given[0])], weights))
        elif index > 1:
            x, y = pairs[-1]
            y = after(y, partials[1 if index == 2 else index - 3], given[-1])
            if index == last:
                y = after(y, *products)
            given.append(partial_product(core, turn, [x, y], weights))
        partials += [swap(part, "head", 1) for part in given[len(partials) :]]
        products.append(project(pairs[-1], out_weight, place, (0, 2), F32))
    out = None
    for product, partial, (first, _) in zip(products, partials, cuts):
        out = join(product, partial, first, rows, out)
    return out


def any_line(query_rows, key_rows, value_rows, frequencies, norm_gain, out_weight):
    core, place, turn = positions()
    parts = (query_rows, key_rows, value_rows, frequencies, norm_gain)
    blocks_of, _ = normed_output(core, place, turn, *parts)
    (normed,) = blocks_of(((0, query_rows.shape[0]),))
    gathered = lax.all_gather(normed, "head", axis=1, tiled=True)
    return jnp.dot(gathered, out_weight, preferred_element_type=F32).astype(BF16)


def solution(mesh):
    return jax.shard_map(
        line_of_four if mesh.shape["head"] == 4 and mesh.shape["ctx"] % 8 == 0 else any_line,
        mesh=mesh,
        in_specs=(
            P("ctx", "head"),
            P("ctx", "head"),
            P("ctx", "head"),
            P("head", None, None),
            P("head"),
            P(None, "head"),
        ),
        out_specs=P("ctx", "head"),
        check_vma=False,
    )
```

```python
import functools
import math

import jax
import jax.numpy as jnp
from jax import lax
from jax.experimental import pallas as pl
from jax.experimental.pallas import tpu as pltpu
from jax.sharding import PartitionSpec as P

F32 = jnp.float32
BF16 = jnp.bfloat16
SPAN = 512
TILE = 256
SIN_TERMS = (3.1415820220956054, -5.167142794166117, 2.5418990064386224, -0.5546361406826548)
COS_TERMS = (0.9999932955183647, -4.933938020185013, 4.0412838463445455, -1.2221270624224843)
ROUNDER = 1.5 * 2.0**23
LARGE = pltpu.CompilerParams(vmem_limit_bytes=56 << 20)
SMALL = pltpu.CompilerParams(vmem_limit_bytes=20 << 20)
FREE = pl.CostEstimate(flops=0, bytes_accessed=0, transcendentals=0)


def dot(a, b, contract):
    return lax.dot_general(a, b, ((contract[:1], contract[1:]), ((), ())), preferred_element_type=F32)


def poly(terms, scale, u):
    value = F32(terms[-1] * scale)
    for term in terms[-2::-1]:
        value = value * u + F32(term * scale)
    return value


def cos_sin(phase, amplitude):
    turns = phase * F32(1.0 / (2.0 * math.pi))
    part = turns - ((turns + F32(ROUNDER)) - F32(ROUNDER))
    u = part * part
    scale = math.sqrt(2.0 * amplitude)
    half_sin = poly(SIN_TERMS, scale, u) * part
    half_cos = poly(COS_TERMS, scale, u)
    return F32(amplitude) - half_sin * half_sin, half_sin * half_cos


def key_kernel(has_weight, core_ref, place_ref, turn_ref, key_ref, value_ref, freq_ref, *refs):
    if has_weight:
        refs[-1][...] = refs[0][...]
        refs = refs[1:]
    feat_ref, sent_ref, kept_ref, prefix_ref = refs[:4]
    rows = key_ref.shape[0]
    group, width, count = freq_ref.shape
    span = min(SPAN, rows)
    amplitude = 1.0 / math.sqrt(count)
    tiles = [(head, start) for head in range(group) for start in range(0, rows, TILE)]
    turned = [freq_ref[head].T for head in range(group)]

    def phase_of(head, start):
        lanes = slice(head * width, (head + 1) * width)
        return dot(turned[head], key_ref[start : start + TILE, lanes], (1, 1))

    def add_state(head, start, features):
        lanes = slice(head * width, (head + 1) * width)
        state = dot(features, value_ref[start : start + TILE, lanes], (1, 0))
        sums[head] = state if start == 0 else sums[head] + state
        index = (start + TILE) // span - 1
        if (start + TILE) % span == 0 and index < prefix_ref.shape[1]:
            prefix_ref[head, index] = sums[head]

    sums = [None] * group
    phase, waiting = phase_of(*tiles[0]), None
    for index, (head, start) in enumerate(tiles):
        following = phase_of(*tiles[index + 1]) if index + 1 < len(tiles) else None
        cosine, sine = cos_sin(phase, amplitude)
        features = jnp.concatenate([cosine.astype(BF16), sine.astype(BF16)], axis=0)
        feat_ref[head, :, start : start + TILE] = features
        if waiting is not None:
            add_state(*waiting)
        phase, waiting = following, (head, start, features)
    add_state(*waiting)
    sums = [total.astype(BF16) for total in sums]
    half = pl.num_programs(0) // 2

    @pl.when(pl.program_id(0) < half)
    def _():
        for head in range(group):
            sent_ref[head] = sums[head]

    @pl.when(pl.program_id(0) >= half)
    def _():
        for head in range(group):
            kept_ref[head] = sums[head]


def key_side(core, place, turn, key_rows, value_rows, frequencies, weight=None):
    rows = key_rows.shape[0]
    heads, width, count = frequencies.shape
    prior = max(1, rows // min(SPAN, rows) - 1)
    half = heads // 2
    group = 2 if half % 2 == 0 else 1
    steps, half_steps = heads // group, half // group

    def block(g, c):
        return (g + half_steps * (1 - c[0])) % steps

    in_specs = [
        pl.BlockSpec((rows, group * width), lambda g, c, p, t: (0, block(g, c))),
        pl.BlockSpec((rows, group * width), lambda g, c, p, t: (0, block(g, c))),
        pl.BlockSpec((group, width, count), lambda g, c, p, t: (block(g, c), 0, 0)),
    ]
    out_specs = [
        pl.BlockSpec((group, 2 * count, rows), lambda g, c, p, t: (block(g, c), 0, 0)),
        pl.BlockSpec((group, 2 * count, width), lambda g, c, p, t: (jnp.minimum(g, half_steps - 1), 0, 0)),
        pl.BlockSpec((group, 2 * count, width), lambda g, c, p, t: (jnp.maximum(g - half_steps, 0), 0, 0)),
        pl.BlockSpec((group, prior, 2 * count, width), lambda g, c, p, t: (block(g, c), 0, 0, 0)),
    ]
    out_shape = [
        jax.ShapeDtypeStruct((heads, 2 * count, rows), BF16),
        jax.ShapeDtypeStruct((half, 2 * count, width), BF16),
        jax.ShapeDtypeStruct((half, 2 * count, width), BF16),
        jax.ShapeDtypeStruct((heads, prior, 2 * count, width), F32),
    ]
    operands = [key_rows, value_rows, frequencies]
    if weight is not None:
        depth, cols = weight.shape[0] // 4, weight.shape[1]
        piece = depth // 2 // steps

        def rows_of(g, c, p, t):
            return ((p[0] ^ (1 + 2 * c[0])) * 2 + t[0]) * steps + g, 0

        in_specs.append(pl.BlockSpec((piece, cols), rows_of))
        out_specs.append(pl.BlockSpec((piece, cols), lambda g, c, p, t: (g, 0)))
        out_shape.append(jax.ShapeDtypeStruct((depth // 2, cols), weight.dtype))
        operands.append(weight)
    return pl.pallas_call(
        functools.partial(key_kernel, weight is not None),
        grid_spec=pltpu.PrefetchScalarGridSpec(
            num_scalar_prefetch=3, grid=(steps,), in_specs=in_specs, out_specs=out_specs
        ),
        out_shape=out_shape,
        compiler_params=LARGE,
        cost_estimate=FREE,
        name="key_side",
    )(core, place, turn, *operands)


def query_kernel(query_ref, value_ref, freq_ref, key_feat_ref, feat_ref, local_ref):
    rows = query_ref.shape[0]
    group, width, count = freq_ref.shape
    span = min(SPAN, rows)
    amplitude = 1.0 / math.sqrt(count)
    below = lax.broadcasted_iota(jnp.int32, (TILE, TILE), 0)
    causal = below >= lax.broadcasted_iota(jnp.int32, (TILE, TILE), 1)
    tiles = [(head, start) for head in range(group) for start in range(0, rows, TILE)]

    def phase_of(head, start):
        lanes = slice(head * width, (head + 1) * width)
        return dot(query_ref[start : start + TILE, lanes], freq_ref[head], (1, 0))

    def attend(head, start, features):
        lanes = slice(head * width, (head + 1) * width)
        total = None
        for other in range(start // span * span, start + TILE, TILE):
            theirs = slice(other, other + TILE)
            scores = dot(features, key_feat_ref[head, :, theirs], (1, 0))
            if other == start:
                scores = jnp.where(causal, scores, F32(0.0))
            part = dot(scores.astype(BF16), value_ref[theirs, lanes], (1, 0))
            total = part if total is None else total + part
        local_ref[start : start + TILE, lanes] = total.astype(local_ref.dtype)

    phase, waiting = phase_of(*tiles[0]), None
    for index, (head, start) in enumerate(tiles):
        following = phase_of(*tiles[index + 1]) if index + 1 < len(tiles) else None
        cosine, sine = cos_sin(phase, amplitude)
        features = jnp.concatenate([cosine.astype(BF16), sine.astype(BF16)], axis=1)
        feat_ref[head, start : start + TILE, :] = features
        if waiting is not None:
            attend(*waiting)
        phase, waiting = following, (head, start, features)
    attend(*waiting)


def query_side(query_rows, value_rows, frequencies, key_feat):
    rows = query_rows.shape[0]
    heads, width, count = frequencies.shape
    group = 2 if heads % 2 == 0 else 1
    return pl.pallas_call(
        query_kernel,
        grid=(heads // group,),
        in_specs=[
            pl.BlockSpec((rows, group * width), lambda h: (0, h)),
            pl.BlockSpec((rows, group * width), lambda h: (0, h)),
            pl.BlockSpec((group, width, count), lambda h: (h, 0, 0)),
            pl.BlockSpec((group, 2 * count, rows), lambda h: (h, 0, 0)),
        ],
        out_specs=[
            pl.BlockSpec((group, rows, 2 * count), lambda h: (h, 0, 0)),
            pl.BlockSpec((rows, group * width), lambda h: (0, h)),
        ],
        out_shape=[
            jax.ShapeDtypeStruct((heads, rows, 2 * count), BF16),
            jax.ShapeDtypeStruct((rows, heads * width), BF16),
        ],
        compiler_params=LARGE,
        cost_estimate=FREE,
        name="query_side",
    )(query_rows, value_rows, frequencies, key_feat)


def finish_kernel(
    heads, span, cuts, core_ref, feat_ref, local_ref, theirs_ref, mine_ref, gain_ref, *refs
):
    prefix_ref, out_refs = refs[0], refs[-len(cuts) :]
    width = local_ref.shape[1] // heads
    steps = pl.num_programs(0)
    kept = pl.program_id(0) >= steps // 2
    first_head = lax.rem(pl.program_id(0) + steps // 2 * (1 - core_ref[0]), steps) * heads
    gains = gain_ref[...].astype(F32)
    row = lax.broadcasted_iota(jnp.int32, gains.shape, 0)
    for head in range(heads):
        cols = slice(head * width, (head + 1) * width)
        gain = jnp.sum(jnp.where(row == first_head + head, gains, F32(0.0)), axis=0, keepdims=True)
        before = jnp.where(kept, mine_ref[head].astype(F32), theirs_ref[head].astype(F32))
        for out_ref, (first, last) in zip(out_refs, cuts):
            starts = [first, *range(first - first % TILE + TILE, last, TILE)]
            for start, stop in zip(starts, starts[1:] + [last]):
                mine = slice(start, stop)
                carried = before
                if start // span:
                    carried = carried + prefix_ref[head, start // span - 1]
                prior = dot(feat_ref[head, mine, :], carried.astype(BF16), (1, 0))
                attended = local_ref[mine, cols].astype(F32) + prior
                square = jnp.mean(attended * attended, axis=-1, keepdims=True)
                normed = attended * lax.rsqrt(square + F32(1e-6)) * gain
                out_ref[start - first : stop - first, cols] = normed.astype(BF16)


def finish(core, feat, local_part, theirs, mine, gain, prefix, cuts):
    heads, all_rows, feats = feat.shape
    rows = cuts[-1][1]
    span = min(SPAN, all_rows)
    width = local_part.shape[1] // heads
    prior = prefix.shape[1]
    half = heads // 2
    group = 4 if half % 4 == 0 and rows < span else 2 if half % 2 == 0 else 1
    steps, half_steps = heads // group, half // group

    def block(g, c):
        return (g + half_steps * (1 - c[0])) % steps

    in_specs = [
        pl.BlockSpec((group, rows, feats), lambda g, c: (block(g, c), 0, 0)),
        pl.BlockSpec((rows, group * width), lambda g, c: (0, block(g, c))),
        pl.BlockSpec((group, feats, width), lambda g, c: (jnp.minimum(g, half_steps - 1), 0, 0)),
        pl.BlockSpec((group, feats, width), lambda g, c: (jnp.maximum(g - half_steps, 0), 0, 0)),
        pl.BlockSpec(gain.shape, lambda g, c: (0, 0)),
    ]
    operands = [feat, local_part, theirs, mine, gain]
    if rows > span:
        in_specs.append(pl.BlockSpec((group, prior, feats, width), lambda g, c: (block(g, c), 0, 0, 0)))
        operands.append(prefix)
    return pl.pallas_call(
        functools.partial(finish_kernel, group, span, cuts),
        grid_spec=pltpu.PrefetchScalarGridSpec(
            num_scalar_prefetch=1,
            grid=(steps,),
            in_specs=in_specs,
            out_specs=[
                pl.BlockSpec((last - first, group * width), lambda g, c: (0, block(g, c))) for first, last in cuts
            ],
        ),
        out_shape=[jax.ShapeDtypeStruct((last - first, heads * width), BF16) for first, last in cuts],
        compiler_params=LARGE,
        cost_estimate=FREE,
        name="finish",
    )(core, *operands)


def project_kernel(sources, place_ref, *refs):
    out_ref = refs[-1]
    total = None
    for x_ref, w_ref in zip(refs[:sources], refs[sources : 2 * sources]):
        part = dot(x_ref[...], w_ref[...], (1, 0))
        total = part if total is None else total + part
    out_ref[...] = total.astype(out_ref.dtype)


def project(blocks, weight, place, hops, dtype=BF16):
    size, depth = blocks[0].shape
    cols = weight.shape[1]
    step = min(256, cols)

    def rows_of(source):
        return lambda n, p: (p[0] ^ hops[source], n)

    sources = len(blocks)
    return pl.pallas_call(
        functools.partial(project_kernel, sources),
        grid_spec=pltpu.PrefetchScalarGridSpec(
            num_scalar_prefetch=1,
            grid=(cols // step,),
            in_specs=[pl.BlockSpec((size, depth), lambda n, p: (0, 0)) for _ in blocks]
            + [pl.BlockSpec((depth, step), rows_of(source)) for source in range(sources)],
            out_specs=pl.BlockSpec((size, step), lambda n, p: (0, n)),
        ),
        out_shape=jax.ShapeDtypeStruct((size, cols), dtype),
        compiler_params=SMALL,
        cost_estimate=FREE,
        name="project",
    )(place, *blocks, *[weight] * sources)


def partial_kernel(core_ref, turn_ref, x_ref, y_ref, *refs):
    weights, out_ref = refs[:-1], refs[-1]
    count = len(weights) // 2
    swapped, turned = core_ref[0] != 0, turn_ref[0] != 0
    x, y = x_ref[...], y_ref[...]
    half = x.shape[1] // 2
    total = None
    for rows, pieces in ((jnp.where(swapped, y, x), weights[:count]), (jnp.where(swapped, x, y), weights[count:])):
        left, right = rows[:, :half], rows[:, half:]
        sides = [jnp.where(turned, right, left), jnp.where(turned, left, right)]
        rows = jnp.concatenate(sides, axis=1)
        first = 0
        for piece in pieces:
            last = first + piece.shape[0]
            part = dot(rows[:, first:last], piece[...], (1, 0))
            total = part if total is None else total + part
            first = last
    out_ref[...] = total.astype(out_ref.dtype)


def partial_product(core, turn, blocks, weights):
    size, depth = blocks[0].shape
    cols = weights[0].shape[1]
    step = min(256, cols)
    return pl.pallas_call(
        partial_kernel,
        grid_spec=pltpu.PrefetchScalarGridSpec(
            num_scalar_prefetch=2,
            grid=(cols // step,),
            in_specs=[pl.BlockSpec((size, depth), lambda n, c, t: (0, 0)) for _ in blocks]
            + [pl.BlockSpec((weight.shape[0], step), lambda n, c, t: (0, n)) for weight in weights],
            out_specs=pl.BlockSpec((size, step), lambda n, c, t: (0, n)),
        ),
        out_shape=jax.ShapeDtypeStruct((size, cols), BF16),
        compiler_params=SMALL,
        cost_estimate=FREE,
        name="partial_product",
    )(core, turn, *blocks, *weights)


def join_kernel(a_ref, b_ref, *refs):
    out_ref = refs[-1]
    out_ref[...] = (a_ref[...] + b_ref[...].astype(F32)).astype(out_ref.dtype)


def join(a, b, first, rows, into=None):
    size, cols = a.shape
    step = math.gcd(first, size, 256)
    index = first // step
    spec = pl.BlockSpec((step, cols), lambda r: (r, 0))
    return pl.pallas_call(
        join_kernel,
        grid=(size // step,),
        in_specs=[spec, spec] + [pl.BlockSpec(memory_space=pl.ANY)] * (into is not None),
        out_specs=pl.BlockSpec((step, cols), lambda r: (index + r, 0)),
        out_shape=jax.ShapeDtypeStruct((rows, cols), BF16),
        input_output_aliases={} if into is None else {2: 0},
        compiler_params=SMALL,
        cost_estimate=FREE,
        name="join",
    )(a, b, *([] if into is None else [into]))


def after(value, *others):
    return lax.optimization_barrier((value, *others))[0]


def swap(value, axis, distance):
    return lax.ppermute(value, axis, [(i, i ^ distance) for i in range(lax.axis_size(axis))])


def earlier_states(sent, kept, meanwhile):
    count, mine = lax.axis_size("ctx"), lax.axis_index("ctx")
    core = mine % 2
    partner = swap(sent, "ctx", 1)
    total = (kept.astype(F32) + partner.astype(F32)).astype(BF16)
    earlier = jnp.zeros(kept.shape, F32)
    beside = meanwhile(total)
    distance = 2
    while distance < count:
        radix = min(4, count // distance)
        last = distance * radix >= count
        added = total.astype(F32)
        for step in range(1, radix):
            hop = step * distance
            pairs = [(i, i ^ hop) for i in range(count) if not last or i < i ^ hop]
            theirs = lax.ppermute(total, "ctx", pairs)
            if last:
                theirs = after(theirs, *beside)
            theirs = theirs.astype(F32)
            lower = (mine ^ hop) < mine
            earlier = earlier + jnp.where(lower, theirs, F32(0.0))
            added = added + theirs
        total = added.astype(BF16)
        distance *= radix
    own = earlier + jnp.where(core == 1, partner.astype(F32), F32(0.0))
    given = earlier + jnp.where(core == 0, kept.astype(F32), F32(0.0))
    return swap(given.astype(BF16), "ctx", 1), own.astype(BF16), beside


def normed_output(core, place, turn, query_rows, key_rows, value_rows, frequencies, norm_gain, weight=None):
    key_feat, sent, kept, prefix, *share = key_side(core, place, turn, key_rows, value_rows, frequencies, weight)

    gain = norm_gain.reshape(frequencies.shape[0], -1)

    def meanwhile(total):
        return query_side(query_rows, value_rows, after(frequencies, total), key_feat)

    theirs, own, (query_feat, local_part) = earlier_states(sent, kept, meanwhile)

    def blocks_of(cuts, *others):
        return finish(core, after(query_feat, *others), local_part, theirs, own, gain, prefix, cuts)

    return blocks_of, share


def positions():
    spot, place = lax.axis_index("ctx"), lax.axis_index("head")
    return [value.astype(jnp.int32).reshape(1) for value in (spot % 2, place, (spot // 2 + spot // 4) % 2)]


def line_of_four(query_rows, key_rows, value_rows, frequencies, norm_gain, out_weight):
    rows = query_rows.shape[0]
    core, place, turn = positions()
    sizes = [rows * part // 16 for part in (2, 2, 3, 3, 3, 2, 1)]
    edges = [sum(sizes[:i]) for i in range(len(sizes) + 1)]
    cuts = tuple(zip(edges[:-1], edges[1:]))
    parts = (query_rows, key_rows, value_rows, frequencies, norm_gain)
    blocks_of, (share,) = normed_output(core, place, turn, *parts, out_weight)
    blocks = blocks_of(cuts[:1])
    share = after(swap(share, "head", 1), *blocks)
    half = share.shape[0] // 2
    halves = [share[:half], share[half:]]
    blocks = [*blocks, *blocks_of(cuts[1:], *halves)]
    last = len(blocks) - 1
    pairs, given, partials, products = [], [], [], []
    weights = None
    for index, block in enumerate(blocks):
        if index > 2:
            block = after(block, partials[0] if index == 3 else given[index - 2], products[max(1, index - 3)])
        pairs.append([block, swap(block, "head", 2)])
        if index == 1:
            others = [swap(part, "ctx", hop) for part, hop in zip(halves, (2, 4))]
            shares = [after(share, blocks[-1], pairs[0][1])] + [after(other, pairs[0][1]) for other in others]
            weights = shares + [swap(part, "ctx", 1) for part in shares]
            x, y = pairs[0]
            given.append(partial_product(core, turn, [x, y], weights))
            x, y = pairs[1]
            given.append(partial_product(core, turn, [x, after(y, given[0])], weights))
        elif index > 1:
            x, y = pairs[-1]
            y = after(y, partials[1 if index == 2 else index - 3], given[-1])
            if index == last:
                y = after(y, *products)
            given.append(partial_product(core, turn, [x, y], weights))
        partials += [swap(part, "head", 1) for part in given[len(partials) :]]
        products.append(project(pairs[-1], out_weight, place, (0, 2), F32))
    out = None
    for product, partial, (first, _) in zip(products, partials, cuts):
        out = join(product, partial, first, rows, out)
    return out


def any_line(query_rows, key_rows, value_rows, frequencies, norm_gain, out_weight):
    core, place, turn = positions()
    parts = (query_rows, key_rows, value_rows, frequencies, norm_gain)
    blocks_of, _ = normed_output(core, place, turn, *parts)
    (normed,) = blocks_of(((0, query_rows.shape[0]),))
    gathered = lax.all_gather(normed, "head", axis=1, tiled=True)
    return jnp.dot(gathered, out_weight, preferred_element_type=F32).astype(BF16)


def solution(mesh):
    return jax.shard_map(
        line_of_four if mesh.shape["head"] == 4 and mesh.shape["ctx"] % 8 == 0 else any_line,
        mesh=mesh,
        in_specs=(
            P("ctx", "head"),
            P("ctx", "head"),
            P("ctx", "head"),
            P("head", None, None),
            P("head"),
            P(None, "head"),
        ),
        out_specs=P("ctx", "head"),
        check_vma=False,
    )
```

```python
import functools
import math

import jax
import jax.numpy as jnp
from jax import lax
from jax.experimental import pallas as pl
from jax.experimental.pallas import tpu as pltpu
from jax.sharding import PartitionSpec as P

F32 = jnp.float32
BF16 = jnp.bfloat16
SPAN = 512
TILE = 256
SIN_TERMS = (3.1415820220956054, -5.167142794166117, 2.5418990064386224, -0.5546361406826548)
COS_TERMS = (0.9999932955183647, -4.933938020185013, 4.0412838463445455, -1.2221270624224843)
ROUNDER = 1.5 * 2.0**23
LARGE = pltpu.CompilerParams(vmem_limit_bytes=56 << 20)
SMALL = pltpu.CompilerParams(vmem_limit_bytes=20 << 20)
FREE = pl.CostEstimate(flops=0, bytes_accessed=0, transcendentals=0)


def dot(a, b, contract):
    return lax.dot_general(a, b, ((contract[:1], contract[1:]), ((), ())), preferred_element_type=F32)


def poly(terms, scale, u):
    value = F32(terms[-1] * scale)
    for term in terms[-2::-1]:
        value = value * u + F32(term * scale)
    return value


def cos_sin(phase, amplitude):
    turns = phase * F32(1.0 / (2.0 * math.pi))
    part = turns - ((turns + F32(ROUNDER)) - F32(ROUNDER))
    u = part * part
    scale = math.sqrt(2.0 * amplitude)
    half_sin = poly(SIN_TERMS, scale, u) * part
    half_cos = poly(COS_TERMS, scale, u)
    return F32(amplitude) - half_sin * half_sin, half_sin * half_cos


def key_kernel(has_weight, core_ref, place_ref, turn_ref, key_ref, value_ref, freq_ref, *refs):
    if has_weight:
        refs[-1][...] = refs[0][...]
        refs = refs[1:]
    feat_ref, sent_ref, kept_ref, prefix_ref = refs[:4]
    rows = key_ref.shape[0]
    group, width, count = freq_ref.shape
    span = min(SPAN, rows)
    amplitude = 1.0 / math.sqrt(count)
    tiles = [(head, start) for head in range(group) for start in range(0, rows, TILE)]
    turned = [freq_ref[head].T for head in range(group)]

    def phase_of(head, start):
        lanes = slice(head * width, (head + 1) * width)
        return dot(turned[head], key_ref[start : start + TILE, lanes], (1, 1))

    def add_state(head, start, features):
        lanes = slice(head * width, (head + 1) * width)
        state = dot(features, value_ref[start : start + TILE, lanes], (1, 0))
        sums[head] = state if start == 0 else sums[head] + state
        index = (start + TILE) // span - 1
        if (start + TILE) % span == 0 and index < prefix_ref.shape[1]:
            prefix_ref[head, index] = sums[head]

    sums = [None] * group
    phase, waiting = phase_of(*tiles[0]), None
    for index, (head, start) in enumerate(tiles):
        following = phase_of(*tiles[index + 1]) if index + 1 < len(tiles) else None
        cosine, sine = cos_sin(phase, amplitude)
        features = jnp.concatenate([cosine.astype(BF16), sine.astype(BF16)], axis=0)
        feat_ref[head, :, start : start + TILE] = features
        if waiting is not None:
            add_state(*waiting)
        phase, waiting = following, (head, start, features)
    add_state(*waiting)
    sums = [total.astype(BF16) for total in sums]
    half = pl.num_programs(0) // 2

    @pl.when(pl.program_id(0) < half)
    def _():
        for head in range(group):
            sent_ref[head] = sums[head]

    @pl.when(pl.program_id(0) >= half)
    def _():
        for head in range(group):
            kept_ref[head] = sums[head]


def key_side(core, place, turn, key_rows, value_rows, frequencies, weight=None):
    rows = key_rows.shape[0]
    heads, width, count = frequencies.shape
    prior = max(1, rows // min(SPAN, rows) - 1)
    half = heads // 2
    group = 2 if half % 2 == 0 else 1
    steps, half_steps = heads // group, half // group

    def block(g, c):
        return (g + half_steps * (1 - c[0])) % steps

    in_specs = [
        pl.BlockSpec((rows, group * width), lambda g, c, p, t: (0, block(g, c))),
        pl.BlockSpec((rows, group * width), lambda g, c, p, t: (0, block(g, c))),
        pl.BlockSpec((group, width, count), lambda g, c, p, t: (block(g, c), 0, 0)),
    ]
    out_specs = [
        pl.BlockSpec((group, 2 * count, rows), lambda g, c, p, t: (block(g, c), 0, 0)),
        pl.BlockSpec((group, 2 * count, width), lambda g, c, p, t: (jnp.minimum(g, half_steps - 1), 0, 0)),
        pl.BlockSpec((group, 2 * count, width), lambda g, c, p, t: (jnp.maximum(g - half_steps, 0), 0, 0)),
        pl.BlockSpec((group, prior, 2 * count, width), lambda g, c, p, t: (block(g, c), 0, 0, 0)),
    ]
    out_shape = [
        jax.ShapeDtypeStruct((heads, 2 * count, rows), BF16),
        jax.ShapeDtypeStruct((half, 2 * count, width), BF16),
        jax.ShapeDtypeStruct((half, 2 * count, width), BF16),
        jax.ShapeDtypeStruct((heads, prior, 2 * count, width), F32),
    ]
    operands = [key_rows, value_rows, frequencies]
    if weight is not None:
        depth, cols = weight.shape[0] // 4, weight.shape[1]
        piece = depth // 2 // steps

        def rows_of(g, c, p, t):
            return ((p[0] ^ (1 + 2 * c[0])) * 2 + t[0]) * steps + g, 0

        in_specs.append(pl.BlockSpec((piece, cols), rows_of))
        out_specs.append(pl.BlockSpec((piece, cols), lambda g, c, p, t: (g, 0)))
        out_shape.append(jax.ShapeDtypeStruct((depth // 2, cols), weight.dtype))
        operands.append(weight)
    return pl.pallas_call(
        functools.partial(key_kernel, weight is not None),
        grid_spec=pltpu.PrefetchScalarGridSpec(
            num_scalar_prefetch=3, grid=(steps,), in_specs=in_specs, out_specs=out_specs
        ),
        out_shape=out_shape,
        compiler_params=LARGE,
        cost_estimate=FREE,
        name="key_side",
    )(core, place, turn, *operands)


def query_kernel(query_ref, value_ref, freq_ref, key_feat_ref, feat_ref, local_ref):
    rows = query_ref.shape[0]
    group, width, count = freq_ref.shape
    span = min(SPAN, rows)
    amplitude = 1.0 / math.sqrt(count)
    below = lax.broadcasted_iota(jnp.int32, (TILE, TILE), 0)
    causal = below >= lax.broadcasted_iota(jnp.int32, (TILE, TILE), 1)
    tiles = [(head, start) for head in range(group) for start in range(0, rows, TILE)]

    def phase_of(head, start):
        lanes = slice(head * width, (head + 1) * width)
        return dot(query_ref[start : start + TILE, lanes], freq_ref[head], (1, 0))

    def attend(head, start, features):
        lanes = slice(head * width, (head + 1) * width)
        total = None
        for other in range(start // span * span, start + TILE, TILE):
            theirs = slice(other, other + TILE)
            scores = dot(features, key_feat_ref[head, :, theirs], (1, 0))
            if other == start:
                scores = jnp.where(causal, scores, F32(0.0))
            part = dot(scores.astype(BF16), value_ref[theirs, lanes], (1, 0))
            total = part if total is None else total + part
        local_ref[start : start + TILE, lanes] = total.astype(local_ref.dtype)

    phase, waiting = phase_of(*tiles[0]), None
    for index, (head, start) in enumerate(tiles):
        following = phase_of(*tiles[index + 1]) if index + 1 < len(tiles) else None
        cosine, sine = cos_sin(phase, amplitude)
        features = jnp.concatenate([cosine.astype(BF16), sine.astype(BF16)], axis=1)
        feat_ref[head, start : start + TILE, :] = features
        if waiting is not None:
            attend(*waiting)
        phase, waiting = following, (head, start, features)
    attend(*waiting)


def query_side(query_rows, value_rows, frequencies, key_feat):
    rows = query_rows.shape[0]
    heads, width, count = frequencies.shape
    group = 2 if heads % 2 == 0 else 1
    return pl.pallas_call(
        query_kernel,
        grid=(heads // group,),
        in_specs=[
            pl.BlockSpec((rows, group * width), lambda h: (0, h)),
            pl.BlockSpec((rows, group * width), lambda h: (0, h)),
            pl.BlockSpec((group, width, count), lambda h: (h, 0, 0)),
            pl.BlockSpec((group, 2 * count, rows), lambda h: (h, 0, 0)),
        ],
        out_specs=[
            pl.BlockSpec((group, rows, 2 * count), lambda h: (h, 0, 0)),
            pl.BlockSpec((rows, group * width), lambda h: (0, h)),
        ],
        out_shape=[
            jax.ShapeDtypeStruct((heads, rows, 2 * count), BF16),
            jax.ShapeDtypeStruct((rows, heads * width), BF16),
        ],
        compiler_params=LARGE,
        cost_estimate=FREE,
        name="query_side",
    )(query_rows, value_rows, frequencies, key_feat)


def finish_kernel(
    heads, span, cuts, core_ref, feat_ref, local_ref, theirs_ref, mine_ref, gain_ref, *refs
):
    prefix_ref, out_refs = refs[0], refs[-len(cuts) :]
    width = local_ref.shape[1] // heads
    steps = pl.num_programs(0)
    kept = pl.program_id(0) >= steps // 2
    first_head = lax.rem(pl.program_id(0) + steps // 2 * (1 - core_ref[0]), steps) * heads
    gains = gain_ref[...].astype(F32)
    row = lax.broadcasted_iota(jnp.int32, gains.shape, 0)
    for head in range(heads):
        cols = slice(head * width, (head + 1) * width)
        gain = jnp.sum(jnp.where(row == first_head + head, gains, F32(0.0)), axis=0, keepdims=True)
        before = jnp.where(kept, mine_ref[head].astype(F32), theirs_ref[head].astype(F32))
        for out_ref, (first, last) in zip(out_refs, cuts):
            starts = [first, *range(first - first % TILE + TILE, last, TILE)]
            for start, stop in zip(starts, starts[1:] + [last]):
                mine = slice(start, stop)
                carried = before
                if start // span:
                    carried = carried + prefix_ref[head, start // span - 1]
                prior = dot(feat_ref[head, mine, :], carried.astype(BF16), (1, 0))
                attended = local_ref[mine, cols].astype(F32) + prior
                square = jnp.mean(attended * attended, axis=-1, keepdims=True)
                normed = attended * lax.rsqrt(square + F32(1e-6)) * gain
                out_ref[start - first : stop - first, cols] = normed.astype(BF16)


def finish(core, feat, local_part, theirs, mine, gain, prefix, cuts):
    heads, all_rows, feats = feat.shape
    rows = cuts[-1][1]
    span = min(SPAN, all_rows)
    width = local_part.shape[1] // heads
    prior = prefix.shape[1]
    half = heads // 2
    group = 4 if half % 4 == 0 and rows < span else 2 if half % 2 == 0 else 1
    steps, half_steps = heads // group, half // group

    def block(g, c):
        return (g + half_steps * (1 - c[0])) % steps

    in_specs = [
        pl.BlockSpec((group, rows, feats), lambda g, c: (block(g, c), 0, 0)),
        pl.BlockSpec((rows, group * width), lambda g, c: (0, block(g, c))),
        pl.BlockSpec((group, feats, width), lambda g, c: (jnp.minimum(g, half_steps - 1), 0, 0)),
        pl.BlockSpec((group, feats, width), lambda g, c: (jnp.maximum(g - half_steps, 0), 0, 0)),
        pl.BlockSpec(gain.shape, lambda g, c: (0, 0)),
    ]
    operands = [feat, local_part, theirs, mine, gain]
    if rows > span:
        in_specs.append(pl.BlockSpec((group, prior, feats, width), lambda g, c: (block(g, c), 0, 0, 0)))
        operands.append(prefix)
    return pl.pallas_call(
        functools.partial(finish_kernel, group, span, cuts),
        grid_spec=pltpu.PrefetchScalarGridSpec(
            num_scalar_prefetch=1,
            grid=(steps,),
            in_specs=in_specs,
            out_specs=[
                pl.BlockSpec((last - first, group * width), lambda g, c: (0, block(g, c))) for first, last in cuts
            ],
        ),
        out_shape=[jax.ShapeDtypeStruct((last - first, heads * width), BF16) for first, last in cuts],
        compiler_params=LARGE,
        cost_estimate=FREE,
        name="finish",
    )(core, *operands)


def project_kernel(sources, place_ref, *refs):
    out_ref = refs[-1]
    total = None
    for x_ref, w_ref in zip(refs[:sources], refs[sources : 2 * sources]):
        part = dot(x_ref[...], w_ref[...], (1, 0))
        total = part if total is None else total + part
    out_ref[...] = total.astype(out_ref.dtype)


def project(blocks, weight, place, hops, dtype=BF16):
    size, depth = blocks[0].shape
    cols = weight.shape[1]
    step = min(256, cols)

    def rows_of(source):
        return lambda n, p: (p[0] ^ hops[source], n)

    sources = len(blocks)
    return pl.pallas_call(
        functools.partial(project_kernel, sources),
        grid_spec=pltpu.PrefetchScalarGridSpec(
            num_scalar_prefetch=1,
            grid=(cols // step,),
            in_specs=[pl.BlockSpec((size, depth), lambda n, p: (0, 0)) for _ in blocks]
            + [pl.BlockSpec((depth, step), rows_of(source)) for source in range(sources)],
            out_specs=pl.BlockSpec((size, step), lambda n, p: (0, n)),
        ),
        out_shape=jax.ShapeDtypeStruct((size, cols), dtype),
        compiler_params=SMALL,
        cost_estimate=FREE,
        name="project",
    )(place, *blocks, *[weight] * sources)


def partial_kernel(core_ref, turn_ref, x_ref, y_ref, *refs):
    weights, out_ref = refs[:-1], refs[-1]
    count = len(weights) // 2
    swapped, turned = core_ref[0] != 0, turn_ref[0] != 0
    x, y = x_ref[...], y_ref[...]
    half = x.shape[1] // 2
    total = None
    for rows, pieces in ((jnp.where(swapped, y, x), weights[:count]), (jnp.where(swapped, x, y), weights[count:])):
        left, right = rows[:, :half], rows[:, half:]
        sides = [jnp.where(turned, right, left), jnp.where(turned, left, right)]
        rows = jnp.concatenate(sides, axis=1)
        first = 0
        for piece in pieces:
            last = first + piece.shape[0]
            part = dot(rows[:, first:last], piece[...], (1, 0))
            total = part if total is None else total + part
            first = last
    out_ref[...] = total.astype(out_ref.dtype)


def partial_product(core, turn, blocks, weights):
    size, depth = blocks[0].shape
    cols = weights[0].shape[1]
    step = min(256, cols)
    return pl.pallas_call(
        partial_kernel,
        grid_spec=pltpu.PrefetchScalarGridSpec(
            num_scalar_prefetch=2,
            grid=(cols // step,),
            in_specs=[pl.BlockSpec((size, depth), lambda n, c, t: (0, 0)) for _ in blocks]
            + [pl.BlockSpec((weight.shape[0], step), lambda n, c, t: (0, n)) for weight in weights],
            out_specs=pl.BlockSpec((size, step), lambda n, c, t: (0, n)),
        ),
        out_shape=jax.ShapeDtypeStruct((size, cols), BF16),
        compiler_params=SMALL,
        cost_estimate=FREE,
        name="partial_product",
    )(core, turn, *blocks, *weights)


def join_kernel(a_ref, b_ref, *refs):
    out_ref = refs[-1]
    out_ref[...] = (a_ref[...] + b_ref[...].astype(F32)).astype(out_ref.dtype)


def join(a, b, first, rows, into=None):
    size, cols = a.shape
    step = math.gcd(first, size, 256)
    index = first // step
    spec = pl.BlockSpec((step, cols), lambda r: (r, 0))
    return pl.pallas_call(
        join_kernel,
        grid=(size // step,),
        in_specs=[spec, spec] + [pl.BlockSpec(memory_space=pl.ANY)] * (into is not None),
        out_specs=pl.BlockSpec((step, cols), lambda r: (index + r, 0)),
        out_shape=jax.ShapeDtypeStruct((rows, cols), BF16),
        input_output_aliases={} if into is None else {2: 0},
        compiler_params=SMALL,
        cost_estimate=FREE,
        name="join",
    )(a, b, *([] if into is None else [into]))


def after(value, *others):
    return lax.optimization_barrier((value, *others))[0]


def swap(value, axis, distance):
    return lax.ppermute(value, axis, [(i, i ^ distance) for i in range(lax.axis_size(axis))])


def earlier_states(sent, kept, meanwhile):
    count, mine = lax.axis_size("ctx"), lax.axis_index("ctx")
    core = mine % 2
    partner = swap(sent, "ctx", 1)
    total = (kept.astype(F32) + partner.astype(F32)).astype(BF16)
    earlier = jnp.zeros(kept.shape, F32)
    beside = meanwhile(total)
    distance = 2
    while distance < count:
        radix = min(4, count // distance)
        last = distance * radix >= count
        added = total.astype(F32)
        for step in range(1, radix):
            hop = step * distance
            pairs = [(i, i ^ hop) for i in range(count) if not last or i < i ^ hop]
            theirs = lax.ppermute(total, "ctx", pairs)
            if last:
                theirs = after(theirs, *beside)
            theirs = theirs.astype(F32)
            lower = (mine ^ hop) < mine
            earlier = earlier + jnp.where(lower, theirs, F32(0.0))
            added = added + theirs
        total = added.astype(BF16)
        distance *= radix
    own = earlier + jnp.where(core == 1, partner.astype(F32), F32(0.0))
    given = earlier + jnp.where(core == 0, kept.astype(F32), F32(0.0))
    return swap(given.astype(BF16), "ctx", 1), own.astype(BF16), beside


def normed_output(core, place, turn, query_rows, key_rows, value_rows, frequencies, norm_gain, weight=None):
    key_feat, sent, kept, prefix, *share = key_side(core, place, turn, key_rows, value_rows, frequencies, weight)

    gain = norm_gain.reshape(frequencies.shape[0], -1)

    def meanwhile(total):
        return query_side(query_rows, value_rows, after(frequencies, total), key_feat)

    theirs, own, (query_feat, local_part) = earlier_states(sent, kept, meanwhile)

    def blocks_of(cuts, *others):
        return finish(core, after(query_feat, *others), local_part, theirs, own, gain, prefix, cuts)

    return blocks_of, share


def positions():
    spot, place = lax.axis_index("ctx"), lax.axis_index("head")
    return [value.astype(jnp.int32).reshape(1) for value in (spot % 2, place, (spot // 2 + spot // 4) % 2)]


def line_of_four(query_rows, key_rows, value_rows, frequencies, norm_gain, out_weight):
    rows = query_rows.shape[0]
    core, place, turn = positions()
    sizes = [rows * part // 16 for part in (2,) * 8]
    edges = [sum(sizes[:i]) for i in range(len(sizes) + 1)]
    cuts = tuple(zip(edges[:-1], edges[1:]))
    parts = (query_rows, key_rows, value_rows, frequencies, norm_gain)
    blocks_of, (share,) = normed_output(core, place, turn, *parts, out_weight)
    blocks = blocks_of(cuts[:1])
    share = after(swap(share, "head", 1), *blocks)
    half = share.shape[0] // 2
    halves = [share[:half], share[half:]]
    blocks = [*blocks, *blocks_of(cuts[1:], *halves)]
    last = len(blocks) - 1
    pairs, given, partials, products = [], [], [], []
    weights = None
    for index, block in enumerate(blocks):
        if index > 2:
            block = after(block, given[index - 2], partials[index - 3], products[max(0, index - 3)])
        pairs.append([block, swap(block, "head", 2)])
        if index == 1:
            others = [swap(part, "ctx", hop) for part, hop in zip(halves, (2, 4))]
            shares = [after(share, blocks[-1], pairs[0][1])] + [after(other, pairs[0][1]) for other in others]
            weights = shares + [swap(part, "ctx", 1) for part in shares]
            x, y = pairs[0]
            given.append(partial_product(core, turn, [x, y], weights))
            x, y = pairs[1]
            given.append(partial_product(core, turn, [x, after(y, given[0])], weights))
        elif index > 1:
            x, y = pairs[-1]
            y = after(y, partials[max(0, index - 3)], given[-1])
            if index == last:
                y = after(y, *products)
            given.append(partial_product(core, turn, [x, y], weights))
        partials += [swap(part, "head", 1) for part in given[len(partials) :]]
        products.append(project(pairs[-1], out_weight, place, (0, 2), F32))
    out = None
    for product, partial, (first, _) in zip(products, partials, cuts):
        out = join(product, partial, first, rows, out)
    return out


def any_line(query_rows, key_rows, value_rows, frequencies, norm_gain, out_weight):
    core, place, turn = positions()
    parts = (query_rows, key_rows, value_rows, frequencies, norm_gain)
    blocks_of, _ = normed_output(core, place, turn, *parts)
    (normed,) = blocks_of(((0, query_rows.shape[0]),))
    gathered = lax.all_gather(normed, "head", axis=1, tiled=True)
    return jnp.dot(gathered, out_weight, preferred_element_type=F32).astype(BF16)


def solution(mesh):
    return jax.shard_map(
        line_of_four if mesh.shape["head"] == 4 and mesh.shape["ctx"] % 8 == 0 else any_line,
        mesh=mesh,
        in_specs=(
            P("ctx", "head"),
            P("ctx", "head"),
            P("ctx", "head"),
            P("head", None, None),
            P("head"),
            P(None, "head"),
        ),
        out_specs=P("ctx", "head"),
        check_vma=False,
    )
```

```python
import functools
import math

import jax
import jax.numpy as jnp
from jax import lax
from jax.experimental import pallas as pl
from jax.experimental.pallas import tpu as pltpu
from jax.sharding import PartitionSpec as P

F32 = jnp.float32
BF16 = jnp.bfloat16
SPAN = 512
TILE = 256
SIN_TERMS = (3.1415820220956054, -5.167142794166117, 2.5418990064386224, -0.5546361406826548)
COS_TERMS = (0.9999932955183647, -4.933938020185013, 4.0412838463445455, -1.2221270624224843)
ROUNDER = 1.5 * 2.0**23
LARGE = pltpu.CompilerParams(vmem_limit_bytes=56 << 20)
SMALL = pltpu.CompilerParams(vmem_limit_bytes=20 << 20)
FREE = pl.CostEstimate(flops=0, bytes_accessed=0, transcendentals=0)


def dot(a, b, contract):
    return lax.dot_general(a, b, ((contract[:1], contract[1:]), ((), ())), preferred_element_type=F32)


def poly(terms, scale, u):
    value = F32(terms[-1] * scale)
    for term in terms[-2::-1]:
        value = value * u + F32(term * scale)
    return value


def cos_sin(phase, amplitude):
    turns = phase * F32(1.0 / (2.0 * math.pi))
    part = turns - ((turns + F32(ROUNDER)) - F32(ROUNDER))
    u = part * part
    scale = math.sqrt(2.0 * amplitude)
    half_sin = poly(SIN_TERMS, scale, u) * part
    half_cos = poly(COS_TERMS, scale, u)
    return F32(amplitude) - half_sin * half_sin, half_sin * half_cos


def key_kernel(has_weight, core_ref, place_ref, turn_ref, key_ref, value_ref, freq_ref, *refs):
    if has_weight:
        refs[-1][...] = refs[0][...]
        refs = refs[1:]
    feat_ref, sent_ref, kept_ref, prefix_ref = refs[:4]
    rows = key_ref.shape[0]
    group, width, count = freq_ref.shape
    span = min(SPAN, rows)
    amplitude = 1.0 / math.sqrt(count)
    tiles = [(head, start) for head in range(group) for start in range(0, rows, TILE)]
    turned = [freq_ref[head].T for head in range(group)]

    def phase_of(head, start):
        lanes = slice(head * width, (head + 1) * width)
        return dot(turned[head], key_ref[start : start + TILE, lanes], (1, 1))

    def add_state(head, start, features):
        lanes = slice(head * width, (head + 1) * width)
        state = dot(features, value_ref[start : start + TILE, lanes], (1, 0))
        sums[head] = state if start == 0 else sums[head] + state
        index = (start + TILE) // span - 1
        if (start + TILE) % span == 0 and index < prefix_ref.shape[1]:
            prefix_ref[head, index] = sums[head]

    sums = [None] * group
    phase, waiting = phase_of(*tiles[0]), None
    for index, (head, start) in enumerate(tiles):
        following = phase_of(*tiles[index + 1]) if index + 1 < len(tiles) else None
        cosine, sine = cos_sin(phase, amplitude)
        features = jnp.concatenate([cosine.astype(BF16), sine.astype(BF16)], axis=0)
        feat_ref[head, :, start : start + TILE] = features
        if waiting is not None:
            add_state(*waiting)
        phase, waiting = following, (head, start, features)
    add_state(*waiting)
    sums = [total.astype(BF16) for total in sums]
    half = pl.num_programs(0) // 2

    @pl.when(pl.program_id(0) < half)
    def _():
        for head in range(group):
            sent_ref[head] = sums[head]

    @pl.when(pl.program_id(0) >= half)
    def _():
        for head in range(group):
            kept_ref[head] = sums[head]


def key_side(core, place, turn, key_rows, value_rows, frequencies, weight=None):
    rows = key_rows.shape[0]
    heads, width, count = frequencies.shape
    prior = max(1, rows // min(SPAN, rows) - 1)
    half = heads // 2
    group = 2 if half % 2 == 0 else 1
    steps, half_steps = heads // group, half // group

    def block(g, c):
        return (g + half_steps * (1 - c[0])) % steps

    in_specs = [
        pl.BlockSpec((rows, group * width), lambda g, c, p, t: (0, block(g, c))),
        pl.BlockSpec((rows, group * width), lambda g, c, p, t: (0, block(g, c))),
        pl.BlockSpec((group, width, count), lambda g, c, p, t: (block(g, c), 0, 0)),
    ]
    out_specs = [
        pl.BlockSpec((group, 2 * count, rows), lambda g, c, p, t: (block(g, c), 0, 0)),
        pl.BlockSpec((group, 2 * count, width), lambda g, c, p, t: (jnp.minimum(g, half_steps - 1), 0, 0)),
        pl.BlockSpec((group, 2 * count, width), lambda g, c, p, t: (jnp.maximum(g - half_steps, 0), 0, 0)),
        pl.BlockSpec((group, prior, 2 * count, width), lambda g, c, p, t: (block(g, c), 0, 0, 0)),
    ]
    out_shape = [
        jax.ShapeDtypeStruct((heads, 2 * count, rows), BF16),
        jax.ShapeDtypeStruct((half, 2 * count, width), BF16),
        jax.ShapeDtypeStruct((half, 2 * count, width), BF16),
        jax.ShapeDtypeStruct((heads, prior, 2 * count, width), F32),
    ]
    operands = [key_rows, value_rows, frequencies]
    if weight is not None:
        depth, cols = weight.shape[0] // 4, weight.shape[1]
        piece = depth // 2 // steps

        def rows_of(g, c, p, t):
            return ((p[0] ^ (1 + 2 * c[0])) * 2 + t[0]) * steps + g, 0

        in_specs.append(pl.BlockSpec((piece, cols), rows_of))
        out_specs.append(pl.BlockSpec((piece, cols), lambda g, c, p, t: (g, 0)))
        out_shape.append(jax.ShapeDtypeStruct((depth // 2, cols), weight.dtype))
        operands.append(weight)
    return pl.pallas_call(
        functools.partial(key_kernel, weight is not None),
        grid_spec=pltpu.PrefetchScalarGridSpec(
            num_scalar_prefetch=3, grid=(steps,), in_specs=in_specs, out_specs=out_specs
        ),
        out_shape=out_shape,
        compiler_params=LARGE,
        cost_estimate=FREE,
        name="key_side",
    )(core, place, turn, *operands)


def query_kernel(query_ref, value_ref, freq_ref, key_feat_ref, feat_ref, local_ref):
    rows = query_ref.shape[0]
    group, width, count = freq_ref.shape
    span = min(SPAN, rows)
    amplitude = 1.0 / math.sqrt(count)
    below = lax.broadcasted_iota(jnp.int32, (TILE, TILE), 0)
    causal = below >= lax.broadcasted_iota(jnp.int32, (TILE, TILE), 1)
    tiles = [(head, start) for head in range(group) for start in range(0, rows, TILE)]

    def phase_of(head, start):
        lanes = slice(head * width, (head + 1) * width)
        return dot(query_ref[start : start + TILE, lanes], freq_ref[head], (1, 0))

    def attend(head, start, features):
        lanes = slice(head * width, (head + 1) * width)
        total = None
        for other in range(start // span * span, start + TILE, TILE):
            theirs = slice(other, other + TILE)
            scores = dot(features, key_feat_ref[head, :, theirs], (1, 0))
            if other == start:
                scores = jnp.where(causal, scores, F32(0.0))
            part = dot(scores.astype(BF16), value_ref[theirs, lanes], (1, 0))
            total = part if total is None else total + part
        local_ref[start : start + TILE, lanes] = total.astype(local_ref.dtype)

    phase, waiting = phase_of(*tiles[0]), None
    for index, (head, start) in enumerate(tiles):
        following = phase_of(*tiles[index + 1]) if index + 1 < len(tiles) else None
        cosine, sine = cos_sin(phase, amplitude)
        features = jnp.concatenate([cosine.astype(BF16), sine.astype(BF16)], axis=1)
        feat_ref[head, start : start + TILE, :] = features
        if waiting is not None:
            attend(*waiting)
        phase, waiting = following, (head, start, features)
    attend(*waiting)


def query_side(query_rows, value_rows, frequencies, key_feat):
    rows = query_rows.shape[0]
    heads, width, count = frequencies.shape
    group = 2 if heads % 2 == 0 else 1
    return pl.pallas_call(
        query_kernel,
        grid=(heads // group,),
        in_specs=[
            pl.BlockSpec((rows, group * width), lambda h: (0, h)),
            pl.BlockSpec((rows, group * width), lambda h: (0, h)),
            pl.BlockSpec((group, width, count), lambda h: (h, 0, 0)),
            pl.BlockSpec((group, 2 * count, rows), lambda h: (h, 0, 0)),
        ],
        out_specs=[
            pl.BlockSpec((group, rows, 2 * count), lambda h: (h, 0, 0)),
            pl.BlockSpec((rows, group * width), lambda h: (0, h)),
        ],
        out_shape=[
            jax.ShapeDtypeStruct((heads, rows, 2 * count), BF16),
            jax.ShapeDtypeStruct((rows, heads * width), BF16),
        ],
        compiler_params=LARGE,
        cost_estimate=FREE,
        name="query_side",
    )(query_rows, value_rows, frequencies, key_feat)


def finish_kernel(
    heads, span, cuts, core_ref, feat_ref, local_ref, theirs_ref, mine_ref, gain_ref, *refs
):
    prefix_ref, out_refs = refs[0], refs[-len(cuts) :]
    width = local_ref.shape[1] // heads
    steps = pl.num_programs(0)
    kept = pl.program_id(0) >= steps // 2
    first_head = lax.rem(pl.program_id(0) + steps // 2 * (1 - core_ref[0]), steps) * heads
    gains = gain_ref[...].astype(F32)
    row = lax.broadcasted_iota(jnp.int32, gains.shape, 0)
    for head in range(heads):
        cols = slice(head * width, (head + 1) * width)
        gain = jnp.sum(jnp.where(row == first_head + head, gains, F32(0.0)), axis=0, keepdims=True)
        before = jnp.where(kept, mine_ref[head].astype(F32), theirs_ref[head].astype(F32))
        for out_ref, (first, last) in zip(out_refs, cuts):
            starts = [first, *range(first - first % TILE + TILE, last, TILE)]
            for start, stop in zip(starts, starts[1:] + [last]):
                mine = slice(start, stop)
                carried = before
                if start // span:
                    carried = carried + prefix_ref[head, start // span - 1]
                prior = dot(feat_ref[head, mine, :], carried.astype(BF16), (1, 0))
                attended = local_ref[mine, cols].astype(F32) + prior
                square = jnp.mean(attended * attended, axis=-1, keepdims=True)
                normed = attended * lax.rsqrt(square + F32(1e-6)) * gain
                out_ref[start - first : stop - first, cols] = normed.astype(BF16)


def finish(core, feat, local_part, theirs, mine, gain, prefix, cuts):
    heads, all_rows, feats = feat.shape
    rows = cuts[-1][1]
    span = min(SPAN, all_rows)
    width = local_part.shape[1] // heads
    prior = prefix.shape[1]
    half = heads // 2
    group = 4 if half % 4 == 0 and rows < span else 2 if half % 2 == 0 else 1
    steps, half_steps = heads // group, half // group

    def block(g, c):
        return (g + half_steps * (1 - c[0])) % steps

    in_specs = [
        pl.BlockSpec((group, rows, feats), lambda g, c: (block(g, c), 0, 0)),
        pl.BlockSpec((rows, group * width), lambda g, c: (0, block(g, c))),
        pl.BlockSpec((group, feats, width), lambda g, c: (jnp.minimum(g, half_steps - 1), 0, 0)),
        pl.BlockSpec((group, feats, width), lambda g, c: (jnp.maximum(g - half_steps, 0), 0, 0)),
        pl.BlockSpec(gain.shape, lambda g, c: (0, 0)),
    ]
    operands = [feat, local_part, theirs, mine, gain]
    if rows > span:
        in_specs.append(pl.BlockSpec((group, prior, feats, width), lambda g, c: (block(g, c), 0, 0, 0)))
        operands.append(prefix)
    return pl.pallas_call(
        functools.partial(finish_kernel, group, span, cuts),
        grid_spec=pltpu.PrefetchScalarGridSpec(
            num_scalar_prefetch=1,
            grid=(steps,),
            in_specs=in_specs,
            out_specs=[
                pl.BlockSpec((last - first, group * width), lambda g, c: (0, block(g, c))) for first, last in cuts
            ],
        ),
        out_shape=[jax.ShapeDtypeStruct((last - first, heads * width), BF16) for first, last in cuts],
        compiler_params=LARGE,
        cost_estimate=FREE,
        name="finish",
    )(core, *operands)


def project_kernel(sources, place_ref, *refs):
    out_ref = refs[-1]
    total = None
    for x_ref, w_ref in zip(refs[:sources], refs[sources : 2 * sources]):
        part = dot(x_ref[...], w_ref[...], (1, 0))
        total = part if total is None else total + part
    out_ref[...] = total.astype(out_ref.dtype)


def project(blocks, weight, place, hops, dtype=BF16):
    size, depth = blocks[0].shape
    cols = weight.shape[1]
    step = min(256, cols)

    def rows_of(source):
        return lambda n, p: (p[0] ^ hops[source], n)

    sources = len(blocks)
    return pl.pallas_call(
        functools.partial(project_kernel, sources),
        grid_spec=pltpu.PrefetchScalarGridSpec(
            num_scalar_prefetch=1,
            grid=(cols // step,),
            in_specs=[pl.BlockSpec((size, depth), lambda n, p: (0, 0)) for _ in blocks]
            + [pl.BlockSpec((depth, step), rows_of(source)) for source in range(sources)],
            out_specs=pl.BlockSpec((size, step), lambda n, p: (0, n)),
        ),
        out_shape=jax.ShapeDtypeStruct((size, cols), dtype),
        compiler_params=SMALL,
        cost_estimate=FREE,
        name="project",
    )(place, *blocks, *[weight] * sources)


def partial_kernel(core_ref, turn_ref, x_ref, y_ref, *refs):
    weights, out_ref = refs[:-1], refs[-1]
    count = len(weights) // 2
    swapped, turned = core_ref[0] != 0, turn_ref[0] != 0
    x, y = x_ref[...], y_ref[...]
    half = x.shape[1] // 2
    total = None
    for rows, pieces in ((jnp.where(swapped, y, x), weights[:count]), (jnp.where(swapped, x, y), weights[count:])):
        left, right = rows[:, :half], rows[:, half:]
        sides = [jnp.where(turned, right, left), jnp.where(turned, left, right)]
        rows = jnp.concatenate(sides, axis=1)
        first = 0
        for piece in pieces:
            last = first + piece.shape[0]
            part = dot(rows[:, first:last], piece[...], (1, 0))
            total = part if total is None else total + part
            first = last
    out_ref[...] = total.astype(out_ref.dtype)


def partial_product(core, turn, blocks, weights):
    size, depth = blocks[0].shape
    cols = weights[0].shape[1]
    step = min(256, cols)
    return pl.pallas_call(
        partial_kernel,
        grid_spec=pltpu.PrefetchScalarGridSpec(
            num_scalar_prefetch=2,
            grid=(cols // step,),
            in_specs=[pl.BlockSpec((size, depth), lambda n, c, t: (0, 0)) for _ in blocks]
            + [pl.BlockSpec((weight.shape[0], step), lambda n, c, t: (0, n)) for weight in weights],
            out_specs=pl.BlockSpec((size, step), lambda n, c, t: (0, n)),
        ),
        out_shape=jax.ShapeDtypeStruct((size, cols), BF16),
        compiler_params=SMALL,
        cost_estimate=FREE,
        name="partial_product",
    )(core, turn, *blocks, *weights)


def join_kernel(a_ref, b_ref, *refs):
    out_ref = refs[-1]
    out_ref[...] = (a_ref[...] + b_ref[...].astype(F32)).astype(out_ref.dtype)


def join(a, b, first, rows, into=None):
    size, cols = a.shape
    step = math.gcd(first, size, 256)
    index = first // step
    spec = pl.BlockSpec((step, cols), lambda r: (r, 0))
    return pl.pallas_call(
        join_kernel,
        grid=(size // step,),
        in_specs=[spec, spec] + [pl.BlockSpec(memory_space=pl.ANY)] * (into is not None),
        out_specs=pl.BlockSpec((step, cols), lambda r: (index + r, 0)),
        out_shape=jax.ShapeDtypeStruct((rows, cols), BF16),
        input_output_aliases={} if into is None else {2: 0},
        compiler_params=SMALL,
        cost_estimate=FREE,
        name="join",
    )(a, b, *([] if into is None else [into]))


def after(value, *others):
    return lax.optimization_barrier((value, *others))[0]


def swap(value, axis, distance):
    return lax.ppermute(value, axis, [(i, i ^ distance) for i in range(lax.axis_size(axis))])


def earlier_states(sent, kept, meanwhile):
    count, mine = lax.axis_size("ctx"), lax.axis_index("ctx")
    core = mine % 2
    partner = swap(sent, "ctx", 1)
    total = (kept.astype(F32) + partner.astype(F32)).astype(BF16)
    earlier = jnp.zeros(kept.shape, F32)
    beside = meanwhile(total)
    distance = 2
    while distance < count:
        radix = min(4, count // distance)
        last = distance * radix >= count
        added = total.astype(F32)
        for step in range(1, radix):
            hop = step * distance
            pairs = [(i, i ^ hop) for i in range(count) if not last or i < i ^ hop]
            theirs = lax.ppermute(total, "ctx", pairs)
            if last:
                theirs = after(theirs, *beside)
            theirs = theirs.astype(F32)
            lower = (mine ^ hop) < mine
            earlier = earlier + jnp.where(lower, theirs, F32(0.0))
            added = added + theirs
        total = added.astype(BF16)
        distance *= radix
    own = earlier + jnp.where(core == 1, partner.astype(F32), F32(0.0))
    given = earlier + jnp.where(core == 0, kept.astype(F32), F32(0.0))
    return swap(given.astype(BF16), "ctx", 1), own.astype(BF16), beside


def normed_output(core, place, turn, query_rows, key_rows, value_rows, frequencies, norm_gain, weight=None):
    key_feat, sent, kept, prefix, *share = key_side(core, place, turn, key_rows, value_rows, frequencies, weight)

    gain = norm_gain.reshape(frequencies.shape[0], -1)

    def meanwhile(total):
        return query_side(query_rows, value_rows, after(frequencies, total), key_feat)

    theirs, own, (query_feat, local_part) = earlier_states(sent, kept, meanwhile)

    def blocks_of(cuts, *others):
        return finish(core, after(query_feat, *others), local_part, theirs, own, gain, prefix, cuts)

    return blocks_of, share


def positions():
    spot, place = lax.axis_index("ctx"), lax.axis_index("head")
    return [value.astype(jnp.int32).reshape(1) for value in (spot % 2, place, (spot // 2 + spot // 4) % 2)]


def line_of_four(query_rows, key_rows, value_rows, frequencies, norm_gain, out_weight):
    rows = query_rows.shape[0]
    core, place, turn = positions()
    sizes = [rows * part // 16 for part in (2, 2, 2, 2, 2, 3, 2, 1)]
    edges = [sum(sizes[:i]) for i in range(len(sizes) + 1)]
    cuts = tuple(zip(edges[:-1], edges[1:]))
    parts = (query_rows, key_rows, value_rows, frequencies, norm_gain)
    blocks_of, (share,) = normed_output(core, place, turn, *parts, out_weight)
    blocks = blocks_of(cuts[:1])
    share = after(swap(share, "head", 1), *blocks)
    half = share.shape[0] // 2
    halves = [share[:half], share[half:]]
    blocks = [*blocks, *blocks_of(cuts[1:], *halves)]
    pairs, given, partials, products = [], [], [], []
    out, joined = None, 0
    for index, block in enumerate(blocks):
        if index > 2:
            block = after(block, given[index - 2], partials[index - 3], products[max(0, index - 3)])
        if index >= 4:
            out = join(products[joined], partials[joined], cuts[joined][0], rows, out)
            joined += 1
            block, out = lax.optimization_barrier((block, out))
        pairs.append([block, swap(block, "head", 2)])
        if index == 1:
            others = [swap(part, "ctx", hop) for part, hop in zip(halves, (2, 4))]
            shares = [after(share, blocks[-1], pairs[0][1])] + [after(other, pairs[0][1]) for other in others]
            weights = shares + [swap(part, "ctx", 1) for part in shares]
            x, y = pairs[0]
            given.append(partial_product(core, turn, [x, y], weights))
            x, y = pairs[1]
            given.append(partial_product(core, turn, [x, after(y, given[0])], weights))
        elif index > 1:
            x, y = pairs[-1]
            y = after(y, partials[max(0, index - 3)], given[-1], *products[: max(0, index - 1)])
            given.append(partial_product(core, turn, [x, y], weights))
        partials += [swap(part, "head", 1) for part in given[len(partials) :]]
        products.append(project(pairs[-1], out_weight, place, (0, 2), F32))
    for product, partial, (first, _) in list(zip(products, partials, cuts))[joined:]:
        out = join(product, partial, first, rows, out)
    return out


def any_line(query_rows, key_rows, value_rows, frequencies, norm_gain, out_weight):
    core, place, turn = positions()
    parts = (query_rows, key_rows, value_rows, frequencies, norm_gain)
    blocks_of, _ = normed_output(core, place, turn, *parts)
    (normed,) = blocks_of(((0, query_rows.shape[0]),))
    gathered = lax.all_gather(normed, "head", axis=1, tiled=True)
    return jnp.dot(gathered, out_weight, preferred_element_type=F32).astype(BF16)


def solution(mesh):
    return jax.shard_map(
        line_of_four if mesh.shape["head"] == 4 and mesh.shape["ctx"] % 8 == 0 else any_line,
        mesh=mesh,
        in_specs=(
            P("ctx", "head"),
            P("ctx", "head"),
            P("ctx", "head"),
            P("head", None, None),
            P("head"),
            P(None, "head"),
        ),
        out_specs=P("ctx", "head"),
        check_vma=False,
    )
```

```python
import functools
import math

import jax
import jax.numpy as jnp
from jax import lax
from jax.experimental import pallas as pl
from jax.experimental.pallas import tpu as pltpu
from jax.sharding import PartitionSpec as P

F32 = jnp.float32
BF16 = jnp.bfloat16
SPAN = 512
TILE = 256
SIN_TERMS = (3.1406400334639137, -5.136905232797424, 2.2995469238543222)
COS_TERMS = (0.9999932955183647, -4.933938020185013, 4.0412838463445455, -1.2221270624224843)
ROUNDER = 1.5 * 2.0**23
LARGE = pltpu.CompilerParams(vmem_limit_bytes=56 << 20)
SMALL = pltpu.CompilerParams(vmem_limit_bytes=20 << 20)
FREE = pl.CostEstimate(flops=0, bytes_accessed=0, transcendentals=0)


def dot(a, b, contract):
    return lax.dot_general(a, b, ((contract[:1], contract[1:]), ((), ())), preferred_element_type=F32)


def poly(terms, scale, u):
    value = F32(terms[-1] * scale)
    for term in terms[-2::-1]:
        value = value * u + F32(term * scale)
    return value


def cos_sin(phase, amplitude):
    turns = phase * F32(1.0 / (2.0 * math.pi))
    part = turns - ((turns + F32(ROUNDER)) - F32(ROUNDER))
    u = part * part
    scale = math.sqrt(2.0 * amplitude)
    half_sin = poly(SIN_TERMS, scale, u) * part
    half_cos = poly(COS_TERMS, scale, u)
    return F32(amplitude) - half_sin * half_sin, half_sin * half_cos


def key_kernel(has_weight, core_ref, place_ref, turn_ref, key_ref, value_ref, freq_ref, *refs):
    if has_weight:
        refs[-1][...] = refs[0][...]
        refs = refs[1:]
    feat_ref, sent_ref, kept_ref, prefix_ref = refs[:4]
    rows = key_ref.shape[0]
    group, width, count = freq_ref.shape
    span = min(SPAN, rows)
    amplitude = 1.0 / math.sqrt(count)
    tiles = [(head, start) for head in range(group) for start in range(0, rows, TILE)]
    turned = [freq_ref[head].T for head in range(group)]

    def phase_of(head, start):
        lanes = slice(head * width, (head + 1) * width)
        return dot(turned[head], key_ref[start : start + TILE, lanes], (1, 1))

    def add_state(head, start, features):
        lanes = slice(head * width, (head + 1) * width)
        state = dot(features, value_ref[start : start + TILE, lanes], (1, 0))
        sums[head] = state if start == 0 else sums[head] + state
        index = (start + TILE) // span - 1
        if (start + TILE) % span == 0 and index < prefix_ref.shape[1]:
            prefix_ref[head, index] = sums[head]

    sums = [None] * group
    phase, waiting = phase_of(*tiles[0]), None
    for index, (head, start) in enumerate(tiles):
        following = phase_of(*tiles[index + 1]) if index + 1 < len(tiles) else None
        cosine, sine = cos_sin(phase, amplitude)
        features = jnp.concatenate([cosine.astype(BF16), sine.astype(BF16)], axis=0)
        feat_ref[head, :, start : start + TILE] = features
        if waiting is not None:
            add_state(*waiting)
        phase, waiting = following, (head, start, features)
    add_state(*waiting)
    sums = [total.astype(BF16) for total in sums]
    half = pl.num_programs(0) // 2

    @pl.when(pl.program_id(0) < half)
    def _():
        for head in range(group):
            sent_ref[head] = sums[head]

    @pl.when(pl.program_id(0) >= half)
    def _():
        for head in range(group):
            kept_ref[head] = sums[head]


def key_side(core, place, turn, key_rows, value_rows, frequencies, weight=None):
    rows = key_rows.shape[0]
    heads, width, count = frequencies.shape
    prior = max(1, rows // min(SPAN, rows) - 1)
    half = heads // 2
    group = 2 if half % 2 == 0 else 1
    steps, half_steps = heads // group, half // group

    def block(g, c):
        return (g + half_steps * (1 - c[0])) % steps

    in_specs = [
        pl.BlockSpec((rows, group * width), lambda g, c, p, t: (0, block(g, c))),
        pl.BlockSpec((rows, group * width), lambda g, c, p, t: (0, block(g, c))),
        pl.BlockSpec((group, width, count), lambda g, c, p, t: (block(g, c), 0, 0)),
    ]
    out_specs = [
        pl.BlockSpec((group, 2 * count, rows), lambda g, c, p, t: (block(g, c), 0, 0)),
        pl.BlockSpec((group, 2 * count, width), lambda g, c, p, t: (jnp.minimum(g, half_steps - 1), 0, 0)),
        pl.BlockSpec((group, 2 * count, width), lambda g, c, p, t: (jnp.maximum(g - half_steps, 0), 0, 0)),
        pl.BlockSpec((group, prior, 2 * count, width), lambda g, c, p, t: (block(g, c), 0, 0, 0)),
    ]
    out_shape = [
        jax.ShapeDtypeStruct((heads, 2 * count, rows), BF16),
        jax.ShapeDtypeStruct((half, 2 * count, width), BF16),
        jax.ShapeDtypeStruct((half, 2 * count, width), BF16),
        jax.ShapeDtypeStruct((heads, prior, 2 * count, width), F32),
    ]
    operands = [key_rows, value_rows, frequencies]
    if weight is not None:
        depth, cols = weight.shape[0] // 4, weight.shape[1]
        piece = depth // 2 // steps

        def rows_of(g, c, p, t):
            return ((p[0] ^ (1 + 2 * c[0])) * 2 + t[0]) * steps + g, 0

        in_specs.append(pl.BlockSpec((piece, cols), rows_of))
        out_specs.append(pl.BlockSpec((piece, cols), lambda g, c, p, t: (g, 0)))
        out_shape.append(jax.ShapeDtypeStruct((depth // 2, cols), weight.dtype))
        operands.append(weight)
    return pl.pallas_call(
        functools.partial(key_kernel, weight is not None),
        grid_spec=pltpu.PrefetchScalarGridSpec(
            num_scalar_prefetch=3, grid=(steps,), in_specs=in_specs, out_specs=out_specs
        ),
        out_shape=out_shape,
        compiler_params=LARGE,
        cost_estimate=FREE,
        name="key_side",
    )(core, place, turn, *operands)


def query_kernel(query_ref, value_ref, freq_ref, key_feat_ref, feat_ref, local_ref):
    rows = query_ref.shape[0]
    group, width, count = freq_ref.shape
    span = min(SPAN, rows)
    amplitude = 1.0 / math.sqrt(count)
    below = lax.broadcasted_iota(jnp.int32, (TILE, TILE), 0)
    causal = below >= lax.broadcasted_iota(jnp.int32, (TILE, TILE), 1)
    tiles = [(head, start) for head in range(group) for start in range(0, rows, TILE)]

    def phase_of(head, start):
        lanes = slice(head * width, (head + 1) * width)
        return dot(query_ref[start : start + TILE, lanes], freq_ref[head], (1, 0))

    def attend(head, start, features):
        lanes = slice(head * width, (head + 1) * width)
        total = None
        for other in range(start // span * span, start + TILE, TILE):
            theirs = slice(other, other + TILE)
            scores = dot(features, key_feat_ref[head, :, theirs], (1, 0))
            if other == start:
                scores = jnp.where(causal, scores, F32(0.0))
            part = dot(scores.astype(BF16), value_ref[theirs, lanes], (1, 0))
            total = part if total is None else total + part
        local_ref[start : start + TILE, lanes] = total.astype(local_ref.dtype)

    phase, waiting = phase_of(*tiles[0]), None
    for index, (head, start) in enumerate(tiles):
        following = phase_of(*tiles[index + 1]) if index + 1 < len(tiles) else None
        cosine, sine = cos_sin(phase, amplitude)
        features = jnp.concatenate([cosine.astype(BF16), sine.astype(BF16)], axis=1)
        feat_ref[head, start : start + TILE, :] = features
        if waiting is not None:
            attend(*waiting)
        phase, waiting = following, (head, start, features)
    attend(*waiting)


def query_side(query_rows, value_rows, frequencies, key_feat):
    rows = query_rows.shape[0]
    heads, width, count = frequencies.shape
    group = 2 if heads % 2 == 0 else 1
    return pl.pallas_call(
        query_kernel,
        grid=(heads // group,),
        in_specs=[
            pl.BlockSpec((rows, group * width), lambda h: (0, h)),
            pl.BlockSpec((rows, group * width), lambda h: (0, h)),
            pl.BlockSpec((group, width, count), lambda h: (h, 0, 0)),
            pl.BlockSpec((group, 2 * count, rows), lambda h: (h, 0, 0)),
        ],
        out_specs=[
            pl.BlockSpec((group, rows, 2 * count), lambda h: (h, 0, 0)),
            pl.BlockSpec((rows, group * width), lambda h: (0, h)),
        ],
        out_shape=[
            jax.ShapeDtypeStruct((heads, rows, 2 * count), BF16),
            jax.ShapeDtypeStruct((rows, heads * width), BF16),
        ],
        compiler_params=LARGE,
        cost_estimate=FREE,
        name="query_side",
    )(query_rows, value_rows, frequencies, key_feat)


def finish_kernel(
    heads, span, cuts, core_ref, feat_ref, local_ref, theirs_ref, mine_ref, gain_ref, *refs
):
    prefix_ref, out_refs = refs[0], refs[-len(cuts) :]
    width = local_ref.shape[1] // heads
    steps = pl.num_programs(0)
    kept = pl.program_id(0) >= steps // 2
    first_head = lax.rem(pl.program_id(0) + steps // 2 * (1 - core_ref[0]), steps) * heads
    gains = gain_ref[...].astype(F32)
    row = lax.broadcasted_iota(jnp.int32, gains.shape, 0)
    for head in range(heads):
        cols = slice(head * width, (head + 1) * width)
        gain = jnp.sum(jnp.where(row == first_head + head, gains, F32(0.0)), axis=0, keepdims=True)
        before = jnp.where(kept, mine_ref[head].astype(F32), theirs_ref[head].astype(F32))
        for out_ref, (first, last) in zip(out_refs, cuts):
            starts = [first, *range(first - first % TILE + TILE, last, TILE)]
            for start, stop in zip(starts, starts[1:] + [last]):
                mine = slice(start, stop)
                carried = before
                if start // span:
                    carried = carried + prefix_ref[head, start // span - 1]
                prior = dot(feat_ref[head, mine, :], carried.astype(BF16), (1, 0))
                attended = local_ref[mine, cols].astype(F32) + prior
                square = jnp.mean(attended * attended, axis=-1, keepdims=True)
                normed = attended * lax.rsqrt(square + F32(1e-6)) * gain
                out_ref[start - first : stop - first, cols] = normed.astype(BF16)


def finish(core, feat, local_part, theirs, mine, gain, prefix, cuts):
    heads, all_rows, feats = feat.shape
    rows = cuts[-1][1]
    span = min(SPAN, all_rows)
    width = local_part.shape[1] // heads
    prior = prefix.shape[1]
    half = heads // 2
    group = 4 if half % 4 == 0 and rows < span else 2 if half % 2 == 0 else 1
    steps, half_steps = heads // group, half // group

    def block(g, c):
        return (g + half_steps * (1 - c[0])) % steps

    in_specs = [
        pl.BlockSpec((group, rows, feats), lambda g, c: (block(g, c), 0, 0)),
        pl.BlockSpec((rows, group * width), lambda g, c: (0, block(g, c))),
        pl.BlockSpec((group, feats, width), lambda g, c: (jnp.minimum(g, half_steps - 1), 0, 0)),
        pl.BlockSpec((group, feats, width), lambda g, c: (jnp.maximum(g - half_steps, 0), 0, 0)),
        pl.BlockSpec(gain.shape, lambda g, c: (0, 0)),
    ]
    operands = [feat, local_part, theirs, mine, gain]
    if rows > span:
        in_specs.append(pl.BlockSpec((group, prior, feats, width), lambda g, c: (block(g, c), 0, 0, 0)))
        operands.append(prefix)
    return pl.pallas_call(
        functools.partial(finish_kernel, group, span, cuts),
        grid_spec=pltpu.PrefetchScalarGridSpec(
            num_scalar_prefetch=1,
            grid=(steps,),
            in_specs=in_specs,
            out_specs=[
                pl.BlockSpec((last - first, group * width), lambda g, c: (0, block(g, c))) for first, last in cuts
            ],
        ),
        out_shape=[jax.ShapeDtypeStruct((last - first, heads * width), BF16) for first, last in cuts],
        compiler_params=LARGE,
        cost_estimate=FREE,
        name="finish",
    )(core, *operands)


def project_kernel(sources, place_ref, *refs):
    out_ref = refs[-1]
    total = None
    for x_ref, w_ref in zip(refs[:sources], refs[sources : 2 * sources]):
        part = dot(x_ref[...], w_ref[...], (1, 0))
        total = part if total is None else total + part
    out_ref[...] = total.astype(out_ref.dtype)


def project(blocks, weight, place, hops, dtype=BF16):
    size, depth = blocks[0].shape
    cols = weight.shape[1]
    step = min(256, cols)

    def rows_of(source):
        return lambda n, p: (p[0] ^ hops[source], n)

    sources = len(blocks)
    return pl.pallas_call(
        functools.partial(project_kernel, sources),
        grid_spec=pltpu.PrefetchScalarGridSpec(
            num_scalar_prefetch=1,
            grid=(cols // step,),
            in_specs=[pl.BlockSpec((size, depth), lambda n, p: (0, 0)) for _ in blocks]
            + [pl.BlockSpec((depth, step), rows_of(source)) for source in range(sources)],
            out_specs=pl.BlockSpec((size, step), lambda n, p: (0, n)),
        ),
        out_shape=jax.ShapeDtypeStruct((size, cols), dtype),
        compiler_params=SMALL,
        cost_estimate=FREE,
        name="project",
    )(place, *blocks, *[weight] * sources)


def partial_kernel(core_ref, turn_ref, x_ref, y_ref, *refs):
    weights, out_ref = refs[:-1], refs[-1]
    count = len(weights) // 2
    swapped, turned = core_ref[0] != 0, turn_ref[0] != 0
    x, y = x_ref[...], y_ref[...]
    half = x.shape[1] // 2
    total = None
    for rows, pieces in ((jnp.where(swapped, y, x), weights[:count]), (jnp.where(swapped, x, y), weights[count:])):
        left, right = rows[:, :half], rows[:, half:]
        sides = [jnp.where(turned, right, left), jnp.where(turned, left, right)]
        rows = jnp.concatenate(sides, axis=1)
        first = 0
        for piece in pieces:
            last = first + piece.shape[0]
            part = dot(rows[:, first:last], piece[...], (1, 0))
            total = part if total is None else total + part
            first = last
    out_ref[...] = total.astype(out_ref.dtype)


def partial_product(core, turn, blocks, weights):
    size, depth = blocks[0].shape
    cols = weights[0].shape[1]
    step = min(256, cols)
    return pl.pallas_call(
        partial_kernel,
        grid_spec=pltpu.PrefetchScalarGridSpec(
            num_scalar_prefetch=2,
            grid=(cols // step,),
            in_specs=[pl.BlockSpec((size, depth), lambda n, c, t: (0, 0)) for _ in blocks]
            + [pl.BlockSpec((weight.shape[0], step), lambda n, c, t: (0, n)) for weight in weights],
            out_specs=pl.BlockSpec((size, step), lambda n, c, t: (0, n)),
        ),
        out_shape=jax.ShapeDtypeStruct((size, cols), BF16),
        compiler_params=SMALL,
        cost_estimate=FREE,
        name="partial_product",
    )(core, turn, *blocks, *weights)


def join_kernel(a_ref, b_ref, *refs):
    out_ref = refs[-1]
    out_ref[...] = (a_ref[...] + b_ref[...].astype(F32)).astype(out_ref.dtype)


def join(a, b, first, rows, into=None):
    size, cols = a.shape
    step = math.gcd(first, size, 256)
    index = first // step
    spec = pl.BlockSpec((step, cols), lambda r: (r, 0))
    return pl.pallas_call(
        join_kernel,
        grid=(size // step,),
        in_specs=[spec, spec] + [pl.BlockSpec(memory_space=pl.ANY)] * (into is not None),
        out_specs=pl.BlockSpec((step, cols), lambda r: (index + r, 0)),
        out_shape=jax.ShapeDtypeStruct((rows, cols), BF16),
        input_output_aliases={} if into is None else {2: 0},
        compiler_params=SMALL,
        cost_estimate=FREE,
        name="join",
    )(a, b, *([] if into is None else [into]))


def after(value, *others):
    return lax.optimization_barrier((value, *others))[0]


def swap(value, axis, distance):
    return lax.ppermute(value, axis, [(i, i ^ distance) for i in range(lax.axis_size(axis))])


def earlier_states(sent, kept, meanwhile):
    count, mine = lax.axis_size("ctx"), lax.axis_index("ctx")
    core = mine % 2
    partner = swap(sent, "ctx", 1)
    total = (kept.astype(F32) + partner.astype(F32)).astype(BF16)
    earlier = jnp.zeros(kept.shape, F32)
    beside = meanwhile(total)
    distance = 2
    while distance < count:
        radix = min(4, count // distance)
        last = distance * radix >= count
        added = total.astype(F32)
        for step in range(1, radix):
            hop = step * distance
            pairs = [(i, i ^ hop) for i in range(count) if not last or i < i ^ hop]
            theirs = lax.ppermute(total, "ctx", pairs)
            if last:
                theirs = after(theirs, *beside)
            theirs = theirs.astype(F32)
            lower = (mine ^ hop) < mine
            earlier = earlier + jnp.where(lower, theirs, F32(0.0))
            added = added + theirs
        total = added.astype(BF16)
        distance *= radix
    own = earlier + jnp.where(core == 1, partner.astype(F32), F32(0.0))
    given = earlier + jnp.where(core == 0, kept.astype(F32), F32(0.0))
    return swap(given.astype(BF16), "ctx", 1), own.astype(BF16), beside


def normed_output(core, place, turn, query_rows, key_rows, value_rows, frequencies, norm_gain, weight=None):
    key_feat, sent, kept, prefix, *share = key_side(core, place, turn, key_rows, value_rows, frequencies, weight)

    gain = norm_gain.reshape(frequencies.shape[0], -1)

    def meanwhile(total):
        return query_side(query_rows, value_rows, after(frequencies, total), key_feat)

    theirs, own, (query_feat, local_part) = earlier_states(sent, kept, meanwhile)

    def blocks_of(cuts, *others):
        return finish(core, after(query_feat, *others), local_part, theirs, own, gain, prefix, cuts)

    return blocks_of, share


def positions():
    spot, place = lax.axis_index("ctx"), lax.axis_index("head")
    return [value.astype(jnp.int32).reshape(1) for value in (spot % 2, place, (spot // 2 + spot // 4) % 2)]


def line_of_four(query_rows, key_rows, value_rows, frequencies, norm_gain, out_weight):
    rows = query_rows.shape[0]
    core, place, turn = positions()
    sizes = [rows * part // 16 for part in (2,) * 8]
    edges = [sum(sizes[:i]) for i in range(len(sizes) + 1)]
    cuts = tuple(zip(edges[:-1], edges[1:]))
    parts = (query_rows, key_rows, value_rows, frequencies, norm_gain)
    blocks_of, (share,) = normed_output(core, place, turn, *parts, out_weight)
    blocks = blocks_of(cuts[:1])
    share = after(swap(share, "head", 1), *blocks)
    half = share.shape[0] // 2
    halves = [share[:half], share[half:]]
    blocks = [*blocks, *blocks_of(cuts[1:], *halves)]
    pairs, given, partials, products = [], [], [], []
    out, joined = None, 0
    for index, block in enumerate(blocks):
        if index > 2:
            block = after(block, given[index - 2], partials[index - 3], products[max(0, index - 3)])
        if index == len(blocks) - 1:
            while joined < index - 4:
                out = join(products[joined], partials[joined], cuts[joined][0], rows, out)
                joined += 1
            block, out = lax.optimization_barrier((block, out))
        pairs.append([block, swap(block, "head", 2)])
        if index == 1:
            others = [swap(part, "ctx", hop) for part, hop in zip(halves, (2, 4))]
            shares = [after(share, blocks[-1], pairs[0][1])] + [after(other, pairs[0][1]) for other in others]
            weights = shares + [swap(part, "ctx", 1) for part in shares]
            x, y = pairs[0]
            given.append(partial_product(core, turn, [x, y], weights))
            x, y = pairs[1]
            given.append(partial_product(core, turn, [x, after(y, given[0])], weights))
        elif index > 1:
            x, y = pairs[-1]
            y = after(y, partials[max(0, index - 3)], given[-1], *(products[:-1] if index == len(blocks) - 1 else []))
            given.append(partial_product(core, turn, [x, y], weights))
        partials += [swap(part, "head", 1) for part in given[len(partials) :]]
        products.append(project(pairs[-1], out_weight, place, (0, 2), F32))
    for product, partial, (first, _) in list(zip(products, partials, cuts))[joined:]:
        out = join(product, partial, first, rows, out)
    return out


def any_line(query_rows, key_rows, value_rows, frequencies, norm_gain, out_weight):
    core, place, turn = positions()
    parts = (query_rows, key_rows, value_rows, frequencies, norm_gain)
    blocks_of, _ = normed_output(core, place, turn, *parts)
    (normed,) = blocks_of(((0, query_rows.shape[0]),))
    gathered = lax.all_gather(normed, "head", axis=1, tiled=True)
    return jnp.dot(gathered, out_weight, preferred_element_type=F32).astype(BF16)


def solution(mesh):
    return jax.shard_map(
        line_of_four if mesh.shape["head"] == 4 and mesh.shape["ctx"] % 8 == 0 else any_line,
        mesh=mesh,
        in_specs=(
            P("ctx", "head"),
            P("ctx", "head"),
            P("ctx", "head"),
            P("head", None, None),
            P("head"),
            P(None, "head"),
        ),
        out_specs=P("ctx", "head"),
        check_vma=False,
    )
```

```python
import functools
import math

import jax
import jax.numpy as jnp
from jax import lax
from jax.experimental import pallas as pl
from jax.experimental.pallas import tpu as pltpu
from jax.sharding import PartitionSpec as P

F32 = jnp.float32
BF16 = jnp.bfloat16
SPAN = 512
TILE = 256
SIN_TERMS = (3.1406400334639137, -5.136905232797424, 2.2995469238543222)
COS_TERMS = (0.9999932955183647, -4.933938020185013, 4.0412838463445455, -1.2221270624224843)
ROUNDER = 1.5 * 2.0**23
LARGE = pltpu.CompilerParams(vmem_limit_bytes=56 << 20)
SMALL = pltpu.CompilerParams(vmem_limit_bytes=20 << 20)
FREE = pl.CostEstimate(flops=0, bytes_accessed=0, transcendentals=0)


def dot(a, b, contract):
    return lax.dot_general(a, b, ((contract[:1], contract[1:]), ((), ())), preferred_element_type=F32)


def poly(terms, scale, u):
    value = F32(terms[-1] * scale)
    for term in terms[-2::-1]:
        value = value * u + F32(term * scale)
    return value


def cos_sin(phase, amplitude):
    turns = phase * F32(1.0 / (2.0 * math.pi))
    part = turns - ((turns + F32(ROUNDER)) - F32(ROUNDER))
    u = part * part
    scale = math.sqrt(2.0 * amplitude)
    half_sin = poly(SIN_TERMS, scale, u) * part
    half_cos = poly(COS_TERMS, scale, u)
    return F32(amplitude) - half_sin * half_sin, half_sin * half_cos


def key_kernel(has_weight, core_ref, place_ref, turn_ref, key_ref, value_ref, freq_ref, *refs):
    if has_weight:
        refs[-1][...] = refs[0][...]
        refs = refs[1:]
    feat_ref, sent_ref, kept_ref, prefix_ref = refs[:4]
    rows = key_ref.shape[0]
    group, width, count = freq_ref.shape
    span = min(SPAN, rows)
    amplitude = 1.0 / math.sqrt(count)
    tiles = [(head, start) for head in range(group) for start in range(0, rows, TILE)]
    turned = [freq_ref[head].T for head in range(group)]

    def phase_of(head, start):
        lanes = slice(head * width, (head + 1) * width)
        return dot(turned[head], key_ref[start : start + TILE, lanes], (1, 1))

    def add_state(head, start, features):
        lanes = slice(head * width, (head + 1) * width)
        state = dot(features, value_ref[start : start + TILE, lanes], (1, 0))
        sums[head] = state if start == 0 else sums[head] + state
        index = (start + TILE) // span - 1
        if (start + TILE) % span == 0 and index < prefix_ref.shape[1]:
            prefix_ref[head, index] = sums[head]

    sums = [None] * group
    phase, waiting = phase_of(*tiles[0]), None
    for index, (head, start) in enumerate(tiles):
        following = phase_of(*tiles[index + 1]) if index + 1 < len(tiles) else None
        cosine, sine = cos_sin(phase, amplitude)
        features = jnp.concatenate([cosine.astype(BF16), sine.astype(BF16)], axis=0)
        feat_ref[head, :, start : start + TILE] = features
        if waiting is not None:
            add_state(*waiting)
        phase, waiting = following, (head, start, features)
    add_state(*waiting)
    sums = [total.astype(BF16) for total in sums]
    half = pl.num_programs(0) // 2

    @pl.when(pl.program_id(0) < half)
    def _():
        for head in range(group):
            sent_ref[head] = sums[head]

    @pl.when(pl.program_id(0) >= half)
    def _():
        for head in range(group):
            kept_ref[head] = sums[head]


def key_side(core, place, turn, key_rows, value_rows, frequencies, weight=None):
    rows = key_rows.shape[0]
    heads, width, count = frequencies.shape
    prior = max(1, rows // min(SPAN, rows) - 1)
    half = heads // 2
    group = 2 if half % 2 == 0 else 1
    steps, half_steps = heads // group, half // group

    def block(g, c):
        return (g + half_steps * (1 - c[0])) % steps

    in_specs = [
        pl.BlockSpec((rows, group * width), lambda g, c, p, t: (0, block(g, c))),
        pl.BlockSpec((rows, group * width), lambda g, c, p, t: (0, block(g, c))),
        pl.BlockSpec((group, width, count), lambda g, c, p, t: (block(g, c), 0, 0)),
    ]
    out_specs = [
        pl.BlockSpec((group, 2 * count, rows), lambda g, c, p, t: (block(g, c), 0, 0)),
        pl.BlockSpec((group, 2 * count, width), lambda g, c, p, t: (jnp.minimum(g, half_steps - 1), 0, 0)),
        pl.BlockSpec((group, 2 * count, width), lambda g, c, p, t: (jnp.maximum(g - half_steps, 0), 0, 0)),
        pl.BlockSpec((group, prior, 2 * count, width), lambda g, c, p, t: (block(g, c), 0, 0, 0)),
    ]
    out_shape = [
        jax.ShapeDtypeStruct((heads, 2 * count, rows), BF16),
        jax.ShapeDtypeStruct((half, 2 * count, width), BF16),
        jax.ShapeDtypeStruct((half, 2 * count, width), BF16),
        jax.ShapeDtypeStruct((heads, prior, 2 * count, width), F32),
    ]
    operands = [key_rows, value_rows, frequencies]
    if weight is not None:
        depth, cols = weight.shape[0] // 4, weight.shape[1]
        piece = depth // 2 // steps

        def rows_of(g, c, p, t):
            return ((p[0] ^ (1 + 2 * c[0])) * 2 + t[0]) * steps + g, 0

        in_specs.append(pl.BlockSpec((piece, cols), rows_of))
        out_specs.append(pl.BlockSpec((piece, cols), lambda g, c, p, t: (g, 0)))
        out_shape.append(jax.ShapeDtypeStruct((depth // 2, cols), weight.dtype))
        operands.append(weight)
    return pl.pallas_call(
        functools.partial(key_kernel, weight is not None),
        grid_spec=pltpu.PrefetchScalarGridSpec(
            num_scalar_prefetch=3, grid=(steps,), in_specs=in_specs, out_specs=out_specs
        ),
        out_shape=out_shape,
        compiler_params=LARGE,
        cost_estimate=FREE,
        name="key_side",
    )(core, place, turn, *operands)


def query_kernel(query_ref, value_ref, freq_ref, key_feat_ref, feat_ref, local_ref):
    rows = query_ref.shape[0]
    group, width, count = freq_ref.shape
    span = min(SPAN, rows)
    amplitude = 1.0 / math.sqrt(count)
    below = lax.broadcasted_iota(jnp.int32, (TILE, TILE), 0)
    causal = below >= lax.broadcasted_iota(jnp.int32, (TILE, TILE), 1)
    tiles = [(head, start) for head in range(group) for start in range(0, rows, TILE)]

    def phase_of(head, start):
        lanes = slice(head * width, (head + 1) * width)
        return dot(query_ref[start : start + TILE, lanes], freq_ref[head], (1, 0))

    def attend(head, start, features):
        lanes = slice(head * width, (head + 1) * width)
        total = None
        for other in range(start // span * span, start + TILE, TILE):
            theirs = slice(other, other + TILE)
            scores = dot(features, key_feat_ref[head, :, theirs], (1, 0))
            if other == start:
                scores = jnp.where(causal, scores, F32(0.0))
            part = dot(scores.astype(BF16), value_ref[theirs, lanes], (1, 0))
            total = part if total is None else total + part
        local_ref[start : start + TILE, lanes] = total.astype(local_ref.dtype)

    phase, waiting = phase_of(*tiles[0]), None
    for index, (head, start) in enumerate(tiles):
        following = phase_of(*tiles[index + 1]) if index + 1 < len(tiles) else None
        cosine, sine = cos_sin(phase, amplitude)
        features = jnp.concatenate([cosine.astype(BF16), sine.astype(BF16)], axis=1)
        feat_ref[head, start : start + TILE, :] = features
        if waiting is not None:
            attend(*waiting)
        phase, waiting = following, (head, start, features)
    attend(*waiting)


def query_side(query_rows, value_rows, frequencies, key_feat):
    rows = query_rows.shape[0]
    heads, width, count = frequencies.shape
    group = 2 if heads % 2 == 0 else 1
    return pl.pallas_call(
        query_kernel,
        grid=(heads // group,),
        in_specs=[
            pl.BlockSpec((rows, group * width), lambda h: (0, h)),
            pl.BlockSpec((rows, group * width), lambda h: (0, h)),
            pl.BlockSpec((group, width, count), lambda h: (h, 0, 0)),
            pl.BlockSpec((group, 2 * count, rows), lambda h: (h, 0, 0)),
        ],
        out_specs=[
            pl.BlockSpec((group, rows, 2 * count), lambda h: (h, 0, 0)),
            pl.BlockSpec((rows, group * width), lambda h: (0, h)),
        ],
        out_shape=[
            jax.ShapeDtypeStruct((heads, rows, 2 * count), BF16),
            jax.ShapeDtypeStruct((rows, heads * width), BF16),
        ],
        compiler_params=LARGE,
        cost_estimate=FREE,
        name="query_side",
    )(query_rows, value_rows, frequencies, key_feat)


def finish_kernel(
    heads, span, cuts, core_ref, feat_ref, local_ref, theirs_ref, mine_ref, gain_ref, *refs
):
    prefix_ref, out_refs = refs[0], refs[-len(cuts) :]
    width = local_ref.shape[1] // heads
    steps = pl.num_programs(0)
    kept = pl.program_id(0) >= steps // 2
    first_head = lax.rem(pl.program_id(0) + steps // 2 * (1 - core_ref[0]), steps) * heads
    gains = gain_ref[...].astype(F32)
    row = lax.broadcasted_iota(jnp.int32, gains.shape, 0)
    for head in range(heads):
        cols = slice(head * width, (head + 1) * width)
        gain = jnp.sum(jnp.where(row == first_head + head, gains, F32(0.0)), axis=0, keepdims=True)
        before = jnp.where(kept, mine_ref[head].astype(F32), theirs_ref[head].astype(F32))
        for out_ref, (first, last) in zip(out_refs, cuts):
            starts = [first, *range(first - first % TILE + TILE, last, TILE)]
            for start, stop in zip(starts, starts[1:] + [last]):
                mine = slice(start, stop)
                carried = before
                if start // span:
                    carried = carried + prefix_ref[head, start // span - 1]
                prior = dot(feat_ref[head, mine, :], carried.astype(BF16), (1, 0))
                attended = local_ref[mine, cols].astype(F32) + prior
                square = jnp.mean(attended * attended, axis=-1, keepdims=True)
                normed = attended * lax.rsqrt(square + F32(1e-6)) * gain
                out_ref[start - first : stop - first, cols] = normed.astype(BF16)


def finish(core, feat, local_part, theirs, mine, gain, prefix, cuts):
    heads, all_rows, feats = feat.shape
    rows = cuts[-1][1]
    span = min(SPAN, all_rows)
    width = local_part.shape[1] // heads
    prior = prefix.shape[1]
    half = heads // 2
    group = 4 if half % 4 == 0 and rows < span else 2 if half % 2 == 0 else 1
    steps, half_steps = heads // group, half // group

    def block(g, c):
        return (g + half_steps * (1 - c[0])) % steps

    in_specs = [
        pl.BlockSpec((group, rows, feats), lambda g, c: (block(g, c), 0, 0)),
        pl.BlockSpec((rows, group * width), lambda g, c: (0, block(g, c))),
        pl.BlockSpec((group, feats, width), lambda g, c: (jnp.minimum(g, half_steps - 1), 0, 0)),
        pl.BlockSpec((group, feats, width), lambda g, c: (jnp.maximum(g - half_steps, 0), 0, 0)),
        pl.BlockSpec(gain.shape, lambda g, c: (0, 0)),
    ]
    operands = [feat, local_part, theirs, mine, gain]
    if rows > span:
        in_specs.append(pl.BlockSpec((group, prior, feats, width), lambda g, c: (block(g, c), 0, 0, 0)))
        operands.append(prefix)
    return pl.pallas_call(
        functools.partial(finish_kernel, group, span, cuts),
        grid_spec=pltpu.PrefetchScalarGridSpec(
            num_scalar_prefetch=1,
            grid=(steps,),
            in_specs=in_specs,
            out_specs=[
                pl.BlockSpec((last - first, group * width), lambda g, c: (0, block(g, c))) for first, last in cuts
            ],
        ),
        out_shape=[jax.ShapeDtypeStruct((last - first, heads * width), BF16) for first, last in cuts],
        compiler_params=LARGE,
        cost_estimate=FREE,
        name="finish",
    )(core, *operands)


def project_kernel(sources, place_ref, *refs):
    out_ref = refs[-1]
    total = None
    for x_ref, w_ref in zip(refs[:sources], refs[sources : 2 * sources]):
        part = dot(x_ref[...], w_ref[...], (1, 0))
        total = part if total is None else total + part
    out_ref[...] = total.astype(out_ref.dtype)


def project(blocks, weight, place, hops, dtype=BF16):
    size, depth = blocks[0].shape
    cols = weight.shape[1]
    step = min(256, cols)

    def rows_of(source):
        return lambda n, p: (p[0] ^ hops[source], n)

    sources = len(blocks)
    return pl.pallas_call(
        functools.partial(project_kernel, sources),
        grid_spec=pltpu.PrefetchScalarGridSpec(
            num_scalar_prefetch=1,
            grid=(cols // step,),
            in_specs=[pl.BlockSpec((size, depth), lambda n, p: (0, 0)) for _ in blocks]
            + [pl.BlockSpec((depth, step), rows_of(source)) for source in range(sources)],
            out_specs=pl.BlockSpec((size, step), lambda n, p: (0, n)),
        ),
        out_shape=jax.ShapeDtypeStruct((size, cols), dtype),
        compiler_params=SMALL,
        cost_estimate=FREE,
        name="project",
    )(place, *blocks, *[weight] * sources)


def partial_kernel(core_ref, turn_ref, x_ref, y_ref, *refs):
    weights, out_ref = refs[:-1], refs[-1]
    count = len(weights) // 2
    swapped, turned = core_ref[0] != 0, turn_ref[0] != 0
    x, y = x_ref[...], y_ref[...]
    half = x.shape[1] // 2
    total = None
    for rows, pieces in ((jnp.where(swapped, y, x), weights[:count]), (jnp.where(swapped, x, y), weights[count:])):
        left, right = rows[:, :half], rows[:, half:]
        sides = [jnp.where(turned, right, left), jnp.where(turned, left, right)]
        rows = jnp.concatenate(sides, axis=1)
        first = 0
        for piece in pieces:
            last = first + piece.shape[0]
            part = dot(rows[:, first:last], piece[...], (1, 0))
            total = part if total is None else total + part
            first = last
    out_ref[...] = total.astype(out_ref.dtype)


def partial_product(core, turn, blocks, weights):
    size, depth = blocks[0].shape
    cols = weights[0].shape[1]
    step = min(256, cols)
    return pl.pallas_call(
        partial_kernel,
        grid_spec=pltpu.PrefetchScalarGridSpec(
            num_scalar_prefetch=2,
            grid=(cols // step,),
            in_specs=[pl.BlockSpec((size, depth), lambda n, c, t: (0, 0)) for _ in blocks]
            + [pl.BlockSpec((weight.shape[0], step), lambda n, c, t: (0, n)) for weight in weights],
            out_specs=pl.BlockSpec((size, step), lambda n, c, t: (0, n)),
        ),
        out_shape=jax.ShapeDtypeStruct((size, cols), BF16),
        compiler_params=SMALL,
        cost_estimate=FREE,
        name="partial_product",
    )(core, turn, *blocks, *weights)


def join_kernel(a_ref, b_ref, *refs):
    out_ref = refs[-1]
    out_ref[...] = (a_ref[...] + b_ref[...].astype(F32)).astype(out_ref.dtype)


def join(a, b, first, rows, into=None):
    size, cols = a.shape
    step = math.gcd(first, size, 256)
    index = first // step
    spec = pl.BlockSpec((step, cols), lambda r: (r, 0))
    return pl.pallas_call(
        join_kernel,
        grid=(size // step,),
        in_specs=[spec, spec] + [pl.BlockSpec(memory_space=pl.ANY)] * (into is not None),
        out_specs=pl.BlockSpec((step, cols), lambda r: (index + r, 0)),
        out_shape=jax.ShapeDtypeStruct((rows, cols), BF16),
        input_output_aliases={} if into is None else {2: 0},
        compiler_params=SMALL,
        cost_estimate=FREE,
        name="join",
    )(a, b, *([] if into is None else [into]))


def after(value, *others):
    return lax.optimization_barrier((value, *others))[0]


def swap(value, axis, distance):
    return lax.ppermute(value, axis, [(i, i ^ distance) for i in range(lax.axis_size(axis))])


def earlier_states(sent, kept, meanwhile):
    count, mine = lax.axis_size("ctx"), lax.axis_index("ctx")
    core = mine % 2
    partner = swap(sent, "ctx", 1)
    total = (kept.astype(F32) + partner.astype(F32)).astype(BF16)
    earlier = jnp.zeros(kept.shape, F32)
    beside = meanwhile(total)
    distance = 2
    while distance < count:
        radix = min(4, count // distance)
        last = distance * radix >= count
        added = total.astype(F32)
        for step in range(1, radix):
            hop = step * distance
            pairs = [(i, i ^ hop) for i in range(count) if not last or i < i ^ hop]
            theirs = lax.ppermute(total, "ctx", pairs)
            if last:
                theirs = after(theirs, *beside)
            theirs = theirs.astype(F32)
            lower = (mine ^ hop) < mine
            earlier = earlier + jnp.where(lower, theirs, F32(0.0))
            added = added + theirs
        total = added.astype(BF16)
        distance *= radix
    own = earlier + jnp.where(core == 1, partner.astype(F32), F32(0.0))
    given = earlier + jnp.where(core == 0, kept.astype(F32), F32(0.0))
    return swap(given.astype(BF16), "ctx", 1), own.astype(BF16), beside


def normed_output(core, place, turn, query_rows, key_rows, value_rows, frequencies, norm_gain, weight=None):
    key_feat, sent, kept, prefix, *share = key_side(core, place, turn, key_rows, value_rows, frequencies, weight)

    gain = norm_gain.reshape(frequencies.shape[0], -1)

    def meanwhile(total):
        return query_side(query_rows, value_rows, after(frequencies, total), key_feat)

    theirs, own, (query_feat, local_part) = earlier_states(sent, kept, meanwhile)

    def blocks_of(cuts, *others):
        return finish(core, after(query_feat, *others), local_part, theirs, own, gain, prefix, cuts)

    return blocks_of, share


def positions():
    spot, place = lax.axis_index("ctx"), lax.axis_index("head")
    return [value.astype(jnp.int32).reshape(1) for value in (spot % 2, place, (spot // 2 + spot // 4) % 2)]


def line_of_four(query_rows, key_rows, value_rows, frequencies, norm_gain, out_weight):
    rows = query_rows.shape[0]
    core, place, turn = positions()
    sizes = [rows * part // 16 for part in (2,) * 8]
    edges = [sum(sizes[:i]) for i in range(len(sizes) + 1)]
    cuts = tuple(zip(edges[:-1], edges[1:]))
    parts = (query_rows, key_rows, value_rows, frequencies, norm_gain)
    blocks_of, (share,) = normed_output(core, place, turn, *parts, out_weight)
    blocks = blocks_of(cuts[:1])
    share = after(swap(share, "head", 1), *blocks)
    half = share.shape[0] // 2
    halves = [share[:half], share[half:]]
    blocks = [*blocks, *blocks_of(cuts[1:], *halves)]
    pairs, given, partials, products = [], [], [], []
    out, joined = None, 0
    for index, block in enumerate(blocks):
        if index > 2:
            block = after(block, given[index - 2], partials[max(0, index - 4)], products[max(0, index - 4)])
        if index == len(blocks) - 1:
            while joined < index - 4:
                out = join(after(products[joined], given[index - 2]), partials[joined], cuts[joined][0], rows, out)
                joined += 1
            block, out = lax.optimization_barrier((block, out))
        pairs.append([block, swap(block, "head", 2)])
        if index == 1:
            others = [swap(part, "ctx", hop) for part, hop in zip(halves, (2, 4))]
            shares = [after(share, blocks[-1], pairs[0][1])] + [after(other, pairs[0][1]) for other in others]
            weights = shares + [swap(part, "ctx", 1) for part in shares]
            x, y = pairs[0]
            given.append(partial_product(core, turn, [x, y], weights))
            x, y = pairs[1]
            given.append(partial_product(core, turn, [x, after(y, given[0])], weights))
        elif index > 1:
            x, y = pairs[-1]
            y = after(y, partials[index - 2], given[-1], *(products[:-1] if index == len(blocks) - 1 else []))
            given.append(partial_product(core, turn, [x, y], weights))
        partials += [swap(part, "head", 1) for part in given[len(partials) :]]
        products.append(project(pairs[-1], out_weight, place, (0, 2), F32))
    for product, partial, (first, _) in list(zip(products, partials, cuts))[joined:]:
        out = join(product, partial, first, rows, out)
    return out


def any_line(query_rows, key_rows, value_rows, frequencies, norm_gain, out_weight):
    core, place, turn = positions()
    parts = (query_rows, key_rows, value_rows, frequencies, norm_gain)
    blocks_of, _ = normed_output(core, place, turn, *parts)
    (normed,) = blocks_of(((0, query_rows.shape[0]),))
    gathered = lax.all_gather(normed, "head", axis=1, tiled=True)
    return jnp.dot(gathered, out_weight, preferred_element_type=F32).astype(BF16)


def solution(mesh):
    return jax.shard_map(
        line_of_four if mesh.shape["head"] == 4 and mesh.shape["ctx"] % 8 == 0 else any_line,
        mesh=mesh,
        in_specs=(
            P("ctx", "head"),
            P("ctx", "head"),
            P("ctx", "head"),
            P("head", None, None),
            P("head"),
            P(None, "head"),
        ),
        out_specs=P("ctx", "head"),
        check_vma=False,
    )
```

```python
import functools
import math

import jax
import jax.numpy as jnp
from jax import lax
from jax.experimental import pallas as pl
from jax.experimental.pallas import tpu as pltpu
from jax.sharding import PartitionSpec as P

F32 = jnp.float32
BF16 = jnp.bfloat16
SPAN = 512
TILE = 256
SIN_TERMS = (3.1406400334639137, -5.136905232797424, 2.2995469238543222)
COS_TERMS = (0.9999932955183647, -4.933938020185013, 4.0412838463445455, -1.2221270624224843)
ROUNDER = 1.5 * 2.0**23
LARGE = pltpu.CompilerParams(vmem_limit_bytes=56 << 20)
MIDDLE = pltpu.CompilerParams(vmem_limit_bytes=52 << 20)
SMALL = pltpu.CompilerParams(vmem_limit_bytes=20 << 20)
FREE = pl.CostEstimate(flops=0, bytes_accessed=0, transcendentals=0)


def dot(a, b, contract):
    return lax.dot_general(a, b, ((contract[:1], contract[1:]), ((), ())), preferred_element_type=F32)


def poly(terms, scale, u):
    value = F32(terms[-1] * scale)
    for term in terms[-2::-1]:
        value = value * u + F32(term * scale)
    return value


def cos_sin(phase, amplitude):
    turns = phase * F32(1.0 / (2.0 * math.pi))
    part = turns - ((turns + F32(ROUNDER)) - F32(ROUNDER))
    u = part * part
    scale = math.sqrt(2.0 * amplitude)
    half_sin = poly(SIN_TERMS, scale, u) * part
    half_cos = poly(COS_TERMS, scale, u)
    return F32(amplitude) - half_sin * half_sin, half_sin * half_cos


def key_kernel(has_weight, core_ref, place_ref, turn_ref, key_ref, value_ref, freq_ref, *refs):
    if has_weight:
        refs[-1][...] = refs[0][...]
        refs = refs[1:]
    feat_ref, sent_ref, kept_ref, prefix_ref = refs[:4]
    rows = key_ref.shape[0]
    group, width, count = freq_ref.shape
    span = min(SPAN, rows)
    amplitude = 1.0 / math.sqrt(count)
    tiles = [(head, start) for head in range(group) for start in range(0, rows, TILE)]
    turned = [freq_ref[head].T for head in range(group)]

    def phase_of(head, start):
        lanes = slice(head * width, (head + 1) * width)
        return dot(turned[head], key_ref[start : start + TILE, lanes], (1, 1))

    def add_state(head, start, features):
        lanes = slice(head * width, (head + 1) * width)
        state = dot(features, value_ref[start : start + TILE, lanes], (1, 0))
        sums[head] = state if start == 0 else sums[head] + state
        index = (start + TILE) // span - 1
        if (start + TILE) % span == 0 and index < prefix_ref.shape[1]:
            prefix_ref[head, index] = sums[head]

    sums = [None] * group
    phase, waiting = phase_of(*tiles[0]), None
    for index, (head, start) in enumerate(tiles):
        following = phase_of(*tiles[index + 1]) if index + 1 < len(tiles) else None
        cosine, sine = cos_sin(phase, amplitude)
        features = jnp.concatenate([cosine.astype(BF16), sine.astype(BF16)], axis=0)
        feat_ref[head, :, start : start + TILE] = features
        if waiting is not None:
            add_state(*waiting)
        phase, waiting = following, (head, start, features)
    add_state(*waiting)
    sums = [total.astype(BF16) for total in sums]
    half = pl.num_programs(0) // 2

    @pl.when(pl.program_id(0) < half)
    def _():
        for head in range(group):
            sent_ref[head] = sums[head]

    @pl.when(pl.program_id(0) >= half)
    def _():
        for head in range(group):
            kept_ref[head] = sums[head]


def key_side(core, place, turn, key_rows, value_rows, frequencies, weight=None):
    rows = key_rows.shape[0]
    heads, width, count = frequencies.shape
    prior = max(1, rows // min(SPAN, rows) - 1)
    half = heads // 2
    group = 2 if half % 2 == 0 else 1
    steps, half_steps = heads // group, half // group

    def block(g, c):
        return (g + half_steps * (1 - c[0])) % steps

    in_specs = [
        pl.BlockSpec((rows, group * width), lambda g, c, p, t: (0, block(g, c))),
        pl.BlockSpec((rows, group * width), lambda g, c, p, t: (0, block(g, c))),
        pl.BlockSpec((group, width, count), lambda g, c, p, t: (block(g, c), 0, 0)),
    ]
    out_specs = [
        pl.BlockSpec((group, 2 * count, rows), lambda g, c, p, t: (block(g, c), 0, 0)),
        pl.BlockSpec((group, 2 * count, width), lambda g, c, p, t: (jnp.minimum(g, half_steps - 1), 0, 0)),
        pl.BlockSpec((group, 2 * count, width), lambda g, c, p, t: (jnp.maximum(g - half_steps, 0), 0, 0)),
        pl.BlockSpec((group, prior, 2 * count, width), lambda g, c, p, t: (block(g, c), 0, 0, 0)),
    ]
    out_shape = [
        jax.ShapeDtypeStruct((heads, 2 * count, rows), BF16),
        jax.ShapeDtypeStruct((half, 2 * count, width), BF16),
        jax.ShapeDtypeStruct((half, 2 * count, width), BF16),
        jax.ShapeDtypeStruct((heads, prior, 2 * count, width), F32),
    ]
    operands = [key_rows, value_rows, frequencies]
    if weight is not None:
        depth, cols = weight.shape[0] // 4, weight.shape[1]
        piece = depth // 2 // steps

        def rows_of(g, c, p, t):
            return ((p[0] ^ (1 + 2 * c[0])) * 2 + t[0]) * steps + g, 0

        in_specs.append(pl.BlockSpec((piece, cols), rows_of))
        out_specs.append(pl.BlockSpec((piece, cols), lambda g, c, p, t: (g, 0)))
        out_shape.append(jax.ShapeDtypeStruct((depth // 2, cols), weight.dtype))
        operands.append(weight)
    return pl.pallas_call(
        functools.partial(key_kernel, weight is not None),
        grid_spec=pltpu.PrefetchScalarGridSpec(
            num_scalar_prefetch=3, grid=(steps,), in_specs=in_specs, out_specs=out_specs
        ),
        out_shape=out_shape,
        compiler_params=LARGE,
        cost_estimate=FREE,
        name="key_side",
    )(core, place, turn, *operands)


def query_kernel(query_ref, value_ref, freq_ref, key_feat_ref, feat_ref, local_ref):
    rows = query_ref.shape[0]
    group, width, count = freq_ref.shape
    span = min(SPAN, rows)
    amplitude = 1.0 / math.sqrt(count)
    below = lax.broadcasted_iota(jnp.int32, (TILE, TILE), 0)
    causal = below >= lax.broadcasted_iota(jnp.int32, (TILE, TILE), 1)
    tiles = [(head, start) for head in range(group) for start in range(0, rows, TILE)]

    def phase_of(head, start):
        lanes = slice(head * width, (head + 1) * width)
        return dot(query_ref[start : start + TILE, lanes], freq_ref[head], (1, 0))

    def attend(head, start, features):
        lanes = slice(head * width, (head + 1) * width)
        total = None
        for other in range(start // span * span, start + TILE, TILE):
            theirs = slice(other, other + TILE)
            scores = dot(features, key_feat_ref[head, :, theirs], (1, 0))
            if other == start:
                scores = jnp.where(causal, scores, F32(0.0))
            part = dot(scores.astype(BF16), value_ref[theirs, lanes], (1, 0))
            total = part if total is None else total + part
        local_ref[start : start + TILE, lanes] = total.astype(local_ref.dtype)

    phase, waiting = phase_of(*tiles[0]), None
    for index, (head, start) in enumerate(tiles):
        following = phase_of(*tiles[index + 1]) if index + 1 < len(tiles) else None
        cosine, sine = cos_sin(phase, amplitude)
        features = jnp.concatenate([cosine.astype(BF16), sine.astype(BF16)], axis=1)
        feat_ref[head, start : start + TILE, :] = features
        if waiting is not None:
            attend(*waiting)
        phase, waiting = following, (head, start, features)
    attend(*waiting)


def query_side(query_rows, value_rows, frequencies, key_feat):
    rows = query_rows.shape[0]
    heads, width, count = frequencies.shape
    group = 2 if heads % 2 == 0 else 1
    return pl.pallas_call(
        query_kernel,
        grid=(heads // group,),
        in_specs=[
            pl.BlockSpec((rows, group * width), lambda h: (0, h)),
            pl.BlockSpec((rows, group * width), lambda h: (0, h)),
            pl.BlockSpec((group, width, count), lambda h: (h, 0, 0)),
            pl.BlockSpec((group, 2 * count, rows), lambda h: (h, 0, 0)),
        ],
        out_specs=[
            pl.BlockSpec((group, rows, 2 * count), lambda h: (h, 0, 0)),
            pl.BlockSpec((rows, group * width), lambda h: (0, h)),
        ],
        out_shape=[
            jax.ShapeDtypeStruct((heads, rows, 2 * count), BF16),
            jax.ShapeDtypeStruct((rows, heads * width), BF16),
        ],
        compiler_params=LARGE,
        cost_estimate=FREE,
        name="query_side",
    )(query_rows, value_rows, frequencies, key_feat)


def finish_kernel(
    heads, span, cuts, core_ref, feat_ref, local_ref, theirs_ref, mine_ref, gain_ref, *refs
):
    prefix_ref, out_refs = refs[0], refs[-len(cuts) :]
    width = local_ref.shape[1] // heads
    steps = pl.num_programs(0)
    kept = pl.program_id(0) >= steps // 2
    first_head = lax.rem(pl.program_id(0) + steps // 2 * (1 - core_ref[0]), steps) * heads
    gains = gain_ref[...].astype(F32)
    row = lax.broadcasted_iota(jnp.int32, gains.shape, 0)
    for head in range(heads):
        cols = slice(head * width, (head + 1) * width)
        gain = jnp.sum(jnp.where(row == first_head + head, gains, F32(0.0)), axis=0, keepdims=True)
        before = jnp.where(kept, mine_ref[head].astype(F32), theirs_ref[head].astype(F32))
        for out_ref, (first, last) in zip(out_refs, cuts):
            starts = [first, *range(first - first % TILE + TILE, last, TILE)]
            for start, stop in zip(starts, starts[1:] + [last]):
                mine = slice(start, stop)
                carried = before
                if start // span:
                    carried = carried + prefix_ref[head, start // span - 1]
                prior = dot(feat_ref[head, mine, :], carried.astype(BF16), (1, 0))
                attended = local_ref[mine, cols].astype(F32) + prior
                square = jnp.mean(attended * attended, axis=-1, keepdims=True)
                normed = attended * lax.rsqrt(square + F32(1e-6)) * gain
                out_ref[start - first : stop - first, cols] = normed.astype(BF16)


def finish(core, feat, local_part, theirs, mine, gain, prefix, cuts):
    heads, all_rows, feats = feat.shape
    rows = cuts[-1][1]
    span = min(SPAN, all_rows)
    width = local_part.shape[1] // heads
    prior = prefix.shape[1]
    half = heads // 2
    group = 4 if half % 4 == 0 and rows < span else 2 if half % 2 == 0 else 1
    steps, half_steps = heads // group, half // group

    def block(g, c):
        return (g + half_steps * (1 - c[0])) % steps

    in_specs = [
        pl.BlockSpec((group, rows, feats), lambda g, c: (block(g, c), 0, 0)),
        pl.BlockSpec((rows, group * width), lambda g, c: (0, block(g, c))),
        pl.BlockSpec((group, feats, width), lambda g, c: (jnp.minimum(g, half_steps - 1), 0, 0)),
        pl.BlockSpec((group, feats, width), lambda g, c: (jnp.maximum(g - half_steps, 0), 0, 0)),
        pl.BlockSpec(gain.shape, lambda g, c: (0, 0)),
    ]
    operands = [feat, local_part, theirs, mine, gain]
    if rows > span:
        in_specs.append(pl.BlockSpec((group, prior, feats, width), lambda g, c: (block(g, c), 0, 0, 0)))
        operands.append(prefix)
    return pl.pallas_call(
        functools.partial(finish_kernel, group, span, cuts),
        grid_spec=pltpu.PrefetchScalarGridSpec(
            num_scalar_prefetch=1,
            grid=(steps,),
            in_specs=in_specs,
            out_specs=[
                pl.BlockSpec((last - first, group * width), lambda g, c: (0, block(g, c))) for first, last in cuts
            ],
        ),
        out_shape=[jax.ShapeDtypeStruct((last - first, heads * width), BF16) for first, last in cuts],
        compiler_params=LARGE if rows > span else MIDDLE,
        cost_estimate=FREE,
        name="finish",
    )(core, *operands)


def project_kernel(sources, place_ref, *refs):
    out_ref = refs[-1]
    total = None
    for x_ref, w_ref in zip(refs[:sources], refs[sources : 2 * sources]):
        part = dot(x_ref[...], w_ref[...], (1, 0))
        total = part if total is None else total + part
    out_ref[...] = total.astype(out_ref.dtype)


def project(blocks, weight, place, hops, dtype=BF16):
    size, depth = blocks[0].shape
    cols = weight.shape[1]
    step = min(512, cols)

    def rows_of(source):
        return lambda n, p: (p[0] ^ hops[source], n)

    sources = len(blocks)
    return pl.pallas_call(
        functools.partial(project_kernel, sources),
        grid_spec=pltpu.PrefetchScalarGridSpec(
            num_scalar_prefetch=1,
            grid=(cols // step,),
            in_specs=[pl.BlockSpec((size, depth), lambda n, p: (0, 0)) for _ in blocks]
            + [pl.BlockSpec((depth, step), rows_of(source)) for source in range(sources)],
            out_specs=pl.BlockSpec((size, step), lambda n, p: (0, n)),
        ),
        out_shape=jax.ShapeDtypeStruct((size, cols), dtype),
        compiler_params=SMALL,
        cost_estimate=FREE,
        name="project",
    )(place, *blocks, *[weight] * sources)


def partial_kernel(core_ref, turn_ref, x_ref, y_ref, *refs):
    weights, out_ref = refs[:-1], refs[-1]
    count = len(weights) // 2
    swapped, turned = core_ref[0] != 0, turn_ref[0] != 0
    x, y = x_ref[...], y_ref[...]
    half = x.shape[1] // 2
    total = None
    for rows, pieces in ((jnp.where(swapped, y, x), weights[:count]), (jnp.where(swapped, x, y), weights[count:])):
        left, right = rows[:, :half], rows[:, half:]
        sides = [jnp.where(turned, right, left), jnp.where(turned, left, right)]
        rows = jnp.concatenate(sides, axis=1)
        first = 0
        for piece in pieces:
            last = first + piece.shape[0]
            part = dot(rows[:, first:last], piece[...], (1, 0))
            total = part if total is None else total + part
            first = last
    out_ref[...] = total.astype(out_ref.dtype)


def partial_product(core, turn, blocks, weights):
    size, depth = blocks[0].shape
    cols = weights[0].shape[1]
    step = min(512, cols)
    return pl.pallas_call(
        partial_kernel,
        grid_spec=pltpu.PrefetchScalarGridSpec(
            num_scalar_prefetch=2,
            grid=(cols // step,),
            in_specs=[pl.BlockSpec((size, depth), lambda n, c, t: (0, 0)) for _ in blocks]
            + [pl.BlockSpec((weight.shape[0], step), lambda n, c, t: (0, n)) for weight in weights],
            out_specs=pl.BlockSpec((size, step), lambda n, c, t: (0, n)),
        ),
        out_shape=jax.ShapeDtypeStruct((size, cols), BF16),
        compiler_params=SMALL,
        cost_estimate=FREE,
        name="partial_product",
    )(core, turn, *blocks, *weights)


def join_kernel(a_ref, b_ref, *refs):
    out_ref = refs[-1]
    out_ref[...] = (a_ref[...] + b_ref[...].astype(F32)).astype(out_ref.dtype)


def join(a, b, first, rows, into=None):
    size, cols = a.shape
    step = math.gcd(first, size, 256)
    index = first // step
    spec = pl.BlockSpec((step, cols), lambda r: (r, 0))
    return pl.pallas_call(
        join_kernel,
        grid=(size // step,),
        in_specs=[spec, spec] + [pl.BlockSpec(memory_space=pl.ANY)] * (into is not None),
        out_specs=pl.BlockSpec((step, cols), lambda r: (index + r, 0)),
        out_shape=jax.ShapeDtypeStruct((rows, cols), BF16),
        input_output_aliases={} if into is None else {2: 0},
        compiler_params=SMALL,
        cost_estimate=FREE,
        name="join",
    )(a, b, *([] if into is None else [into]))


def after(value, *others):
    return lax.optimization_barrier((value, *others))[0]


def swap(value, axis, distance):
    return lax.ppermute(value, axis, [(i, i ^ distance) for i in range(lax.axis_size(axis))])


def earlier_states(sent, kept, meanwhile):
    count, mine = lax.axis_size("ctx"), lax.axis_index("ctx")
    core = mine % 2
    partner = swap(sent, "ctx", 1)
    total = (kept.astype(F32) + partner.astype(F32)).astype(BF16)
    earlier = jnp.zeros(kept.shape, F32)
    beside = meanwhile(total)
    distance = 2
    while distance < count:
        radix = min(4, count // distance)
        last = distance * radix >= count
        added = total.astype(F32)
        for step in range(1, radix):
            hop = step * distance
            pairs = [(i, i ^ hop) for i in range(count) if not last or i < i ^ hop]
            theirs = lax.ppermute(total, "ctx", pairs)
            if last:
                theirs = after(theirs, *beside)
            theirs = theirs.astype(F32)
            lower = (mine ^ hop) < mine
            earlier = earlier + jnp.where(lower, theirs, F32(0.0))
            added = added + theirs
        total = added.astype(BF16)
        distance *= radix
    own = earlier + jnp.where(core == 1, partner.astype(F32), F32(0.0))
    given = earlier + jnp.where(core == 0, kept.astype(F32), F32(0.0))
    return swap(given.astype(BF16), "ctx", 1), own.astype(BF16), beside


def normed_output(core, place, turn, query_rows, key_rows, value_rows, frequencies, norm_gain, weight=None):
    key_feat, sent, kept, prefix, *share = key_side(core, place, turn, key_rows, value_rows, frequencies, weight)

    gain = norm_gain.reshape(frequencies.shape[0], -1)

    def meanwhile(total):
        return query_side(query_rows, value_rows, after(frequencies, total), key_feat)

    theirs, own, (query_feat, local_part) = earlier_states(sent, kept, meanwhile)

    def blocks_of(cuts, *others):
        return finish(core, after(query_feat, *others), local_part, theirs, own, gain, prefix, cuts)

    return blocks_of, share


def positions():
    spot, place = lax.axis_index("ctx"), lax.axis_index("head")
    return [value.astype(jnp.int32).reshape(1) for value in (spot % 2, place, (spot // 2 + spot // 4) % 2)]


def line_of_four(query_rows, key_rows, value_rows, frequencies, norm_gain, out_weight):
    rows = query_rows.shape[0]
    core, place, turn = positions()
    sizes = [rows * part // 16 for part in (2,) * 8]
    edges = [sum(sizes[:i]) for i in range(len(sizes) + 1)]
    cuts = tuple(zip(edges[:-1], edges[1:]))
    parts = (query_rows, key_rows, value_rows, frequencies, norm_gain)
    blocks_of, (share,) = normed_output(core, place, turn, *parts, out_weight)
    blocks = blocks_of(cuts[:1])
    share = after(swap(share, "head", 1), *blocks)
    half = share.shape[0] // 2
    halves = [share[:half], share[half:]]
    blocks = [*blocks, *blocks_of(cuts[1:], *halves)]
    pairs, given, partials, products = [], [], [], []
    out, joined = None, 0
    for index, block in enumerate(blocks):
        if index > 2:
            block = after(block, given[index - 2], partials[max(0, index - 4)], products[max(0, index - 4)])
        if index == len(blocks) - 1:
            while joined < index - 4:
                out = join(after(products[joined], given[index - 2]), partials[joined], cuts[joined][0], rows, out)
                joined += 1
            block, out = lax.optimization_barrier((block, out))
        pairs.append([block, swap(block, "head", 2)])
        if index == 1:
            others = [swap(part, "ctx", hop) for part, hop in zip(halves, (2, 4))]
            shares = [after(share, blocks[-1], pairs[0][1])] + [after(other, pairs[0][1]) for other in others]
            weights = shares + [swap(part, "ctx", 1) for part in shares]
            x, y = pairs[0]
            given.append(partial_product(core, turn, [x, y], weights))
            x, y = pairs[1]
            given.append(partial_product(core, turn, [x, after(y, given[0])], weights))
        elif index > 1:
            x, y = pairs[-1]
            y = after(y, partials[index - 2], given[-1], *(products[:-1] if index == len(blocks) - 1 else []))
            given.append(partial_product(core, turn, [x, y], weights))
        partials += [swap(part, "head", 1) for part in given[len(partials) :]]
        products.append(project(pairs[-1], out_weight, place, (0, 2), F32))
    for product, partial, (first, _) in list(zip(products, partials, cuts))[joined:]:
        out = join(product, partial, first, rows, out)
    return out


def any_line(query_rows, key_rows, value_rows, frequencies, norm_gain, out_weight):
    core, place, turn = positions()
    parts = (query_rows, key_rows, value_rows, frequencies, norm_gain)
    blocks_of, _ = normed_output(core, place, turn, *parts)
    (normed,) = blocks_of(((0, query_rows.shape[0]),))
    gathered = lax.all_gather(normed, "head", axis=1, tiled=True)
    return jnp.dot(gathered, out_weight, preferred_element_type=F32).astype(BF16)


def solution(mesh):
    return jax.shard_map(
        line_of_four if mesh.shape["head"] == 4 and mesh.shape["ctx"] % 8 == 0 else any_line,
        mesh=mesh,
        in_specs=(
            P("ctx", "head"),
            P("ctx", "head"),
            P("ctx", "head"),
            P("head", None, None),
            P("head"),
            P(None, "head"),
        ),
        out_specs=P("ctx", "head"),
        check_vma=False,
    )
```

```python
import functools
import math

import jax
import jax.numpy as jnp
from jax import lax
from jax.experimental import pallas as pl
from jax.experimental.pallas import tpu as pltpu
from jax.sharding import PartitionSpec as P

F32 = jnp.float32
BF16 = jnp.bfloat16
SPAN = 512
TILE = 256
SIN_TERMS = (3.1406400334639137, -5.136905232797424, 2.2995469238543222)
COS_TERMS = (0.9999932955183647, -4.933938020185013, 4.0412838463445455, -1.2221270624224843)
ROUNDER = 1.5 * 2.0**23
LARGE = pltpu.CompilerParams(vmem_limit_bytes=56 << 20)
MIDDLE = pltpu.CompilerParams(vmem_limit_bytes=52 << 20)
SMALL = pltpu.CompilerParams(vmem_limit_bytes=20 << 20)
FREE = pl.CostEstimate(flops=0, bytes_accessed=0, transcendentals=0)


def dot(a, b, contract):
    return lax.dot_general(a, b, ((contract[:1], contract[1:]), ((), ())), preferred_element_type=F32)


def poly(terms, scale, u):
    value = F32(terms[-1] * scale)
    for term in terms[-2::-1]:
        value = value * u + F32(term * scale)
    return value


def cos_sin(phase, amplitude):
    turns = phase * F32(1.0 / (2.0 * math.pi))
    part = turns - ((turns + F32(ROUNDER)) - F32(ROUNDER))
    u = part * part
    scale = math.sqrt(2.0 * amplitude)
    half_sin = poly(SIN_TERMS, scale, u) * part
    half_cos = poly(COS_TERMS, scale, u)
    return F32(amplitude) - half_sin * half_sin, half_sin * half_cos


def key_kernel(has_weight, core_ref, place_ref, turn_ref, key_ref, value_ref, freq_ref, *refs):
    if has_weight:
        refs[-1][...] = refs[0][...]
        refs = refs[1:]
    feat_ref, sent_ref, kept_ref, prefix_ref = refs[:4]
    rows = key_ref.shape[0]
    group, width, count = freq_ref.shape
    span = min(SPAN, rows)
    amplitude = 1.0 / math.sqrt(count)
    tiles = [(head, start) for head in range(group) for start in range(0, rows, TILE)]
    turned = [freq_ref[head].T for head in range(group)]

    def phase_of(head, start):
        lanes = slice(head * width, (head + 1) * width)
        return dot(turned[head], key_ref[start : start + TILE, lanes], (1, 1))

    def add_state(head, start, features):
        lanes = slice(head * width, (head + 1) * width)
        state = dot(features, value_ref[start : start + TILE, lanes], (1, 0))
        sums[head] = state if start == 0 else sums[head] + state
        index = (start + TILE) // span - 1
        if (start + TILE) % span == 0 and index < prefix_ref.shape[1]:
            prefix_ref[head, index] = sums[head]

    sums = [None] * group
    phase, waiting = phase_of(*tiles[0]), None
    for index, (head, start) in enumerate(tiles):
        following = phase_of(*tiles[index + 1]) if index + 1 < len(tiles) else None
        cosine, sine = cos_sin(phase, amplitude)
        features = jnp.concatenate([cosine.astype(BF16), sine.astype(BF16)], axis=0)
        feat_ref[head, :, start : start + TILE] = features
        if waiting is not None:
            add_state(*waiting)
        phase, waiting = following, (head, start, features)
    add_state(*waiting)
    sums = [total.astype(BF16) for total in sums]
    half = pl.num_programs(0) // 2

    @pl.when(pl.program_id(0) < half)
    def _():
        for head in range(group):
            sent_ref[head] = sums[head]

    @pl.when(pl.program_id(0) >= half)
    def _():
        for head in range(group):
            kept_ref[head] = sums[head]


def key_side(core, place, turn, key_rows, value_rows, frequencies, weight=None):
    rows = key_rows.shape[0]
    heads, width, count = frequencies.shape
    prior = max(1, rows // min(SPAN, rows) - 1)
    half = heads // 2
    group = 2 if half % 2 == 0 else 1
    steps, half_steps = heads // group, half // group

    def block(g, c):
        return (g + half_steps * (1 - c[0])) % steps

    in_specs = [
        pl.BlockSpec((rows, group * width), lambda g, c, p, t: (0, block(g, c))),
        pl.BlockSpec((rows, group * width), lambda g, c, p, t: (0, block(g, c))),
        pl.BlockSpec((group, width, count), lambda g, c, p, t: (block(g, c), 0, 0)),
    ]
    out_specs = [
        pl.BlockSpec((group, 2 * count, rows), lambda g, c, p, t: (block(g, c), 0, 0)),
        pl.BlockSpec((group, 2 * count, width), lambda g, c, p, t: (jnp.minimum(g, half_steps - 1), 0, 0)),
        pl.BlockSpec((group, 2 * count, width), lambda g, c, p, t: (jnp.maximum(g - half_steps, 0), 0, 0)),
        pl.BlockSpec((group, prior, 2 * count, width), lambda g, c, p, t: (block(g, c), 0, 0, 0)),
    ]
    out_shape = [
        jax.ShapeDtypeStruct((heads, 2 * count, rows), BF16),
        jax.ShapeDtypeStruct((half, 2 * count, width), BF16),
        jax.ShapeDtypeStruct((half, 2 * count, width), BF16),
        jax.ShapeDtypeStruct((heads, prior, 2 * count, width), F32),
    ]
    operands = [key_rows, value_rows, frequencies]
    if weight is not None:
        depth, cols = weight.shape[0] // 4, weight.shape[1]
        piece = depth // 2 // steps

        def rows_of(g, c, p, t):
            return ((p[0] ^ (1 + 2 * c[0])) * 2 + t[0]) * steps + g, 0

        in_specs.append(pl.BlockSpec((piece, cols), rows_of))
        out_specs.append(pl.BlockSpec((piece, cols), lambda g, c, p, t: (g, 0)))
        out_shape.append(jax.ShapeDtypeStruct((depth // 2, cols), weight.dtype))
        operands.append(weight)
    return pl.pallas_call(
        functools.partial(key_kernel, weight is not None),
        grid_spec=pltpu.PrefetchScalarGridSpec(
            num_scalar_prefetch=3, grid=(steps,), in_specs=in_specs, out_specs=out_specs
        ),
        out_shape=out_shape,
        compiler_params=pltpu.CompilerParams(vmem_limit_bytes=53 << 20),
        cost_estimate=FREE,
        name="key_side",
    )(core, place, turn, *operands)


def query_kernel(query_ref, value_ref, freq_ref, key_feat_ref, feat_ref, local_ref):
    rows = query_ref.shape[0]
    group, width, count = freq_ref.shape
    span = min(SPAN, rows)
    amplitude = 1.0 / math.sqrt(count)
    below = lax.broadcasted_iota(jnp.int32, (TILE, TILE), 0)
    causal = below >= lax.broadcasted_iota(jnp.int32, (TILE, TILE), 1)
    tiles = [(head, start) for head in range(group) for start in range(0, rows, TILE)]

    def phase_of(head, start):
        lanes = slice(head * width, (head + 1) * width)
        return dot(query_ref[start : start + TILE, lanes], freq_ref[head], (1, 0))

    def attend(head, start, features):
        lanes = slice(head * width, (head + 1) * width)
        total = None
        for other in range(start // span * span, start + TILE, TILE):
            theirs = slice(other, other + TILE)
            scores = dot(features, key_feat_ref[head, :, theirs], (1, 0))
            if other == start:
                scores = jnp.where(causal, scores, F32(0.0))
            part = dot(scores.astype(BF16), value_ref[theirs, lanes], (1, 0))
            total = part if total is None else total + part
        local_ref[start : start + TILE, lanes] = total.astype(local_ref.dtype)

    phase, waiting = phase_of(*tiles[0]), None
    for index, (head, start) in enumerate(tiles):
        following = phase_of(*tiles[index + 1]) if index + 1 < len(tiles) else None
        cosine, sine = cos_sin(phase, amplitude)
        features = jnp.concatenate([cosine.astype(BF16), sine.astype(BF16)], axis=1)
        feat_ref[head, start : start + TILE, :] = features
        if waiting is not None:
            attend(*waiting)
        phase, waiting = following, (head, start, features)
    attend(*waiting)


def query_side(query_rows, value_rows, frequencies, key_feat):
    rows = query_rows.shape[0]
    heads, width, count = frequencies.shape
    group = 2 if heads % 2 == 0 else 1
    return pl.pallas_call(
        query_kernel,
        grid=(heads // group,),
        in_specs=[
            pl.BlockSpec((rows, group * width), lambda h: (0, h)),
            pl.BlockSpec((rows, group * width), lambda h: (0, h)),
            pl.BlockSpec((group, width, count), lambda h: (h, 0, 0)),
            pl.BlockSpec((group, 2 * count, rows), lambda h: (h, 0, 0)),
        ],
        out_specs=[
            pl.BlockSpec((group, rows, 2 * count), lambda h: (h, 0, 0)),
            pl.BlockSpec((rows, group * width), lambda h: (0, h)),
        ],
        out_shape=[
            jax.ShapeDtypeStruct((heads, rows, 2 * count), BF16),
            jax.ShapeDtypeStruct((rows, heads * width), BF16),
        ],
        compiler_params=MIDDLE,
        cost_estimate=FREE,
        name="query_side",
    )(query_rows, value_rows, frequencies, key_feat)


def finish_kernel(
    heads, span, cuts, core_ref, feat_ref, local_ref, theirs_ref, mine_ref, gain_ref, *refs
):
    prefix_ref, out_refs = refs[0], refs[-len(cuts) :]
    width = local_ref.shape[1] // heads
    steps = pl.num_programs(0)
    kept = pl.program_id(0) >= steps // 2
    first_head = lax.rem(pl.program_id(0) + steps // 2 * (1 - core_ref[0]), steps) * heads
    gains = gain_ref[...].astype(F32)
    row = lax.broadcasted_iota(jnp.int32, gains.shape, 0)
    for head in range(heads):
        cols = slice(head * width, (head + 1) * width)
        gain = jnp.sum(jnp.where(row == first_head + head, gains, F32(0.0)), axis=0, keepdims=True)
        before = jnp.where(kept, mine_ref[head].astype(F32), theirs_ref[head].astype(F32))
        for out_ref, (first, last) in zip(out_refs, cuts):
            starts = [first, *range(first - first % TILE + TILE, last, TILE)]
            for start, stop in zip(starts, starts[1:] + [last]):
                mine = slice(start, stop)
                carried = before
                if start // span:
                    carried = carried + prefix_ref[head, start // span - 1]
                prior = dot(feat_ref[head, mine, :], carried.astype(BF16), (1, 0))
                attended = local_ref[mine, cols].astype(F32) + prior
                square = jnp.mean(attended * attended, axis=-1, keepdims=True)
                normed = attended * lax.rsqrt(square + F32(1e-6)) * gain
                out_ref[start - first : stop - first, cols] = normed.astype(BF16)


def finish(core, feat, local_part, theirs, mine, gain, prefix, cuts):
    heads, all_rows, feats = feat.shape
    rows = cuts[-1][1]
    span = min(SPAN, all_rows)
    width = local_part.shape[1] // heads
    prior = prefix.shape[1]
    half = heads // 2
    group = 4 if half % 4 == 0 and rows < span else 2 if half % 2 == 0 else 1
    steps, half_steps = heads // group, half // group

    def block(g, c):
        return (g + half_steps * (1 - c[0])) % steps

    in_specs = [
        pl.BlockSpec((group, rows, feats), lambda g, c: (block(g, c), 0, 0)),
        pl.BlockSpec((rows, group * width), lambda g, c: (0, block(g, c))),
        pl.BlockSpec((group, feats, width), lambda g, c: (jnp.minimum(g, half_steps - 1), 0, 0)),
        pl.BlockSpec((group, feats, width), lambda g, c: (jnp.maximum(g - half_steps, 0), 0, 0)),
        pl.BlockSpec(gain.shape, lambda g, c: (0, 0)),
    ]
    operands = [feat, local_part, theirs, mine, gain]
    if rows > span:
        in_specs.append(pl.BlockSpec((group, prior, feats, width), lambda g, c: (block(g, c), 0, 0, 0)))
        operands.append(prefix)
    return pl.pallas_call(
        functools.partial(finish_kernel, group, span, cuts),
        grid_spec=pltpu.PrefetchScalarGridSpec(
            num_scalar_prefetch=1,
            grid=(steps,),
            in_specs=in_specs,
            out_specs=[
                pl.BlockSpec((last - first, group * width), lambda g, c: (0, block(g, c))) for first, last in cuts
            ],
        ),
        out_shape=[jax.ShapeDtypeStruct((last - first, heads * width), BF16) for first, last in cuts],
        compiler_params=LARGE if rows > span else MIDDLE,
        cost_estimate=FREE,
        name="finish",
    )(core, *operands)


def project_kernel(sources, place_ref, *refs):
    out_ref = refs[-1]
    total = None
    for x_ref, w_ref in zip(refs[:sources], refs[sources : 2 * sources]):
        part = dot(x_ref[...], w_ref[...], (1, 0))
        total = part if total is None else total + part
    out_ref[...] = total.astype(out_ref.dtype)


def project(blocks, weight, place, hops, dtype=BF16):
    size, depth = blocks[0].shape
    cols = weight.shape[1]
    step = min(1024, cols)

    def rows_of(source):
        return lambda n, p: (p[0] ^ hops[source], n)

    sources = len(blocks)
    return pl.pallas_call(
        functools.partial(project_kernel, sources),
        grid_spec=pltpu.PrefetchScalarGridSpec(
            num_scalar_prefetch=1,
            grid=(cols // step,),
            in_specs=[pl.BlockSpec((size, depth), lambda n, p: (0, 0)) for _ in blocks]
            + [pl.BlockSpec((depth, step), rows_of(source)) for source in range(sources)],
            out_specs=pl.BlockSpec((size, step), lambda n, p: (0, n)),
        ),
        out_shape=jax.ShapeDtypeStruct((size, cols), dtype),
        compiler_params=SMALL,
        cost_estimate=FREE,
        name="project",
    )(place, *blocks, *[weight] * sources)


def partial_kernel(core_ref, turn_ref, x_ref, y_ref, *refs):
    weights, out_ref = refs[:-1], refs[-1]
    count = len(weights) // 2
    swapped, turned = core_ref[0] != 0, turn_ref[0] != 0
    x, y = x_ref[...], y_ref[...]
    half = x.shape[1] // 2
    total = None
    for rows, pieces in ((jnp.where(swapped, y, x), weights[:count]), (jnp.where(swapped, x, y), weights[count:])):
        left, right = rows[:, :half], rows[:, half:]
        sides = [jnp.where(turned, right, left), jnp.where(turned, left, right)]
        rows = jnp.concatenate(sides, axis=1)
        first = 0
        for piece in pieces:
            last = first + piece.shape[0]
            part = dot(rows[:, first:last], piece[...], (1, 0))
            total = part if total is None else total + part
            first = last
    out_ref[...] = total.astype(out_ref.dtype)


def partial_product(core, turn, blocks, weights):
    size, depth = blocks[0].shape
    cols = weights[0].shape[1]
    step = min(1024, cols)
    return pl.pallas_call(
        partial_kernel,
        grid_spec=pltpu.PrefetchScalarGridSpec(
            num_scalar_prefetch=2,
            grid=(cols // step,),
            in_specs=[pl.BlockSpec((size, depth), lambda n, c, t: (0, 0)) for _ in blocks]
            + [pl.BlockSpec((weight.shape[0], step), lambda n, c, t: (0, n)) for weight in weights],
            out_specs=pl.BlockSpec((size, step), lambda n, c, t: (0, n)),
        ),
        out_shape=jax.ShapeDtypeStruct((size, cols), BF16),
        compiler_params=SMALL,
        cost_estimate=FREE,
        name="partial_product",
    )(core, turn, *blocks, *weights)


def join_kernel(a_ref, b_ref, *refs):
    out_ref = refs[-1]
    out_ref[...] = (a_ref[...] + b_ref[...].astype(F32)).astype(out_ref.dtype)


def join(a, b, first, rows, into=None):
    size, cols = a.shape
    step = math.gcd(first, size, 256)
    index = first // step
    spec = pl.BlockSpec((step, cols), lambda r: (r, 0))
    return pl.pallas_call(
        join_kernel,
        grid=(size // step,),
        in_specs=[spec, spec] + [pl.BlockSpec(memory_space=pl.ANY)] * (into is not None),
        out_specs=pl.BlockSpec((step, cols), lambda r: (index + r, 0)),
        out_shape=jax.ShapeDtypeStruct((rows, cols), BF16),
        input_output_aliases={} if into is None else {2: 0},
        compiler_params=SMALL,
        cost_estimate=FREE,
        name="join",
    )(a, b, *([] if into is None else [into]))


def after(value, *others):
    return lax.optimization_barrier((value, *others))[0]


def swap(value, axis, distance):
    return lax.ppermute(value, axis, [(i, i ^ distance) for i in range(lax.axis_size(axis))])


def earlier_states(sent, kept, meanwhile):
    count, mine = lax.axis_size("ctx"), lax.axis_index("ctx")
    core = mine % 2
    partner = swap(sent, "ctx", 1)
    total = (kept.astype(F32) + partner.astype(F32)).astype(BF16)
    earlier = jnp.zeros(kept.shape, F32)
    beside = meanwhile(total)
    distance = 2
    while distance < count:
        radix = min(4, count // distance)
        last = distance * radix >= count
        added = total.astype(F32)
        for step in range(1, radix):
            hop = step * distance
            pairs = [(i, i ^ hop) for i in range(count) if not last or i < i ^ hop]
            theirs = lax.ppermute(total, "ctx", pairs)
            if last:
                theirs = after(theirs, *beside)
            theirs = theirs.astype(F32)
            lower = (mine ^ hop) < mine
            earlier = earlier + jnp.where(lower, theirs, F32(0.0))
            added = added + theirs
        total = added.astype(BF16)
        distance *= radix
    own = earlier + jnp.where(core == 1, partner.astype(F32), F32(0.0))
    given = earlier + jnp.where(core == 0, kept.astype(F32), F32(0.0))
    return swap(given.astype(BF16), "ctx", 1), own.astype(BF16), beside


def normed_output(core, place, turn, query_rows, key_rows, value_rows, frequencies, norm_gain, weight=None):
    key_feat, sent, kept, prefix, *share = key_side(core, place, turn, key_rows, value_rows, frequencies, weight)

    gain = norm_gain.reshape(frequencies.shape[0], -1)

    def meanwhile(total):
        return query_side(query_rows, value_rows, after(frequencies, total), key_feat)

    theirs, own, (query_feat, local_part) = earlier_states(sent, kept, meanwhile)

    def blocks_of(cuts, *others):
        return finish(core, after(query_feat, *others), local_part, theirs, own, gain, prefix, cuts)

    return blocks_of, share


def positions():
    spot, place = lax.axis_index("ctx"), lax.axis_index("head")
    return [value.astype(jnp.int32).reshape(1) for value in (spot % 2, place, (spot // 2 + spot // 4) % 2)]


def line_of_four(query_rows, key_rows, value_rows, frequencies, norm_gain, out_weight):
    rows = query_rows.shape[0]
    core, place, turn = positions()
    sizes = [rows * part // 16 for part in (2,) * 8]
    edges = [sum(sizes[:i]) for i in range(len(sizes) + 1)]
    cuts = tuple(zip(edges[:-1], edges[1:]))
    parts = (query_rows, key_rows, value_rows, frequencies, norm_gain)
    blocks_of, (share,) = normed_output(core, place, turn, *parts, out_weight)
    blocks = blocks_of(cuts[:1])
    share = after(swap(share, "head", 1), *blocks)
    half = share.shape[0] // 2
    halves = [share[:half], share[half:]]
    blocks = [*blocks, *blocks_of(cuts[1:], *halves)]
    pairs, given, partials, products = [], [], [], []
    out, joined = None, 0
    for index, block in enumerate(blocks):
        if index > 2:
            block = after(block, given[index - 2], partials[max(0, index - 4)], products[max(0, index - 4)])
        if index == len(blocks) - 1:
            while joined < index - 4:
                out = join(after(products[joined], given[index - 2]), partials[joined], cuts[joined][0], rows, out)
                joined += 1
            block, out = lax.optimization_barrier((block, out))
        pairs.append([block, swap(block, "head", 2)])
        if index == 1:
            others = [swap(part, "ctx", hop) for part, hop in zip(halves, (2, 4))]
            shares = [after(share, blocks[-1], pairs[0][1])] + [after(other, pairs[0][1]) for other in others]
            weights = shares + [swap(part, "ctx", 1) for part in shares]
            x, y = pairs[0]
            given.append(partial_product(core, turn, [x, y], weights))
            x, y = pairs[1]
            given.append(partial_product(core, turn, [x, after(y, given[0])], weights))
        elif index > 1:
            x, y = pairs[-1]
            y = after(y, partials[index - 2], given[-1], *(products[:-1] if index == len(blocks) - 1 else []))
            given.append(partial_product(core, turn, [x, y], weights))
        partials += [swap(part, "head", 1) for part in given[len(partials) :]]
        products.append(project(pairs[-1], out_weight, place, (0, 2), F32))
    for product, partial, (first, _) in list(zip(products, partials, cuts))[joined:]:
        out = join(product, partial, first, rows, out)
    return out


def any_line(query_rows, key_rows, value_rows, frequencies, norm_gain, out_weight):
    core, place, turn = positions()
    parts = (query_rows, key_rows, value_rows, frequencies, norm_gain)
    blocks_of, _ = normed_output(core, place, turn, *parts)
    (normed,) = blocks_of(((0, query_rows.shape[0]),))
    gathered = lax.all_gather(normed, "head", axis=1, tiled=True)
    return jnp.dot(gathered, out_weight, preferred_element_type=F32).astype(BF16)


def solution(mesh):
    return jax.shard_map(
        line_of_four if mesh.shape["head"] == 4 and mesh.shape["ctx"] % 8 == 0 else any_line,
        mesh=mesh,
        in_specs=(
            P("ctx", "head"),
            P("ctx", "head"),
            P("ctx", "head"),
            P("head", None, None),
            P("head"),
            P(None, "head"),
        ),
        out_specs=P("ctx", "head"),
        check_vma=False,
    )
```

```python
import functools
import math

import jax
import jax.numpy as jnp
from jax import lax
from jax.experimental import pallas as pl
from jax.experimental.pallas import tpu as pltpu
from jax.sharding import PartitionSpec as P

F32 = jnp.float32
BF16 = jnp.bfloat16
SPAN = 512
TILE = 256
SIN_TERMS = (3.1406400334639137, -5.136905232797424, 2.2995469238543222)
COS_TERMS = (0.9999932955183647, -4.933938020185013, 4.0412838463445455, -1.2221270624224843)
ROUNDER = 1.5 * 2.0**23
LARGE = pltpu.CompilerParams(vmem_limit_bytes=56 << 20)
MIDDLE = pltpu.CompilerParams(vmem_limit_bytes=52 << 20)
SMALL = pltpu.CompilerParams(vmem_limit_bytes=20 << 20)
FREE = pl.CostEstimate(flops=0, bytes_accessed=0, transcendentals=0)


def dot(a, b, contract):
    return lax.dot_general(a, b, ((contract[:1], contract[1:]), ((), ())), preferred_element_type=F32)


def poly(terms, scale, u):
    value = F32(terms[-1] * scale)
    for term in terms[-2::-1]:
        value = value * u + F32(term * scale)
    return value


def cos_sin(phase, amplitude):
    turns = phase * F32(1.0 / (2.0 * math.pi))
    part = turns - ((turns + F32(ROUNDER)) - F32(ROUNDER))
    u = part * part
    scale = math.sqrt(2.0 * amplitude)
    half_sin = poly(SIN_TERMS, scale, u) * part
    half_cos = poly(COS_TERMS, scale, u)
    return F32(amplitude) - half_sin * half_sin, half_sin * half_cos


def key_kernel(has_weight, core_ref, place_ref, turn_ref, key_ref, value_ref, freq_ref, *refs):
    if has_weight:
        refs[-1][...] = refs[0][...]
        refs = refs[1:]
    feat_ref, sent_ref, kept_ref, prefix_ref = refs[:4]
    rows = key_ref.shape[0]
    group, width, count = freq_ref.shape
    span = min(SPAN, rows)
    amplitude = 1.0 / math.sqrt(count)
    tiles = [(head, start) for head in range(group) for start in range(0, rows, TILE)]
    turned = [freq_ref[head].T for head in range(group)]

    def phase_of(head, start):
        lanes = slice(head * width, (head + 1) * width)
        return dot(turned[head], key_ref[start : start + TILE, lanes], (1, 1))

    def add_state(head, start, features):
        lanes = slice(head * width, (head + 1) * width)
        state = dot(features, value_ref[start : start + TILE, lanes], (1, 0))
        sums[head] = state if start == 0 else sums[head] + state
        index = (start + TILE) // span - 1
        if (start + TILE) % span == 0 and index < prefix_ref.shape[1]:
            prefix_ref[head, index] = sums[head]

    sums = [None] * group
    phase, waiting = phase_of(*tiles[0]), None
    for index, (head, start) in enumerate(tiles):
        following = phase_of(*tiles[index + 1]) if index + 1 < len(tiles) else None
        cosine, sine = cos_sin(phase, amplitude)
        features = jnp.concatenate([cosine.astype(BF16), sine.astype(BF16)], axis=0)
        feat_ref[head, :, start : start + TILE] = features
        if waiting is not None:
            add_state(*waiting)
        phase, waiting = following, (head, start, features)
    add_state(*waiting)
    sums = [total.astype(BF16) for total in sums]
    half = pl.num_programs(0) // 2

    @pl.when(pl.program_id(0) < half)
    def _():
        for head in range(group):
            sent_ref[head] = sums[head]

    @pl.when(pl.program_id(0) >= half)
    def _():
        for head in range(group):
            kept_ref[head] = sums[head]


def key_side(core, place, turn, key_rows, value_rows, frequencies, weight=None):
    rows = key_rows.shape[0]
    heads, width, count = frequencies.shape
    prior = max(1, rows // min(SPAN, rows) - 1)
    half = heads // 2
    group = 2 if half % 2 == 0 else 1
    steps, half_steps = heads // group, half // group

    def block(g, c):
        return (g + half_steps * (1 - c[0])) % steps

    in_specs = [
        pl.BlockSpec((rows, group * width), lambda g, c, p, t: (0, block(g, c))),
        pl.BlockSpec((rows, group * width), lambda g, c, p, t: (0, block(g, c))),
        pl.BlockSpec((group, width, count), lambda g, c, p, t: (block(g, c), 0, 0)),
    ]
    out_specs = [
        pl.BlockSpec((group, 2 * count, rows), lambda g, c, p, t: (block(g, c), 0, 0)),
        pl.BlockSpec((group, 2 * count, width), lambda g, c, p, t: (jnp.minimum(g, half_steps - 1), 0, 0)),
        pl.BlockSpec((group, 2 * count, width), lambda g, c, p, t: (jnp.maximum(g - half_steps, 0), 0, 0)),
        pl.BlockSpec((group, prior, 2 * count, width), lambda g, c, p, t: (block(g, c), 0, 0, 0)),
    ]
    out_shape = [
        jax.ShapeDtypeStruct((heads, 2 * count, rows), BF16),
        jax.ShapeDtypeStruct((half, 2 * count, width), BF16),
        jax.ShapeDtypeStruct((half, 2 * count, width), BF16),
        jax.ShapeDtypeStruct((heads, prior, 2 * count, width), F32),
    ]
    operands = [key_rows, value_rows, frequencies]
    if weight is not None:
        depth, cols = weight.shape[0] // 4, weight.shape[1]
        piece = depth // 2 // steps

        def rows_of(g, c, p, t):
            return ((p[0] ^ (1 + 2 * c[0])) * 2 + t[0]) * steps + g, 0

        in_specs.append(pl.BlockSpec((piece, cols), rows_of))
        out_specs.append(pl.BlockSpec((piece, cols), lambda g, c, p, t: (g, 0)))
        out_shape.append(jax.ShapeDtypeStruct((depth // 2, cols), weight.dtype))
        operands.append(weight)
    return pl.pallas_call(
        functools.partial(key_kernel, weight is not None),
        grid_spec=pltpu.PrefetchScalarGridSpec(
            num_scalar_prefetch=3, grid=(steps,), in_specs=in_specs, out_specs=out_specs
        ),
        out_shape=out_shape,
        compiler_params=LARGE,
        cost_estimate=FREE,
        name="key_side",
    )(core, place, turn, *operands)


def query_kernel(query_ref, value_ref, freq_ref, key_feat_ref, feat_ref, local_ref):
    rows = query_ref.shape[0]
    group, width, count = freq_ref.shape
    span = min(SPAN, rows)
    amplitude = 1.0 / math.sqrt(count)
    below = lax.broadcasted_iota(jnp.int32, (TILE, TILE), 0)
    causal = below >= lax.broadcasted_iota(jnp.int32, (TILE, TILE), 1)
    tiles = [(head, start) for head in range(group) for start in range(0, rows, TILE)]

    def phase_of(head, start):
        lanes = slice(head * width, (head + 1) * width)
        return dot(query_ref[start : start + TILE, lanes], freq_ref[head], (1, 0))

    def attend(head, start, features):
        lanes = slice(head * width, (head + 1) * width)
        total = None
        for other in range(start // span * span, start + TILE, TILE):
            theirs = slice(other, other + TILE)
            scores = dot(features, key_feat_ref[head, :, theirs], (1, 0))
            if other == start:
                scores = jnp.where(causal, scores, F32(0.0))
            part = dot(scores.astype(BF16), value_ref[theirs, lanes], (1, 0))
            total = part if total is None else total + part
        local_ref[start : start + TILE, lanes] = total.astype(local_ref.dtype)

    phase, waiting = phase_of(*tiles[0]), None
    for index, (head, start) in enumerate(tiles):
        following = phase_of(*tiles[index + 1]) if index + 1 < len(tiles) else None
        cosine, sine = cos_sin(phase, amplitude)
        features = jnp.concatenate([cosine.astype(BF16), sine.astype(BF16)], axis=1)
        feat_ref[head, start : start + TILE, :] = features
        if waiting is not None:
            attend(*waiting)
        phase, waiting = following, (head, start, features)
    attend(*waiting)


def query_side(query_rows, value_rows, frequencies, key_feat):
    rows = query_rows.shape[0]
    heads, width, count = frequencies.shape
    group = 2 if heads % 2 == 0 else 1
    return pl.pallas_call(
        query_kernel,
        grid=(heads // group,),
        in_specs=[
            pl.BlockSpec((rows, group * width), lambda h: (0, h)),
            pl.BlockSpec((rows, group * width), lambda h: (0, h)),
            pl.BlockSpec((group, width, count), lambda h: (h, 0, 0)),
            pl.BlockSpec((group, 2 * count, rows), lambda h: (h, 0, 0)),
        ],
        out_specs=[
            pl.BlockSpec((group, rows, 2 * count), lambda h: (h, 0, 0)),
            pl.BlockSpec((rows, group * width), lambda h: (0, h)),
        ],
        out_shape=[
            jax.ShapeDtypeStruct((heads, rows, 2 * count), BF16),
            jax.ShapeDtypeStruct((rows, heads * width), BF16),
        ],
        compiler_params=LARGE,
        cost_estimate=FREE,
        name="query_side",
    )(query_rows, value_rows, frequencies, key_feat)


def finish_kernel(
    heads, span, cuts, core_ref, feat_ref, local_ref, theirs_ref, mine_ref, gain_ref, *refs
):
    prefix_ref, out_refs = refs[0], refs[-len(cuts) :]
    width = local_ref.shape[1] // heads
    steps = pl.num_programs(0)
    kept = pl.program_id(0) >= steps // 2
    first_head = lax.rem(pl.program_id(0) + steps // 2 * (1 - core_ref[0]), steps) * heads
    gains = gain_ref[...].astype(F32)
    row = lax.broadcasted_iota(jnp.int32, gains.shape, 0)
    for head in range(heads):
        cols = slice(head * width, (head + 1) * width)
        gain = jnp.sum(jnp.where(row == first_head + head, gains, F32(0.0)), axis=0, keepdims=True)
        before = jnp.where(kept, mine_ref[head].astype(F32), theirs_ref[head].astype(F32))
        for out_ref, (first, last) in zip(out_refs, cuts):
            starts = [first, *range(first - first % TILE + TILE, last, TILE)]
            for start, stop in zip(starts, starts[1:] + [last]):
                mine = slice(start, stop)
                carried = before
                if start // span:
                    carried = carried + prefix_ref[head, start // span - 1]
                prior = dot(feat_ref[head, mine, :], carried.astype(BF16), (1, 0))
                attended = local_ref[mine, cols].astype(F32) + prior
                square = jnp.mean(attended * attended, axis=-1, keepdims=True)
                normed = attended * lax.rsqrt(square + F32(1e-6)) * gain
                out_ref[start - first : stop - first, cols] = normed.astype(BF16)


def finish(core, feat, local_part, theirs, mine, gain, prefix, cuts):
    heads, all_rows, feats = feat.shape
    rows = cuts[-1][1]
    span = min(SPAN, all_rows)
    width = local_part.shape[1] // heads
    prior = prefix.shape[1]
    half = heads // 2
    group = 4 if half % 4 == 0 and rows < span else 2 if half % 2 == 0 else 1
    steps, half_steps = heads // group, half // group

    def block(g, c):
        return (g + half_steps * (1 - c[0])) % steps

    in_specs = [
        pl.BlockSpec((group, rows, feats), lambda g, c: (block(g, c), 0, 0)),
        pl.BlockSpec((rows, group * width), lambda g, c: (0, block(g, c))),
        pl.BlockSpec((group, feats, width), lambda g, c: (jnp.minimum(g, half_steps - 1), 0, 0)),
        pl.BlockSpec((group, feats, width), lambda g, c: (jnp.maximum(g - half_steps, 0), 0, 0)),
        pl.BlockSpec(gain.shape, lambda g, c: (0, 0)),
    ]
    operands = [feat, local_part, theirs, mine, gain]
    if rows > span:
        in_specs.append(pl.BlockSpec((group, prior, feats, width), lambda g, c: (block(g, c), 0, 0, 0)))
        operands.append(prefix)
    return pl.pallas_call(
        functools.partial(finish_kernel, group, span, cuts),
        grid_spec=pltpu.PrefetchScalarGridSpec(
            num_scalar_prefetch=1,
            grid=(steps,),
            in_specs=in_specs,
            out_specs=[
                pl.BlockSpec((last - first, group * width), lambda g, c: (0, block(g, c))) for first, last in cuts
            ],
        ),
        out_shape=[jax.ShapeDtypeStruct((last - first, heads * width), BF16) for first, last in cuts],
        compiler_params=LARGE if rows > span else MIDDLE,
        cost_estimate=FREE,
        name="finish",
    )(core, *operands)


def project_kernel(sources, place_ref, *refs):
    out_ref = refs[-1]
    total = None
    for x_ref, w_ref in zip(refs[:sources], refs[sources : 2 * sources]):
        part = dot(x_ref[...], w_ref[...], (1, 0))
        total = part if total is None else total + part
    out_ref[...] = total.astype(out_ref.dtype)


def project(blocks, weight, place, hops, dtype=BF16):
    size, depth = blocks[0].shape
    cols = weight.shape[1]
    step = min(1024, cols)

    def rows_of(source):
        return lambda n, p: (p[0] ^ hops[source], n)

    sources = len(blocks)
    return pl.pallas_call(
        functools.partial(project_kernel, sources),
        grid_spec=pltpu.PrefetchScalarGridSpec(
            num_scalar_prefetch=1,
            grid=(cols // step,),
            in_specs=[pl.BlockSpec((size, depth), lambda n, p: (0, 0)) for _ in blocks]
            + [pl.BlockSpec((depth, step), rows_of(source)) for source in range(sources)],
            out_specs=pl.BlockSpec((size, step), lambda n, p: (0, n)),
        ),
        out_shape=jax.ShapeDtypeStruct((size, cols), dtype),
        compiler_params=SMALL,
        cost_estimate=FREE,
        name="project",
    )(place, *blocks, *[weight] * sources)


def partial_kernel(core_ref, turn_ref, x_ref, y_ref, *refs):
    weights, out_ref = refs[:-1], refs[-1]
    count = len(weights) // 2
    swapped, turned = core_ref[0] != 0, turn_ref[0] != 0
    x, y = x_ref[...], y_ref[...]
    half = x.shape[1] // 2
    total = None
    for rows, pieces in ((jnp.where(swapped, y, x), weights[:count]), (jnp.where(swapped, x, y), weights[count:])):
        left, right = rows[:, :half], rows[:, half:]
        sides = [jnp.where(turned, right, left), jnp.where(turned, left, right)]
        rows = jnp.concatenate(sides, axis=1)
        first = 0
        for piece in pieces:
            last = first + piece.shape[0]
            part = dot(rows[:, first:last], piece[...], (1, 0))
            total = part if total is None else total + part
            first = last
    out_ref[...] = total.astype(out_ref.dtype)


def partial_product(core, turn, blocks, weights):
    size, depth = blocks[0].shape
    cols = weights[0].shape[1]
    step = min(1024, cols)
    return pl.pallas_call(
        partial_kernel,
        grid_spec=pltpu.PrefetchScalarGridSpec(
            num_scalar_prefetch=2,
            grid=(cols // step,),
            in_specs=[pl.BlockSpec((size, depth), lambda n, c, t: (0, 0)) for _ in blocks]
            + [pl.BlockSpec((weight.shape[0], step), lambda n, c, t: (0, n)) for weight in weights],
            out_specs=pl.BlockSpec((size, step), lambda n, c, t: (0, n)),
        ),
        out_shape=jax.ShapeDtypeStruct((size, cols), BF16),
        compiler_params=SMALL,
        cost_estimate=FREE,
        name="partial_product",
    )(core, turn, *blocks, *weights)


def join_kernel(a_ref, b_ref, *refs):
    out_ref = refs[-1]
    out_ref[...] = (a_ref[...] + b_ref[...].astype(F32)).astype(out_ref.dtype)


def join(a, b, first, rows, into=None):
    size, cols = a.shape
    step = math.gcd(first, size, 256)
    index = first // step
    spec = pl.BlockSpec((step, cols), lambda r: (r, 0))
    return pl.pallas_call(
        join_kernel,
        grid=(size // step,),
        in_specs=[spec, spec] + [pl.BlockSpec(memory_space=pl.ANY)] * (into is not None),
        out_specs=pl.BlockSpec((step, cols), lambda r: (index + r, 0)),
        out_shape=jax.ShapeDtypeStruct((rows, cols), BF16),
        input_output_aliases={} if into is None else {2: 0},
        compiler_params=SMALL,
        cost_estimate=FREE,
        name="join",
    )(a, b, *([] if into is None else [into]))


def after(value, *others):
    return lax.optimization_barrier((value, *others))[0]


def swap(value, axis, distance):
    return lax.ppermute(value, axis, [(i, i ^ distance) for i in range(lax.axis_size(axis))])


def earlier_states(sent, kept, meanwhile):
    count, mine = lax.axis_size("ctx"), lax.axis_index("ctx")
    core = mine % 2
    partner = swap(sent, "ctx", 1)
    total = (kept.astype(F32) + partner.astype(F32)).astype(BF16)
    earlier = jnp.zeros(kept.shape, F32)
    beside = meanwhile(total)
    distance = 2
    while distance < count:
        radix = min(4, count // distance)
        last = distance * radix >= count
        added = total.astype(F32)
        for step in range(1, radix):
            hop = step * distance
            pairs = [(i, i ^ hop) for i in range(count) if not last or i < i ^ hop]
            theirs = lax.ppermute(total, "ctx", pairs)
            if last:
                theirs = after(theirs, *beside)
            theirs = theirs.astype(F32)
            lower = (mine ^ hop) < mine
            earlier = earlier + jnp.where(lower, theirs, F32(0.0))
            added = added + theirs
        total = added.astype(BF16)
        distance *= radix
    own = earlier + jnp.where(core == 1, partner.astype(F32), F32(0.0))
    given = earlier + jnp.where(core == 0, kept.astype(F32), F32(0.0))
    return swap(given.astype(BF16), "ctx", 1), own.astype(BF16), beside


def normed_output(core, place, turn, query_rows, key_rows, value_rows, frequencies, norm_gain, weight=None):
    key_feat, sent, kept, prefix, *share = key_side(core, place, turn, key_rows, value_rows, frequencies, weight)

    gain = norm_gain.reshape(frequencies.shape[0], -1)

    def meanwhile(total):
        return query_side(query_rows, value_rows, after(frequencies, total), key_feat)

    theirs, own, (query_feat, local_part) = earlier_states(sent, kept, meanwhile)

    def blocks_of(cuts, *others):
        return finish(core, after(query_feat, *others), local_part, theirs, own, gain, prefix, cuts)

    return blocks_of, share


def positions():
    spot, place = lax.axis_index("ctx"), lax.axis_index("head")
    return [value.astype(jnp.int32).reshape(1) for value in (spot % 2, place, (spot // 2 + spot // 4) % 2)]


def line_of_four(query_rows, key_rows, value_rows, frequencies, norm_gain, out_weight):
    rows = query_rows.shape[0]
    core, place, turn = positions()
    sizes = [rows * part // 16 for part in (2,) * 8]
    edges = [sum(sizes[:i]) for i in range(len(sizes) + 1)]
    cuts = tuple(zip(edges[:-1], edges[1:]))
    parts = (query_rows, key_rows, value_rows, frequencies, norm_gain)
    blocks_of, (share,) = normed_output(core, place, turn, *parts, out_weight)
    blocks = blocks_of(cuts[:1])
    share = after(swap(share, "head", 1), *blocks)
    half = share.shape[0] // 2
    halves = [share[:half], share[half:]]
    blocks = [*blocks, *blocks_of(cuts[1:], *halves)]
    pairs, given, partials, products = [], [], [], []
    out, joined = None, 0
    for index, block in enumerate(blocks):
        if index > 2:
            block = after(block, given[index - 2], partials[max(0, index - 4)], products[max(0, index - 4)])
        if index == len(blocks) - 1:
            while joined < index - 4:
                out = join(after(products[joined], given[index - 2]), partials[joined], cuts[joined][0], rows, out)
                joined += 1
            block, out = lax.optimization_barrier((block, out))
        pairs.append([block, swap(block, "head", 2)])
        if index == 1:
            others = [swap(part, "ctx", hop) for part, hop in zip(halves, (2, 4))]
            shares = [after(share, blocks[-1], pairs[0][1])] + [after(other, pairs[0][1]) for other in others]
            weights = shares + [swap(part, "ctx", 1) for part in shares]
            x, y = pairs[0]
            given.append(partial_product(core, turn, [x, y], weights))
            x, y = pairs[1]
            given.append(partial_product(core, turn, [x, after(y, given[0])], weights))
        elif index > 1:
            x, y = pairs[-1]
            y = after(y, partials[index - 2], given[-1], *(products[:-1] if index == len(blocks) - 1 else []))
            given.append(partial_product(core, turn, [x, y], weights))
        partials += [swap(part, "head", 1) for part in given[len(partials) :]]
        products.append(project(pairs[-1], out_weight, place, (0, 2), F32))
    for product, partial, (first, _) in list(zip(products, partials, cuts))[joined:]:
        out = join(product, partial, first, rows, out)
    return out


def any_line(query_rows, key_rows, value_rows, frequencies, norm_gain, out_weight):
    core, place, turn = positions()
    parts = (query_rows, key_rows, value_rows, frequencies, norm_gain)
    blocks_of, _ = normed_output(core, place, turn, *parts)
    (normed,) = blocks_of(((0, query_rows.shape[0]),))
    gathered = lax.all_gather(normed, "head", axis=1, tiled=True)
    return jnp.dot(gathered, out_weight, preferred_element_type=F32).astype(BF16)


def solution(mesh):
    return jax.shard_map(
        line_of_four if mesh.shape["head"] == 4 and mesh.shape["ctx"] % 8 == 0 else any_line,
        mesh=mesh,
        in_specs=(
            P("ctx", "head"),
            P("ctx", "head"),
            P("ctx", "head"),
            P("head", None, None),
            P("head"),
            P(None, "head"),
        ),
        out_specs=P("ctx", "head"),
        check_vma=False,
    )
```

```python
import functools
import math

import jax
import jax.numpy as jnp
from jax import lax
from jax.experimental import pallas as pl
from jax.experimental.pallas import tpu as pltpu
from jax.sharding import PartitionSpec as P

F32 = jnp.float32
BF16 = jnp.bfloat16
SPAN = 512
TILE = 256
SIN_TERMS = (3.1406400334639137, -5.136905232797424, 2.2995469238543222)
COS_TERMS = (0.9999932955183647, -4.933938020185013, 4.0412838463445455, -1.2221270624224843)
ROUNDER = 1.5 * 2.0**23
LARGE = pltpu.CompilerParams(vmem_limit_bytes=56 << 20)
MIDDLE = pltpu.CompilerParams(vmem_limit_bytes=52 << 20)
SMALL = pltpu.CompilerParams(vmem_limit_bytes=20 << 20)
FREE = pl.CostEstimate(flops=0, bytes_accessed=0, transcendentals=0)


def dot(a, b, contract):
    return lax.dot_general(a, b, ((contract[:1], contract[1:]), ((), ())), preferred_element_type=F32)


def poly(terms, scale, u):
    value = F32(terms[-1] * scale)
    for term in terms[-2::-1]:
        value = value * u + F32(term * scale)
    return value


def cos_sin(phase, amplitude):
    turns = phase * F32(1.0 / (2.0 * math.pi))
    part = turns - ((turns + F32(ROUNDER)) - F32(ROUNDER))
    u = part * part
    scale = math.sqrt(2.0 * amplitude)
    half_sin = poly(SIN_TERMS, scale, u) * part
    half_cos = poly(COS_TERMS, scale, u)
    return F32(amplitude) - half_sin * half_sin, half_sin * half_cos


def key_kernel(has_weight, core_ref, place_ref, turn_ref, key_ref, value_ref, freq_ref, *refs):
    if has_weight:
        refs[-1][...] = refs[0][...]
        refs = refs[1:]
    feat_ref, sent_ref, kept_ref, prefix_ref = refs[:4]
    rows = key_ref.shape[0]
    group, width, count = freq_ref.shape
    span = min(SPAN, rows)
    amplitude = 1.0 / math.sqrt(count)
    tiles = [(head, start) for head in range(group) for start in range(0, rows, TILE)]
    turned = [freq_ref[head].T for head in range(group)]

    def phase_of(head, start):
        lanes = slice(head * width, (head + 1) * width)
        return dot(turned[head], key_ref[start : start + TILE, lanes], (1, 1))

    def add_state(head, start, features):
        lanes = slice(head * width, (head + 1) * width)
        state = dot(features, value_ref[start : start + TILE, lanes], (1, 0))
        sums[head] = state if start == 0 else sums[head] + state
        index = (start + TILE) // span - 1
        if (start + TILE) % span == 0 and index < prefix_ref.shape[1]:
            prefix_ref[head, index] = sums[head]

    sums = [None] * group
    phase, waiting = phase_of(*tiles[0]), None
    for index, (head, start) in enumerate(tiles):
        following = phase_of(*tiles[index + 1]) if index + 1 < len(tiles) else None
        cosine, sine = cos_sin(phase, amplitude)
        features = jnp.concatenate([cosine.astype(BF16), sine.astype(BF16)], axis=0)
        feat_ref[head, :, start : start + TILE] = features
        if waiting is not None:
            add_state(*waiting)
        phase, waiting = following, (head, start, features)
    add_state(*waiting)
    sums = [total.astype(BF16) for total in sums]
    half = pl.num_programs(0) // 2

    @pl.when(pl.program_id(0) < half)
    def _():
        for head in range(group):
            sent_ref[head] = sums[head]

    @pl.when(pl.program_id(0) >= half)
    def _():
        for head in range(group):
            kept_ref[head] = sums[head]


def key_side(core, place, turn, key_rows, value_rows, frequencies, weight=None):
    rows = key_rows.shape[0]
    heads, width, count = frequencies.shape
    prior = max(1, rows // min(SPAN, rows) - 1)
    half = heads // 2
    group = 2 if half % 2 == 0 else 1
    steps, half_steps = heads // group, half // group

    def block(g, c):
        return (g + half_steps * (1 - c[0])) % steps

    in_specs = [
        pl.BlockSpec((rows, group * width), lambda g, c, p, t: (0, block(g, c))),
        pl.BlockSpec((rows, group * width), lambda g, c, p, t: (0, block(g, c))),
        pl.BlockSpec((group, width, count), lambda g, c, p, t: (block(g, c), 0, 0)),
    ]
    out_specs = [
        pl.BlockSpec((group, 2 * count, rows), lambda g, c, p, t: (block(g, c), 0, 0)),
        pl.BlockSpec((group, 2 * count, width), lambda g, c, p, t: (jnp.minimum(g, half_steps - 1), 0, 0)),
        pl.BlockSpec((group, 2 * count, width), lambda g, c, p, t: (jnp.maximum(g - half_steps, 0), 0, 0)),
        pl.BlockSpec((group, prior, 2 * count, width), lambda g, c, p, t: (block(g, c), 0, 0, 0)),
    ]
    out_shape = [
        jax.ShapeDtypeStruct((heads, 2 * count, rows), BF16),
        jax.ShapeDtypeStruct((half, 2 * count, width), BF16),
        jax.ShapeDtypeStruct((half, 2 * count, width), BF16),
        jax.ShapeDtypeStruct((heads, prior, 2 * count, width), F32),
    ]
    operands = [key_rows, value_rows, frequencies]
    if weight is not None:
        depth, cols = weight.shape[0] // 4, weight.shape[1]
        piece = depth // 2 // steps

        def rows_of(g, c, p, t):
            return ((p[0] ^ (1 + 2 * c[0])) * 2 + t[0]) * steps + g, 0

        in_specs.append(pl.BlockSpec((piece, cols), rows_of))
        out_specs.append(pl.BlockSpec((piece, cols), lambda g, c, p, t: (g, 0)))
        out_shape.append(jax.ShapeDtypeStruct((depth // 2, cols), weight.dtype))
        operands.append(weight)
    return pl.pallas_call(
        functools.partial(key_kernel, weight is not None),
        grid_spec=pltpu.PrefetchScalarGridSpec(
            num_scalar_prefetch=3, grid=(steps,), in_specs=in_specs, out_specs=out_specs
        ),
        out_shape=out_shape,
        compiler_params=pltpu.CompilerParams(vmem_limit_bytes=213 << 18),
        cost_estimate=FREE,
        name="key_side",
    )(core, place, turn, *operands)


def query_kernel(query_ref, value_ref, freq_ref, key_feat_ref, feat_ref, local_ref):
    rows = query_ref.shape[0]
    group, width, count = freq_ref.shape
    span = min(SPAN, rows)
    amplitude = 1.0 / math.sqrt(count)
    below = lax.broadcasted_iota(jnp.int32, (TILE, TILE), 0)
    causal = below >= lax.broadcasted_iota(jnp.int32, (TILE, TILE), 1)
    tiles = [(head, start) for head in range(group) for start in range(0, rows, TILE)]

    def phase_of(head, start):
        lanes = slice(head * width, (head + 1) * width)
        return dot(query_ref[start : start + TILE, lanes], freq_ref[head], (1, 0))

    def attend(head, start, features):
        lanes = slice(head * width, (head + 1) * width)
        total = None
        for other in range(start // span * span, start + TILE, TILE):
            theirs = slice(other, other + TILE)
            scores = dot(features, key_feat_ref[head, :, theirs], (1, 0))
            if other == start:
                scores = jnp.where(causal, scores, F32(0.0))
            part = dot(scores.astype(BF16), value_ref[theirs, lanes], (1, 0))
            total = part if total is None else total + part
        local_ref[start : start + TILE, lanes] = total.astype(local_ref.dtype)

    phase, waiting = phase_of(*tiles[0]), None
    for index, (head, start) in enumerate(tiles):
        following = phase_of(*tiles[index + 1]) if index + 1 < len(tiles) else None
        cosine, sine = cos_sin(phase, amplitude)
        features = jnp.concatenate([cosine.astype(BF16), sine.astype(BF16)], axis=1)
        feat_ref[head, start : start + TILE, :] = features
        if waiting is not None:
            attend(*waiting)
        phase, waiting = following, (head, start, features)
    attend(*waiting)


def query_side(query_rows, value_rows, frequencies, key_feat):
    rows = query_rows.shape[0]
    heads, width, count = frequencies.shape
    group = 2 if heads % 2 == 0 else 1
    return pl.pallas_call(
        query_kernel,
        grid=(heads // group,),
        in_specs=[
            pl.BlockSpec((rows, group * width), lambda h: (0, h)),
            pl.BlockSpec((rows, group * width), lambda h: (0, h)),
            pl.BlockSpec((group, width, count), lambda h: (h, 0, 0)),
            pl.BlockSpec((group, 2 * count, rows), lambda h: (h, 0, 0)),
        ],
        out_specs=[
            pl.BlockSpec((group, rows, 2 * count), lambda h: (h, 0, 0)),
            pl.BlockSpec((rows, group * width), lambda h: (0, h)),
        ],
        out_shape=[
            jax.ShapeDtypeStruct((heads, rows, 2 * count), BF16),
            jax.ShapeDtypeStruct((rows, heads * width), BF16),
        ],
        compiler_params=MIDDLE,
        cost_estimate=FREE,
        name="query_side",
    )(query_rows, value_rows, frequencies, key_feat)


def finish_kernel(
    heads, span, cuts, core_ref, feat_ref, local_ref, theirs_ref, mine_ref, gain_ref, *refs
):
    prefix_ref, out_refs = refs[0], refs[-len(cuts) :]
    width = local_ref.shape[1] // heads
    steps = pl.num_programs(0)
    kept = pl.program_id(0) >= steps // 2
    first_head = lax.rem(pl.program_id(0) + steps // 2 * (1 - core_ref[0]), steps) * heads
    gains = gain_ref[...].astype(F32)
    row = lax.broadcasted_iota(jnp.int32, gains.shape, 0)
    for head in range(heads):
        cols = slice(head * width, (head + 1) * width)
        gain = jnp.sum(jnp.where(row == first_head + head, gains, F32(0.0)), axis=0, keepdims=True)
        before = jnp.where(kept, mine_ref[head].astype(F32), theirs_ref[head].astype(F32))
        for out_ref, (first, last) in zip(out_refs, cuts):
            starts = [first, *range(first - first % TILE + TILE, last, TILE)]
            for start, stop in zip(starts, starts[1:] + [last]):
                mine = slice(start, stop)
                carried = before
                if start // span:
                    carried = carried + prefix_ref[head, start // span - 1]
                prior = dot(feat_ref[head, mine, :], carried.astype(BF16), (1, 0))
                attended = local_ref[mine, cols].astype(F32) + prior
                square = jnp.mean(attended * attended, axis=-1, keepdims=True)
                normed = attended * lax.rsqrt(square + F32(1e-6)) * gain
                out_ref[start - first : stop - first, cols] = normed.astype(BF16)


def finish(core, feat, local_part, theirs, mine, gain, prefix, cuts):
    heads, all_rows, feats = feat.shape
    rows = cuts[-1][1]
    span = min(SPAN, all_rows)
    width = local_part.shape[1] // heads
    prior = prefix.shape[1]
    half = heads // 2
    group = 4 if half % 4 == 0 and rows < span else 2 if half % 2 == 0 else 1
    steps, half_steps = heads // group, half // group

    def block(g, c):
        return (g + half_steps * (1 - c[0])) % steps

    in_specs = [
        pl.BlockSpec((group, rows, feats), lambda g, c: (block(g, c), 0, 0)),
        pl.BlockSpec((rows, group * width), lambda g, c: (0, block(g, c))),
        pl.BlockSpec((group, feats, width), lambda g, c: (jnp.minimum(g, half_steps - 1), 0, 0)),
        pl.BlockSpec((group, feats, width), lambda g, c: (jnp.maximum(g - half_steps, 0), 0, 0)),
        pl.BlockSpec(gain.shape, lambda g, c: (0, 0)),
    ]
    operands = [feat, local_part, theirs, mine, gain]
    if rows > span:
        in_specs.append(pl.BlockSpec((group, prior, feats, width), lambda g, c: (block(g, c), 0, 0, 0)))
        operands.append(prefix)
    return pl.pallas_call(
        functools.partial(finish_kernel, group, span, cuts),
        grid_spec=pltpu.PrefetchScalarGridSpec(
            num_scalar_prefetch=1,
            grid=(steps,),
            in_specs=in_specs,
            out_specs=[
                pl.BlockSpec((last - first, group * width), lambda g, c: (0, block(g, c))) for first, last in cuts
            ],
        ),
        out_shape=[jax.ShapeDtypeStruct((last - first, heads * width), BF16) for first, last in cuts],
        compiler_params=LARGE if rows > span else MIDDLE,
        cost_estimate=FREE,
        name="finish",
    )(core, *operands)


def project_kernel(sources, place_ref, *refs):
    out_ref = refs[-1]
    total = None
    for x_ref, w_ref in zip(refs[:sources], refs[sources : 2 * sources]):
        part = dot(x_ref[...], w_ref[...], (1, 0))
        total = part if total is None else total + part
    out_ref[...] = total.astype(out_ref.dtype)


def project(blocks, weight, place, hops, dtype=BF16):
    size, depth = blocks[0].shape
    cols = weight.shape[1]
    step = min(1024, cols)

    def rows_of(source):
        return lambda n, p: (p[0] ^ hops[source], n)

    sources = len(blocks)
    return pl.pallas_call(
        functools.partial(project_kernel, sources),
        grid_spec=pltpu.PrefetchScalarGridSpec(
            num_scalar_prefetch=1,
            grid=(cols // step,),
            in_specs=[pl.BlockSpec((size, depth), lambda n, p: (0, 0)) for _ in blocks]
            + [pl.BlockSpec((depth, step), rows_of(source)) for source in range(sources)],
            out_specs=pl.BlockSpec((size, step), lambda n, p: (0, n)),
        ),
        out_shape=jax.ShapeDtypeStruct((size, cols), dtype),
        compiler_params=SMALL,
        cost_estimate=FREE,
        name="project",
    )(place, *blocks, *[weight] * sources)


def partial_kernel(core_ref, turn_ref, x_ref, y_ref, *refs):
    weights, out_ref = refs[:-1], refs[-1]
    count = len(weights) // 2
    swapped, turned = core_ref[0] != 0, turn_ref[0] != 0
    x, y = x_ref[...], y_ref[...]
    half = x.shape[1] // 2
    total = None
    for rows, pieces in ((jnp.where(swapped, y, x), weights[:count]), (jnp.where(swapped, x, y), weights[count:])):
        left, right = rows[:, :half], rows[:, half:]
        sides = [jnp.where(turned, right, left), jnp.where(turned, left, right)]
        rows = jnp.concatenate(sides, axis=1)
        first = 0
        for piece in pieces:
            last = first + piece.shape[0]
            part = dot(rows[:, first:last], piece[...], (1, 0))
            total = part if total is None else total + part
            first = last
    out_ref[...] = total.astype(out_ref.dtype)


def partial_product(core, turn, blocks, weights):
    size, depth = blocks[0].shape
    cols = weights[0].shape[1]
    step = min(1024, cols)
    return pl.pallas_call(
        partial_kernel,
        grid_spec=pltpu.PrefetchScalarGridSpec(
            num_scalar_prefetch=2,
            grid=(cols // step,),
            in_specs=[pl.BlockSpec((size, depth), lambda n, c, t: (0, 0)) for _ in blocks]
            + [pl.BlockSpec((weight.shape[0], step), lambda n, c, t: (0, n)) for weight in weights],
            out_specs=pl.BlockSpec((size, step), lambda n, c, t: (0, n)),
        ),
        out_shape=jax.ShapeDtypeStruct((size, cols), BF16),
        compiler_params=SMALL,
        cost_estimate=FREE,
        name="partial_product",
    )(core, turn, *blocks, *weights)


def join_kernel(a_ref, b_ref, *refs):
    out_ref = refs[-1]
    out_ref[...] = (a_ref[...] + b_ref[...].astype(F32)).astype(out_ref.dtype)


def join(a, b, first, rows, into=None):
    size, cols = a.shape
    step = math.gcd(first, size, 256)
    index = first // step
    spec = pl.BlockSpec((step, cols), lambda r: (r, 0))
    return pl.pallas_call(
        join_kernel,
        grid=(size // step,),
        in_specs=[spec, spec] + [pl.BlockSpec(memory_space=pl.ANY)] * (into is not None),
        out_specs=pl.BlockSpec((step, cols), lambda r: (index + r, 0)),
        out_shape=jax.ShapeDtypeStruct((rows, cols), BF16),
        input_output_aliases={} if into is None else {2: 0},
        compiler_params=SMALL,
        cost_estimate=FREE,
        name="join",
    )(a, b, *([] if into is None else [into]))


def after(value, *others):
    return lax.optimization_barrier((value, *others))[0]


def swap(value, axis, distance):
    return lax.ppermute(value, axis, [(i, i ^ distance) for i in range(lax.axis_size(axis))])


def earlier_states(sent, kept, meanwhile):
    count, mine = lax.axis_size("ctx"), lax.axis_index("ctx")
    core = mine % 2
    partner = swap(sent, "ctx", 1)
    total = (kept.astype(F32) + partner.astype(F32)).astype(BF16)
    earlier = jnp.zeros(kept.shape, F32)
    beside = meanwhile(total)
    distance = 2
    while distance < count:
        radix = min(4, count // distance)
        last = distance * radix >= count
        added = total.astype(F32)
        for step in range(1, radix):
            hop = step * distance
            pairs = [(i, i ^ hop) for i in range(count) if not last or i < i ^ hop]
            theirs = lax.ppermute(total, "ctx", pairs)
            if last:
                theirs = after(theirs, *beside)
            theirs = theirs.astype(F32)
            lower = (mine ^ hop) < mine
            earlier = earlier + jnp.where(lower, theirs, F32(0.0))
            added = added + theirs
        total = added.astype(BF16)
        distance *= radix
    own = earlier + jnp.where(core == 1, partner.astype(F32), F32(0.0))
    given = earlier + jnp.where(core == 0, kept.astype(F32), F32(0.0))
    return swap(given.astype(BF16), "ctx", 1), own.astype(BF16), beside


def normed_output(core, place, turn, query_rows, key_rows, value_rows, frequencies, norm_gain, weight=None):
    key_feat, sent, kept, prefix, *share = key_side(core, place, turn, key_rows, value_rows, frequencies, weight)

    gain = norm_gain.reshape(frequencies.shape[0], -1)

    def meanwhile(total):
        return query_side(query_rows, value_rows, after(frequencies, total), key_feat)

    theirs, own, (query_feat, local_part) = earlier_states(sent, kept, meanwhile)

    def blocks_of(cuts, *others):
        return finish(core, after(query_feat, *others), local_part, theirs, own, gain, prefix, cuts)

    return blocks_of, share


def positions():
    spot, place = lax.axis_index("ctx"), lax.axis_index("head")
    return [value.astype(jnp.int32).reshape(1) for value in (spot % 2, place, (spot // 2 + spot // 4) % 2)]


def line_of_four(query_rows, key_rows, value_rows, frequencies, norm_gain, out_weight):
    rows = query_rows.shape[0]
    core, place, turn = positions()
    sizes = [rows * part // 16 for part in (2,) * 8]
    edges = [sum(sizes[:i]) for i in range(len(sizes) + 1)]
    cuts = tuple(zip(edges[:-1], edges[1:]))
    parts = (query_rows, key_rows, value_rows, frequencies, norm_gain)
    blocks_of, (share,) = normed_output(core, place, turn, *parts, out_weight)
    blocks = blocks_of(cuts[:1])
    share = after(swap(share, "head", 1), *blocks)
    half = share.shape[0] // 2
    halves = [share[:half], share[half:]]
    blocks = [*blocks, *blocks_of(cuts[1:], *halves)]
    pairs, given, partials, products = [], [], [], []
    out, joined = None, 0
    for index, block in enumerate(blocks):
        if index > 2:
            block = after(block, given[index - 2], partials[max(0, index - 4)], products[max(0, index - 4)])
        if index == len(blocks) - 1:
            while joined < index - 4:
                out = join(after(products[joined], given[index - 2]), partials[joined], cuts[joined][0], rows, out)
                joined += 1
            block, out = lax.optimization_barrier((block, out))
        pairs.append([block, swap(block, "head", 2)])
        if index == 1:
            others = [swap(part, "ctx", hop) for part, hop in zip(halves, (2, 4))]
            shares = [after(share, blocks[-1], pairs[0][1])] + [after(other, pairs[0][1]) for other in others]
            weights = shares + [swap(part, "ctx", 1) for part in shares]
            x, y = pairs[0]
            given.append(partial_product(core, turn, [x, y], weights))
            x, y = pairs[1]
            given.append(partial_product(core, turn, [x, after(y, given[0])], weights))
        elif index > 1:
            x, y = pairs[-1]
            y = after(y, partials[index - 2], given[-1], *(products[:-1] if index == len(blocks) - 1 else []))
            given.append(partial_product(core, turn, [x, y], weights))
        partials += [swap(part, "head", 1) for part in given[len(partials) :]]
        products.append(project(pairs[-1], out_weight, place, (0, 2), F32))
    for product, partial, (first, _) in list(zip(products, partials, cuts))[joined:]:
        out = join(product, partial, first, rows, out)
    return out


def any_line(query_rows, key_rows, value_rows, frequencies, norm_gain, out_weight):
    core, place, turn = positions()
    parts = (query_rows, key_rows, value_rows, frequencies, norm_gain)
    blocks_of, _ = normed_output(core, place, turn, *parts)
    (normed,) = blocks_of(((0, query_rows.shape[0]),))
    gathered = lax.all_gather(normed, "head", axis=1, tiled=True)
    return jnp.dot(gathered, out_weight, preferred_element_type=F32).astype(BF16)


def solution(mesh):
    return jax.shard_map(
        line_of_four if mesh.shape["head"] == 4 and mesh.shape["ctx"] % 8 == 0 else any_line,
        mesh=mesh,
        in_specs=(
            P("ctx", "head"),
            P("ctx", "head"),
            P("ctx", "head"),
            P("head", None, None),
            P("head"),
            P(None, "head"),
        ),
        out_specs=P("ctx", "head"),
        check_vma=False,
    )
```

```python
import functools
import math

import jax
import jax.numpy as jnp
from jax import lax
from jax.experimental import pallas as pl
from jax.experimental.pallas import tpu as pltpu
from jax.sharding import PartitionSpec as P

F32 = jnp.float32
BF16 = jnp.bfloat16
SPAN = 512
TILE = 256
SIN_TERMS = (3.1406400334639137, -5.136905232797424, 2.2995469238543222)
COS_TERMS = (0.9999932955183647, -4.933938020185013, 4.0412838463445455, -1.2221270624224843)
ROUNDER = 1.5 * 2.0**23
LARGE = pltpu.CompilerParams(vmem_limit_bytes=56 << 20)
MIDDLE = pltpu.CompilerParams(vmem_limit_bytes=52 << 20)
SMALL = pltpu.CompilerParams(vmem_limit_bytes=20 << 20)
FREE = pl.CostEstimate(flops=0, bytes_accessed=0, transcendentals=0)


def dot(a, b, contract):
    return lax.dot_general(a, b, ((contract[:1], contract[1:]), ((), ())), preferred_element_type=F32)


def poly(terms, scale, u):
    value = F32(terms[-1] * scale)
    for term in terms[-2::-1]:
        value = value * u + F32(term * scale)
    return value


def cos_sin(phase, amplitude):
    turns = phase * F32(1.0 / (2.0 * math.pi))
    part = turns - ((turns + F32(ROUNDER)) - F32(ROUNDER))
    u = part * part
    scale = math.sqrt(2.0 * amplitude)
    half_sin = poly(SIN_TERMS, scale, u) * part
    half_cos = poly(COS_TERMS, scale, u)
    return F32(amplitude) - half_sin * half_sin, half_sin * half_cos


def key_kernel(has_weight, core_ref, place_ref, turn_ref, key_ref, value_ref, freq_ref, *refs):
    if has_weight:
        refs[-1][...] = refs[0][...]
        refs = refs[1:]
    feat_ref, sent_ref, kept_ref, prefix_ref = refs[:4]
    rows = key_ref.shape[0]
    group, width, count = freq_ref.shape
    span = min(SPAN, rows)
    amplitude = 1.0 / math.sqrt(count)
    tiles = [(head, start) for head in range(group) for start in range(0, rows, TILE)]
    turned = [freq_ref[head].T for head in range(group)]

    def phase_of(head, start):
        lanes = slice(head * width, (head + 1) * width)
        return dot(turned[head], key_ref[start : start + TILE, lanes], (1, 1))

    def add_state(head, start, features):
        lanes = slice(head * width, (head + 1) * width)
        state = dot(features, value_ref[start : start + TILE, lanes], (1, 0))
        sums[head] = state if start == 0 else sums[head] + state
        index = (start + TILE) // span - 1
        if (start + TILE) % span == 0 and index < prefix_ref.shape[1]:
            prefix_ref[head, index] = sums[head]

    sums = [None] * group
    phase, waiting = phase_of(*tiles[0]), None
    for index, (head, start) in enumerate(tiles):
        following = phase_of(*tiles[index + 1]) if index + 1 < len(tiles) else None
        cosine, sine = cos_sin(phase, amplitude)
        features = jnp.concatenate([cosine.astype(BF16), sine.astype(BF16)], axis=0)
        feat_ref[head, :, start : start + TILE] = features
        if waiting is not None:
            add_state(*waiting)
        phase, waiting = following, (head, start, features)
    add_state(*waiting)
    sums = [total.astype(BF16) for total in sums]
    half = pl.num_programs(0) // 2

    @pl.when(pl.program_id(0) < half)
    def _():
        for head in range(group):
            sent_ref[head] = sums[head]

    @pl.when(pl.program_id(0) >= half)
    def _():
        for head in range(group):
            kept_ref[head] = sums[head]


def key_side(core, place, turn, key_rows, value_rows, frequencies, weight=None):
    rows = key_rows.shape[0]
    heads, width, count = frequencies.shape
    prior = max(1, rows // min(SPAN, rows) - 1)
    half = heads // 2
    group = 2 if half % 2 == 0 else 1
    steps, half_steps = heads // group, half // group

    def block(g, c):
        return (g + half_steps * (1 - c[0])) % steps

    in_specs = [
        pl.BlockSpec((rows, group * width), lambda g, c, p, t: (0, block(g, c))),
        pl.BlockSpec((rows, group * width), lambda g, c, p, t: (0, block(g, c))),
        pl.BlockSpec((group, width, count), lambda g, c, p, t: (block(g, c), 0, 0)),
    ]
    out_specs = [
        pl.BlockSpec((group, 2 * count, rows), lambda g, c, p, t: (block(g, c), 0, 0)),
        pl.BlockSpec((group, 2 * count, width), lambda g, c, p, t: (jnp.minimum(g, half_steps - 1), 0, 0)),
        pl.BlockSpec((group, 2 * count, width), lambda g, c, p, t: (jnp.maximum(g - half_steps, 0), 0, 0)),
        pl.BlockSpec((group, prior, 2 * count, width), lambda g, c, p, t: (block(g, c), 0, 0, 0)),
    ]
    out_shape = [
        jax.ShapeDtypeStruct((heads, 2 * count, rows), BF16),
        jax.ShapeDtypeStruct((half, 2 * count, width), BF16),
        jax.ShapeDtypeStruct((half, 2 * count, width), BF16),
        jax.ShapeDtypeStruct((heads, prior, 2 * count, width), F32),
    ]
    operands = [key_rows, value_rows, frequencies]
    if weight is not None:
        depth, cols = weight.shape[0] // 4, weight.shape[1]
        piece = depth // 2 // steps

        def rows_of(g, c, p, t):
            return ((p[0] ^ (1 + 2 * c[0])) * 2 + t[0]) * steps + g, 0

        in_specs.append(pl.BlockSpec((piece, cols), rows_of))
        out_specs.append(pl.BlockSpec((piece, cols), lambda g, c, p, t: (g, 0)))
        out_shape.append(jax.ShapeDtypeStruct((depth // 2, cols), weight.dtype))
        operands.append(weight)
    return pl.pallas_call(
        functools.partial(key_kernel, weight is not None),
        grid_spec=pltpu.PrefetchScalarGridSpec(
            num_scalar_prefetch=3, grid=(steps,), in_specs=in_specs, out_specs=out_specs
        ),
        out_shape=out_shape,
        compiler_params=pltpu.CompilerParams(vmem_limit_bytes=213 << 18),
        cost_estimate=FREE,
        name="key_side",
    )(core, place, turn, *operands)


def query_kernel(query_ref, value_ref, freq_ref, key_feat_ref, feat_ref, local_ref):
    rows = query_ref.shape[0]
    group, width, count = freq_ref.shape
    span = min(SPAN, rows)
    amplitude = 1.0 / math.sqrt(count)
    below = lax.broadcasted_iota(jnp.int32, (TILE, TILE), 0)
    causal = below >= lax.broadcasted_iota(jnp.int32, (TILE, TILE), 1)
    tiles = [(head, start) for head in range(group) for start in range(0, rows, TILE)]

    def phase_of(head, start):
        lanes = slice(head * width, (head + 1) * width)
        return dot(query_ref[start : start + TILE, lanes], freq_ref[head], (1, 0))

    def attend(head, start, features):
        lanes = slice(head * width, (head + 1) * width)
        total = None
        for other in range(start // span * span, start + TILE, TILE):
            theirs = slice(other, other + TILE)
            scores = dot(features, key_feat_ref[head, :, theirs], (1, 0))
            if other == start:
                scores = jnp.where(causal, scores, F32(0.0))
            part = dot(scores.astype(BF16), value_ref[theirs, lanes], (1, 0))
            total = part if total is None else total + part
        local_ref[start : start + TILE, lanes] = total.astype(local_ref.dtype)

    phase, waiting = phase_of(*tiles[0]), None
    for index, (head, start) in enumerate(tiles):
        following = phase_of(*tiles[index + 1]) if index + 1 < len(tiles) else None
        cosine, sine = cos_sin(phase, amplitude)
        features = jnp.concatenate([cosine.astype(BF16), sine.astype(BF16)], axis=1)
        feat_ref[head, start : start + TILE, :] = features
        if waiting is not None:
            attend(*waiting)
        phase, waiting = following, (head, start, features)
    attend(*waiting)


def query_side(query_rows, value_rows, frequencies, key_feat):
    rows = query_rows.shape[0]
    heads, width, count = frequencies.shape
    group = 2 if heads % 2 == 0 else 1
    return pl.pallas_call(
        query_kernel,
        grid=(heads // group,),
        in_specs=[
            pl.BlockSpec((rows, group * width), lambda h: (0, h)),
            pl.BlockSpec((rows, group * width), lambda h: (0, h)),
            pl.BlockSpec((group, width, count), lambda h: (h, 0, 0)),
            pl.BlockSpec((group, 2 * count, rows), lambda h: (h, 0, 0)),
        ],
        out_specs=[
            pl.BlockSpec((group, rows, 2 * count), lambda h: (h, 0, 0)),
            pl.BlockSpec((rows, group * width), lambda h: (0, h)),
        ],
        out_shape=[
            jax.ShapeDtypeStruct((heads, rows, 2 * count), BF16),
            jax.ShapeDtypeStruct((rows, heads * width), BF16),
        ],
        compiler_params=MIDDLE,
        cost_estimate=FREE,
        name="query_side",
    )(query_rows, value_rows, frequencies, key_feat)


def finish_kernel(
    heads, span, cuts, core_ref, feat_ref, local_ref, theirs_ref, mine_ref, gain_ref, *refs
):
    prefix_ref, out_refs = refs[0], refs[-len(cuts) :]
    width = local_ref.shape[1] // heads
    steps = pl.num_programs(0)
    kept = pl.program_id(0) >= steps // 2
    first_head = lax.rem(pl.program_id(0) + steps // 2 * (1 - core_ref[0]), steps) * heads
    gains = gain_ref[...].astype(F32)
    row = lax.broadcasted_iota(jnp.int32, gains.shape, 0)
    for head in range(heads):
        cols = slice(head * width, (head + 1) * width)
        gain = jnp.sum(jnp.where(row == first_head + head, gains, F32(0.0)), axis=0, keepdims=True)
        before = jnp.where(kept, mine_ref[head].astype(F32), theirs_ref[head].astype(F32))
        for out_ref, (first, last) in zip(out_refs, cuts):
            starts = [first, *range(first - first % TILE + TILE, last, TILE)]
            for start, stop in zip(starts, starts[1:] + [last]):
                mine = slice(start, stop)
                carried = before
                if start // span:
                    carried = carried + prefix_ref[head, start // span - 1]
                prior = dot(feat_ref[head, mine, :], carried.astype(BF16), (1, 0))
                attended = local_ref[mine, cols].astype(F32) + prior
                square = jnp.mean(attended * attended, axis=-1, keepdims=True)
                normed = attended * lax.rsqrt(square + F32(1e-6)) * gain
                out_ref[start - first : stop - first, cols] = normed.astype(BF16)


def finish(core, feat, local_part, theirs, mine, gain, prefix, cuts):
    heads, all_rows, feats = feat.shape
    rows = cuts[-1][1]
    span = min(SPAN, all_rows)
    width = local_part.shape[1] // heads
    prior = prefix.shape[1]
    half = heads // 2
    group = 4 if half % 4 == 0 and rows < span else 2 if half % 2 == 0 else 1
    steps, half_steps = heads // group, half // group

    def block(g, c):
        return (g + half_steps * (1 - c[0])) % steps

    in_specs = [
        pl.BlockSpec((group, rows, feats), lambda g, c: (block(g, c), 0, 0)),
        pl.BlockSpec((rows, group * width), lambda g, c: (0, block(g, c))),
        pl.BlockSpec((group, feats, width), lambda g, c: (jnp.minimum(g, half_steps - 1), 0, 0)),
        pl.BlockSpec((group, feats, width), lambda g, c: (jnp.maximum(g - half_steps, 0), 0, 0)),
        pl.BlockSpec(gain.shape, lambda g, c: (0, 0)),
    ]
    operands = [feat, local_part, theirs, mine, gain]
    if rows > span:
        in_specs.append(pl.BlockSpec((group, prior, feats, width), lambda g, c: (block(g, c), 0, 0, 0)))
        operands.append(prefix)
    return pl.pallas_call(
        functools.partial(finish_kernel, group, span, cuts),
        grid_spec=pltpu.PrefetchScalarGridSpec(
            num_scalar_prefetch=1,
            grid=(steps,),
            in_specs=in_specs,
            out_specs=[
                pl.BlockSpec((last - first, group * width), lambda g, c: (0, block(g, c))) for first, last in cuts
            ],
        ),
        out_shape=[jax.ShapeDtypeStruct((last - first, heads * width), BF16) for first, last in cuts],
        compiler_params=LARGE if rows > span else MIDDLE,
        cost_estimate=FREE,
        name="finish",
    )(core, *operands)


def project_kernel(sources, place_ref, *refs):
    out_ref = refs[-1]
    total = None
    for x_ref, w_ref in zip(refs[:sources], refs[sources : 2 * sources]):
        part = dot(x_ref[...], w_ref[...], (1, 0))
        total = part if total is None else total + part
    out_ref[...] = total.astype(out_ref.dtype)


def project(blocks, weight, place, hops, dtype=BF16):
    size, depth = blocks[0].shape
    cols = weight.shape[1]
    step = min(1024, cols)

    def rows_of(source):
        return lambda n, p: (p[0] ^ hops[source], n)

    sources = len(blocks)
    return pl.pallas_call(
        functools.partial(project_kernel, sources),
        grid_spec=pltpu.PrefetchScalarGridSpec(
            num_scalar_prefetch=1,
            grid=(cols // step,),
            in_specs=[pl.BlockSpec((size, depth), lambda n, p: (0, 0)) for _ in blocks]
            + [pl.BlockSpec((depth, step), rows_of(source)) for source in range(sources)],
            out_specs=pl.BlockSpec((size, step), lambda n, p: (0, n)),
        ),
        out_shape=jax.ShapeDtypeStruct((size, cols), dtype),
        compiler_params=SMALL,
        cost_estimate=FREE,
        name="project",
    )(place, *blocks, *[weight] * sources)


def partial_kernel(core_ref, turn_ref, x_ref, y_ref, *refs):
    weights, out_ref = refs[:-1], refs[-1]
    count = len(weights) // 2
    swapped, turned = core_ref[0] != 0, turn_ref[0] != 0
    x, y = x_ref[...], y_ref[...]
    half = x.shape[1] // 2
    total = None
    for rows, pieces in ((jnp.where(swapped, y, x), weights[:count]), (jnp.where(swapped, x, y), weights[count:])):
        left, right = rows[:, :half], rows[:, half:]
        sides = [jnp.where(turned, right, left), jnp.where(turned, left, right)]
        rows = jnp.concatenate(sides, axis=1)
        first = 0
        for piece in pieces:
            last = first + piece.shape[0]
            part = dot(rows[:, first:last], piece[...], (1, 0))
            total = part if total is None else total + part
            first = last
    out_ref[...] = total.astype(out_ref.dtype)


def partial_product(core, turn, blocks, weights):
    size, depth = blocks[0].shape
    cols = weights[0].shape[1]
    step = min(1024, cols)
    return pl.pallas_call(
        partial_kernel,
        grid_spec=pltpu.PrefetchScalarGridSpec(
            num_scalar_prefetch=2,
            grid=(cols // step,),
            in_specs=[pl.BlockSpec((size, depth), lambda n, c, t: (0, 0)) for _ in blocks]
            + [pl.BlockSpec((weight.shape[0], step), lambda n, c, t: (0, n)) for weight in weights],
            out_specs=pl.BlockSpec((size, step), lambda n, c, t: (0, n)),
        ),
        out_shape=jax.ShapeDtypeStruct((size, cols), BF16),
        compiler_params=SMALL,
        cost_estimate=FREE,
        name="partial_product",
    )(core, turn, *blocks, *weights)


def join_kernel(a_ref, b_ref, *refs):
    out_ref = refs[-1]
    out_ref[...] = (a_ref[...] + b_ref[...].astype(F32)).astype(out_ref.dtype)


def join(a, b, first, rows, into=None):
    size, cols = a.shape
    step = math.gcd(first, size, 256)
    index = first // step
    spec = pl.BlockSpec((step, cols), lambda r: (r, 0))
    return pl.pallas_call(
        join_kernel,
        grid=(size // step,),
        in_specs=[spec, spec] + [pl.BlockSpec(memory_space=pl.ANY)] * (into is not None),
        out_specs=pl.BlockSpec((step, cols), lambda r: (index + r, 0)),
        out_shape=jax.ShapeDtypeStruct((rows, cols), BF16),
        input_output_aliases={} if into is None else {2: 0},
        compiler_params=SMALL,
        cost_estimate=FREE,
        name="join",
    )(a, b, *([] if into is None else [into]))


def after(value, *others):
    return lax.optimization_barrier((value, *others))[0]


def swap(value, axis, distance):
    return lax.ppermute(value, axis, [(i, i ^ distance) for i in range(lax.axis_size(axis))])


def earlier_states(sent, kept, meanwhile):
    count, mine = lax.axis_size("ctx"), lax.axis_index("ctx")
    core = mine % 2
    partner = swap(sent, "ctx", 1)
    total = (kept.astype(F32) + partner.astype(F32)).astype(BF16)
    earlier = jnp.zeros(kept.shape, F32)
    beside = meanwhile(total)
    distance = 2
    while distance < count:
        radix = min(4, count // distance)
        last = distance * radix >= count
        added = total.astype(F32)
        for step in range(1, radix):
            hop = step * distance
            pairs = [(i, i ^ hop) for i in range(count) if not last or i < i ^ hop]
            theirs = lax.ppermute(total, "ctx", pairs)
            if last:
                theirs = after(theirs, *beside)
            theirs = theirs.astype(F32)
            lower = (mine ^ hop) < mine
            earlier = earlier + jnp.where(lower, theirs, F32(0.0))
            added = added + theirs
        total = added.astype(BF16)
        distance *= radix
    own = earlier + jnp.where(core == 1, partner.astype(F32), F32(0.0))
    given = earlier + jnp.where(core == 0, kept.astype(F32), F32(0.0))
    return swap(given.astype(BF16), "ctx", 1), own.astype(BF16), beside


def normed_output(core, place, turn, query_rows, key_rows, value_rows, frequencies, norm_gain, weight=None):
    key_feat, sent, kept, prefix, *share = key_side(core, place, turn, key_rows, value_rows, frequencies, weight)

    gain = norm_gain.reshape(frequencies.shape[0], -1)

    def meanwhile(total):
        return query_side(query_rows, value_rows, after(frequencies, total), key_feat)

    theirs, own, (query_feat, local_part) = earlier_states(sent, kept, meanwhile)

    def blocks_of(cuts, *others):
        return finish(core, after(query_feat, *others), local_part, theirs, own, gain, prefix, cuts)

    return blocks_of, share


def positions():
    spot, place = lax.axis_index("ctx"), lax.axis_index("head")
    return [value.astype(jnp.int32).reshape(1) for value in (spot % 2, place, (spot // 2 + spot // 4) % 2)]


def line_of_four(query_rows, key_rows, value_rows, frequencies, norm_gain, out_weight):
    rows = query_rows.shape[0]
    core, place, turn = positions()
    sizes = [rows * part // 16 for part in (2, 2, 2, 2, 3, 2, 2, 1)]
    edges = [sum(sizes[:i]) for i in range(len(sizes) + 1)]
    cuts = tuple(zip(edges[:-1], edges[1:]))
    parts = (query_rows, key_rows, value_rows, frequencies, norm_gain)
    blocks_of, (share,) = normed_output(core, place, turn, *parts, out_weight)
    blocks = blocks_of(cuts[:1])
    share = after(swap(share, "head", 1), *blocks)
    half = share.shape[0] // 2
    halves = [share[:half], share[half:]]
    blocks = [*blocks, *blocks_of(cuts[1:], *halves)]
    pairs, given, partials, products = [], [], [], []
    out, joined = None, 0
    for index, block in enumerate(blocks):
        if index > 2:
            block = after(block, given[index - 2], partials[max(0, index - 4)], products[max(0, index - 4)])
        if index == len(blocks) - 1:
            while joined < index - 4:
                out = join(after(products[joined], given[index - 2]), partials[joined], cuts[joined][0], rows, out)
                joined += 1
            block, out = lax.optimization_barrier((block, out))
        pairs.append([block, swap(block, "head", 2)])
        if index == 1:
            others = [swap(part, "ctx", hop) for part, hop in zip(halves, (2, 4))]
            shares = [after(share, blocks[-1], pairs[0][1])] + [after(other, pairs[0][1]) for other in others]
            weights = shares + [swap(part, "ctx", 1) for part in shares]
            x, y = pairs[0]
            given.append(partial_product(core, turn, [x, y], weights))
            x, y = pairs[1]
            given.append(partial_product(core, turn, [x, after(y, given[0])], weights))
        elif index > 1:
            x, y = pairs[-1]
            y = after(y, partials[index - 2], given[-1], *(products[:-1] if index == len(blocks) - 1 else []))
            given.append(partial_product(core, turn, [x, y], weights))
        partials += [swap(part, "head", 1) for part in given[len(partials) :]]
        products.append(project(pairs[-1], out_weight, place, (0, 2), F32))
    for product, partial, (first, _) in list(zip(products, partials, cuts))[joined:]:
        out = join(product, partial, first, rows, out)
    return out


def any_line(query_rows, key_rows, value_rows, frequencies, norm_gain, out_weight):
    core, place, turn = positions()
    parts = (query_rows, key_rows, value_rows, frequencies, norm_gain)
    blocks_of, _ = normed_output(core, place, turn, *parts)
    (normed,) = blocks_of(((0, query_rows.shape[0]),))
    gathered = lax.all_gather(normed, "head", axis=1, tiled=True)
    return jnp.dot(gathered, out_weight, preferred_element_type=F32).astype(BF16)


def solution(mesh):
    return jax.shard_map(
        line_of_four if mesh.shape["head"] == 4 and mesh.shape["ctx"] % 8 == 0 else any_line,
        mesh=mesh,
        in_specs=(
            P("ctx", "head"),
            P("ctx", "head"),
            P("ctx", "head"),
            P("head", None, None),
            P("head"),
            P(None, "head"),
        ),
        out_specs=P("ctx", "head"),
        check_vma=False,
    )
```
